128 devices in a mesh: dp: 16 (over z, x), ctx: 8 (over y, core).
Axes of the slice: x: 4, y: 4, z: 4, core: 2. Of those that a mesh axis runs over, the one named last changes fastest.
Arguments:
- tokens: bfloat16 [16, 1, 2048, 2560], P('dp', None, 'ctx'), may hold values from -6 to 6
- target: bfloat16 [16, 1, 2048, 2560], P('dp', None, 'ctx'), may hold values from -6 to 6
- rewards: float32 [16, 1, 2048], P('dp', None, 'ctx'), may hold values from 0.25 to 4
- doc_lengths: int32 [16, 1, 5], P('dp'), may hold values from 1 to 1024, 2048 in all within a row
- norm_gain: float32 [2560], replicated, may hold values from 0.1 to 1.9
- w_query: bfloat16 [2560, 1024], P(('dp', 'ctx')), as said below
- w_key: bfloat16 [2560, 512], P(('dp', 'ctx')), as said below
- w_value: bfloat16 [2560, 512], P(('dp', 'ctx')), may hold values from -0.125 to 0.125
- w_out: bfloat16 [1024, 2560], P(('dp', 'ctx')), may hold values from -0.1875 to 0.1875
- gossip_bit: int32 [16], P('dp'), may hold values from 0 to 3, as said below
Outputs:
- grad_query: float32 [16, 2560, 1024], P('dp', 'ctx')
- grad_key: float32 [16, 2560, 512], P('dp', 'ctx')
- grad_value: float32 [16, 2560, 512], P('dp', 'ctx')
- grad_out: float32 [16, 1024, 2560], P('dp', 'ctx')
The draws below stay inside these ranges and needn't reach their ends.
Inputs may be any that keep to these rules, and one draw needn't show every extreme that they name: `doc_lengths`: the lengths of one sequence sum to 2048; the longest is exactly 1024. `gossip_bit`: every bit from 0 to 3 is named by some group. `w_query`: a projection's weights. `w_key`: a projection's weights.
All inputs are finite; a program needn't handle non-finite values.
Results may differ from the reference program's by a relative error of at most 0.019.
The reference program's roundings to bfloat16 on the way count: a program that leaves them out, or rounds other values in their place, can miss the bound.
Values may be sent and summed in bfloat16 or wider, within the bound.
A program may use at most 128 MiB of HBM per device.

```python
import math
import jax
import jax.numpy as jnp
import numpy as np
from jax import lax

MODEL_DIM = 2560
QUERY_HEADS = 4
KEY_VALUE_HEADS = 2
HEAD_DIM = 256
WINDOW = 1024
TOK_DEV = 256
SEQ_DEV = 1
QW = 1024
KW = 512
LENGTH = 2048
DOCS = 5
MOST_DOC = 1024
GOSSIP_LEVELS = 4
N_DP = 16
N_CTX = 8


def shared_weights(key):
    query_key = jax.random.fold_in(key, 11)
    local_key = jax.random.fold_in(key, 12)
    query_matrix = jnp.clip(jax.random.normal(query_key, (MODEL_DIM, QUERY_HEADS * HEAD_DIM), jnp.float32), -6.0, 6.0) * MODEL_DIM ** (-0.5)
    key_matrix = jnp.clip(jax.random.normal(local_key, (MODEL_DIM, KEY_VALUE_HEADS * HEAD_DIM), jnp.float32), -6.0, 6.0) * MODEL_DIM ** (-0.5)
    return (query_matrix, key_matrix)


def draw_w_query(key, part):
    return shared_weights(key)[0].astype(jnp.bfloat16)


def draw_w_key(key, part):
    return shared_weights(key)[1].astype(jnp.bfloat16)


def draw_gossip_bit(key, part):
    level_count = GOSSIP_LEVELS
    chosen = jax.random.randint(jax.random.fold_in(key, 21), (N_DP,), 0, level_count, dtype=jnp.int32)
    places = jax.random.permutation(jax.random.fold_in(key, 22), N_DP)[:level_count]
    return chosen.at[places].set(jnp.arange(level_count, dtype=jnp.int32))


def block_scale(rng, shape, shards, least, top_value):
    level, own = 1.0, jax.random.fold_in(rng, 6)
    for position, blocks in shards:
        steps = jnp.exp(jax.random.uniform(jax.random.fold_in(own, position), (blocks,), jnp.float32, least / len(shards), top_value / len(shards)))
        level = level * jnp.repeat(steps, shape[position] // blocks).reshape([-1 if axis == position else 1 for axis in range(len(shape))])
    return level


def split_up(count, total, limit, slope):
    portions = [(1 << 20) // math.isqrt(standing ** slope) + 1 for standing in range(2, count + 1)]
    spare, holding = total - limit - (count - 1), [1] * (count - 1)
    while spare > 0:
        candidates = [i for i in range(count - 1) if holding[i] < limit]
        mass, budget = sum([portions[i] for i in candidates]), spare
        for i in candidates:
            extra = min(limit - holding[i], max(1, budget * portions[i] // mass), spare)
            holding[i] = holding[i] + extra
            spare = spare - extra
    return np.array([limit] + holding)


def uneven_parts(key, count, total, bound, slope):
    if count == 2:
        one = jax.random.randint(key, (), max(1, total - bound), min(bound, total - 1) + 1)
        return jnp.stack([one, total - one])
    sizes = jnp.asarray(split_up(count, total, bound, slope), jnp.int32)
    couples = (count - 1) // 2
    donor, receiver = sizes[1:1 + 2 * couples:2], sizes[2:2 + 2 * couples:2]
    margin = jnp.minimum(donor - 1, bound - receiver)
    moved = jax.random.randint(jax.random.fold_in(key, 1), (couples,), 0, 1 << 20) % (margin + 1)
    sizes = sizes.at[1:1 + 2 * couples:2].set(donor - moved).at[2:2 + 2 * couples:2].set(receiver + moved)
    return sizes[jax.random.permutation(jax.random.fold_in(key, 2), count)]


def gaussian(stream_key, extent, spread, bound, split=(), kind=jnp.bfloat16):
    gain = block_scale(stream_key, extent, split, -0.22, 0.18) if split else 1.0
    values = jax.random.normal(stream_key, extent, jnp.float32) * spread * gain
    return jnp.minimum(jnp.maximum(values, -bound), bound).astype(kind)


def setup_inputs(seed: int = 0) -> dict:
    key_of = jax.random.split(jax.random.key(seed), 11)
    return {
        "tokens": gaussian(key_of[0], (N_DP, SEQ_DEV, LENGTH, MODEL_DIM), 1.0, 6.0, ((0, 16), (2, 8))),
        "target": gaussian(key_of[1], (N_DP, SEQ_DEV, LENGTH, MODEL_DIM), 1.0, 6.0, ((0, 16), (2, 8))),
        "rewards": jnp.clip(jnp.exp(math.log(4.0) - 2.7725887 * jax.random.uniform(key_of[2], (N_DP, SEQ_DEV, LENGTH), jnp.float32) ** block_scale(key_of[2], (N_DP, SEQ_DEV, LENGTH), ((0, 16), (2, 8)), -0.2, 0.2)), 0.25, 4.0),
        "doc_lengths": jax.vmap(lambda own: uneven_parts(own, DOCS, LENGTH, MOST_DOC, 2))(jax.random.split(key_of[3], N_DP * SEQ_DEV)).reshape((N_DP, SEQ_DEV, DOCS)).astype(jnp.int32),
        "norm_gain": jnp.clip(1.0 + 0.18 * jax.random.normal(key_of[4], (MODEL_DIM,), jnp.float32), 0.1, 1.9),
        "w_query": draw_w_query(jax.random.fold_in(key_of[10], 71), 0),
        "w_key": draw_w_key(jax.random.fold_in(key_of[10], 71), 0),
        "w_value": gaussian(key_of[7], (MODEL_DIM, KW), MODEL_DIM ** -0.5, 0.125, ((0, 128),)),
        "w_out": gaussian(key_of[8], (QW, MODEL_DIM), QW ** -0.5, 0.1875, ((0, 128),)),
        "gossip_bit": draw_gossip_bit(jax.random.fold_in(key_of[10], 71), 0),
    }


epsilon = 1e-06
masked_score = -1e+30

def norm_rows(inputs, norm_gain):
    values = inputs.astype(jnp.float32)
    power = lax.optimization_barrier(jnp.mean(values * values, axis=-1, keepdims=True))
    return (values * lax.rsqrt(power + epsilon) * norm_gain.astype(jnp.float32)).astype(jnp.bfloat16)

def doc_index(positions, lengths):
    endings = jnp.cumsum(lengths.astype(jnp.int32), axis=-1)
    return lax.optimization_barrier(jnp.sum((endings[:, None, :] <= positions[:, :, None]).astype(jnp.int32), axis=-1))

def allowed(query_pos, key_pos, lengths):
    query_doc = doc_index(query_pos, lengths)
    key_doc = doc_index(key_pos, lengths)
    distance = query_pos[:, :, None] - key_pos[:, None, :]
    same_doc = query_doc[:, :, None] == key_doc[:, None, :]
    return (key_pos[:, None, :] >= 0) & same_doc & (distance >= 0) & (distance < WINDOW)

def split_heads(query_rows, key_tile, value_tile):
    batch_count, query_length, _ = query_rows.shape
    key_length = key_tile.shape[1]
    query_heads = query_rows.astype(jnp.float32).reshape(batch_count, query_length, KEY_VALUE_HEADS, QUERY_HEADS // KEY_VALUE_HEADS, HEAD_DIM)
    key_heads = key_tile.astype(jnp.float32).reshape(batch_count, key_length, KEY_VALUE_HEADS, HEAD_DIM)
    value_heads = value_tile.astype(jnp.float32).reshape(batch_count, key_length, KEY_VALUE_HEADS, HEAD_DIM)
    return (query_heads, key_heads, value_heads)

def attend(query_rows, key_tile, value_tile, mask):
    query_heads, key_heads, value_heads = split_heads(query_rows, key_tile, value_tile)
    scores = jnp.einsum('btkgd,bskd->bkgts', query_heads, key_heads) * HEAD_DIM ** (-0.5)
    allowed_mask = mask[:, None, None, :, :]
    scores = jnp.where(allowed_mask, scores, masked_score)
    row_max = lax.optimization_barrier(jnp.max(scores, axis=-1, keepdims=True))
    raised = jnp.where(allowed_mask, jnp.exp(scores - row_max), 0.0)
    attn_probs = (raised / lax.optimization_barrier(jnp.sum(raised, axis=-1, keepdims=True))).astype(jnp.bfloat16)
    mixed_heads = jnp.einsum('bkgts,bskd->btkgd', attn_probs.astype(jnp.float32), value_heads)
    return (attn_probs, mixed_heads.reshape(query_rows.shape[0], query_rows.shape[1], QUERY_HEADS * HEAD_DIM).astype(jnp.bfloat16))

def attend_back(query_rows, key_tile, value_tile, attn_probs, blended_block, blended_gradient):
    query_heads, key_heads, value_heads = split_heads(query_rows, key_tile, value_tile)
    batch_count, query_length, _ = query_rows.shape
    key_length = key_tile.shape[1]
    gradient_heads = blended_gradient.astype(jnp.float32).reshape(batch_count, query_length, KEY_VALUE_HEADS, QUERY_HEADS // KEY_VALUE_HEADS, HEAD_DIM)
    output_heads = blended_block.astype(jnp.float32).reshape(batch_count, query_length, KEY_VALUE_HEADS, QUERY_HEADS // KEY_VALUE_HEADS, HEAD_DIM)
    prob_grads = jnp.einsum('btkgd,bskd->bkgts', gradient_heads, value_heads)
    row_dots = jnp.transpose(lax.optimization_barrier(jnp.sum(gradient_heads * output_heads, axis=-1)), (0, 2, 3, 1))[..., None]
    probs_wide = attn_probs.astype(jnp.float32)
    score_grads = (probs_wide * (prob_grads - row_dots) * HEAD_DIM ** (-0.5)).astype(jnp.bfloat16)
    score_wide = score_grads.astype(jnp.float32)
    query_gradients = jnp.einsum('bkgts,bskd->btkgd', score_wide, key_heads)
    key_gradients = jnp.einsum('bkgts,btkgd->bskd', score_wide, query_heads)
    value_gradients = jnp.einsum('bkgts,btkgd->bskd', probs_wide, gradient_heads)
    return (query_gradients.reshape(batch_count, query_length, QUERY_HEADS * HEAD_DIM).astype(jnp.bfloat16), key_gradients.reshape(batch_count, key_length, KEY_VALUE_HEADS * HEAD_DIM).astype(jnp.bfloat16), value_gradients.reshape(batch_count, key_length, KEY_VALUE_HEADS * HEAD_DIM).astype(jnp.bfloat16))

def rounded_term(partial_term):
    return lax.optimization_barrier(partial_term.astype(jnp.bfloat16)).astype(jnp.float32)

def reference(tokens, target, rewards, doc_lengths, norm_gain, w_query, w_key, w_value, w_out, gossip_bit):
    reach_blocks = WINDOW // TOK_DEV
    key_feature_width = KEY_VALUE_HEADS * HEAD_DIM
    query_width = QUERY_HEADS * HEAD_DIM
    joined_width = query_width + 2 * key_feature_width
    span_len = (reach_blocks + 1) * TOK_DEV
    grads_in = []
    grads_out = []
    for group_index in range(N_DP):
        lengths = doc_lengths[group_index]
        normed = norm_rows(tokens[group_index], norm_gain)
        flat_rows = normed.reshape(SEQ_DEV * LENGTH, MODEL_DIM)
        query_rows = jnp.dot(flat_rows, w_query, preferred_element_type=jnp.float32).astype(jnp.bfloat16).reshape(SEQ_DEV, LENGTH, query_width)
        key_all = jnp.dot(flat_rows, w_key, preferred_element_type=jnp.float32).astype(jnp.bfloat16).reshape(SEQ_DEV, LENGTH, key_feature_width)
        value_all = jnp.dot(flat_rows, w_value, preferred_element_type=jnp.float32).astype(jnp.bfloat16).reshape(SEQ_DEV, LENGTH, key_feature_width)
        leading = jnp.zeros((SEQ_DEV, reach_blocks * TOK_DEV, key_feature_width), jnp.bfloat16)
        key_padded = jnp.concatenate([leading, key_all], axis=1)
        value_padded = jnp.concatenate([leading, value_all], axis=1)
        saved_blocks = []
        mixed_parts = []
        for shard_index in range(N_CTX):
            first_pos = shard_index * TOK_DEV
            query_pos = jnp.broadcast_to(first_pos + jnp.arange(TOK_DEV, dtype=jnp.int32), (SEQ_DEV, TOK_DEV))
            key_pos = jnp.broadcast_to(first_pos - reach_blocks * TOK_DEV + jnp.arange(span_len, dtype=jnp.int32), (SEQ_DEV, span_len))
            mask = allowed(query_pos, key_pos, lengths)
            key_tile = key_padded[:, first_pos:first_pos + span_len]
            value_tile = value_padded[:, first_pos:first_pos + span_len]
            query_block = query_rows[:, first_pos:first_pos + TOK_DEV]
            attn_probs, blended_block = attend(query_block, key_tile, value_tile, mask)
            saved_blocks.append((query_block, key_tile, value_tile, attn_probs, blended_block))
            mixed_parts.append(blended_block)
        mixed_heads = jnp.concatenate(mixed_parts, axis=1)
        mixed_flat = mixed_heads.reshape(SEQ_DEV * LENGTH, query_width)
        result = tokens[group_index].reshape(-1, MODEL_DIM).astype(jnp.float32) + jnp.dot(mixed_flat, w_out, preferred_element_type=jnp.float32)
        delta_rows = (rewards[group_index].reshape(-1, 1).astype(jnp.float32) * (result - target[group_index].reshape(-1, MODEL_DIM).astype(jnp.float32))).astype(jnp.bfloat16)
        blended_gradient = jnp.dot(delta_rows, w_out.T, preferred_element_type=jnp.float32).astype(jnp.bfloat16).reshape(SEQ_DEV, LENGTH, query_width)
        key_sum = jnp.zeros((SEQ_DEV, (N_CTX + reach_blocks) * TOK_DEV, key_feature_width), jnp.float32)
        value_sum = jnp.zeros((SEQ_DEV, (N_CTX + reach_blocks) * TOK_DEV, key_feature_width), jnp.float32)
        query_parts = []
        for shard_index in range(N_CTX):
            first_pos = shard_index * TOK_DEV
            query_block, key_tile, value_tile, attn_probs, blended_block = saved_blocks[shard_index]
            grad_block = blended_gradient[:, first_pos:first_pos + TOK_DEV]
            query_gradients, key_gradients, value_gradients = attend_back(query_block, key_tile, value_tile, attn_probs, blended_block, grad_block)
            query_parts.append(query_gradients)
            key_sum = key_sum.at[:, first_pos:first_pos + span_len].add(key_gradients.astype(jnp.float32))
            value_sum = value_sum.at[:, first_pos:first_pos + span_len].add(value_gradients.astype(jnp.float32))
        key_final = key_sum[:, reach_blocks * TOK_DEV:].astype(jnp.bfloat16)
        value_final = value_sum[:, reach_blocks * TOK_DEV:].astype(jnp.bfloat16)
        joined = jnp.concatenate([jnp.concatenate(query_parts, axis=1), key_final, value_final], axis=-1)
        delta_seq = delta_rows.reshape(SEQ_DEV, LENGTH, MODEL_DIM)
        in_total = jnp.zeros((MODEL_DIM, joined_width), jnp.float32)
        out_total = jnp.zeros((query_width, MODEL_DIM), jnp.float32)
        for shard_index in range(N_CTX):
            first_pos = shard_index * TOK_DEV
            normed_block = normed[:, first_pos:first_pos + TOK_DEV].reshape(-1, MODEL_DIM)
            joined_block = joined[:, first_pos:first_pos + TOK_DEV].reshape(-1, joined_width)
            in_total = in_total + rounded_term(jnp.dot(normed_block.T, joined_block, preferred_element_type=jnp.float32))
            blended_block = mixed_heads[:, first_pos:first_pos + TOK_DEV].reshape(-1, query_width)
            delta_block = delta_seq[:, first_pos:first_pos + TOK_DEV].reshape(-1, MODEL_DIM)
            out_total = out_total + rounded_term(jnp.dot(blended_block.T, delta_block, preferred_element_type=jnp.float32))
        grads_in.append(in_total.astype(jnp.bfloat16))
        grads_out.append(out_total.astype(jnp.bfloat16))
    stacked_in = jnp.stack(grads_in)
    stacked_out = jnp.stack(grads_out)
    partner = jnp.bitwise_xor(jnp.arange(N_DP, dtype=jnp.int32), jnp.left_shift(jnp.ones((N_DP,), jnp.int32), gossip_bit.astype(jnp.int32)))
    mates_in = jnp.take(stacked_in, partner, axis=0)
    mates_out = jnp.take(stacked_out, partner, axis=0)
    mean_in = (stacked_in.astype(jnp.float32) + mates_in.astype(jnp.float32)) * 0.5
    mean_out = (stacked_out.astype(jnp.float32) + mates_out.astype(jnp.float32)) * 0.5
    return (mean_in[:, :, :query_width], mean_in[:, :, query_width:query_width + key_feature_width], mean_in[:, :, query_width + key_feature_width:], mean_out)
```

```python
import functools
import jax
import jax.numpy as jnp
from jax import lax
from jax.experimental import pallas as pl
from jax.experimental.pallas import tpu as pltpu
from jax.sharding import PartitionSpec as P

MESH = pl.DeviceIdType.MESH
BF16 = jnp.bfloat16
F32 = jnp.float32
SIDE = 4


def place():
    dp, ctx = lax.axis_index("dp"), lax.axis_index("ctx")
    return {"x": lax.rem(dp, SIDE), "z": lax.div(dp, SIDE), "y": lax.div(ctx, 2), "c": lax.rem(ctx, 2)}


def device(at):
    return (at["z"] * SIDE + at["x"], at["y"] * 2 + at["c"])


def beside(at, axis, step):
    return {**at, axis: lax.rem(at[axis] + step + SIDE, SIDE)}


def sibling(at):
    return {**at, "c": 1 - at["c"]}


def greet(peers):
    barrier = pltpu.get_barrier_semaphore()
    for peer in peers:
        pl.semaphore_signal(barrier, inc=1, device_id=device(peer), device_id_type=MESH)
    pl.semaphore_wait(barrier, len(peers))


def gather_kernel(rows_in, rows_out, in_ref, out_ref, w_in, w_out, slots_in, slots_out, wide, block_in, block_out,
                  swap_send, swap_recv, pair_sem, local_sem, ring_send, ring_recv, twin_send, twin_recv):
    at = place()
    c = at["c"]
    ctx = at["y"] * 2 + c
    twin = sibling(at)
    others = [lax.rem(ctx + k, 8) for k in range(1, 8)]
    group = [{**at, "y": lax.div(j, 2), "c": lax.rem(j, 2)} for j in others]
    greet([beside(at, "x", 1), beside(at, "x", -1), beside(at, "z", 1), beside(at, "z", -1)] + group)

    copies = []
    for k in range(7):
        copies.append(pltpu.make_async_remote_copy(
            in_ref.at[others[k]], slots_in.at[ctx], swap_send.at[k], swap_recv.at[k],
            device_id=device(group[k]), device_id_type=MESH))
    pair = pltpu.make_async_remote_copy(
        out_ref.at[1 - c], slots_out.at[c], pair_sem.at[0], pair_sem.at[1], device_id=device(twin), device_id_type=MESH)
    pair.start()
    for copy in copies:
        copy.start()
    slots_in[ctx] = in_ref[ctx]
    slots_out[c] = out_ref[c]
    pair.wait()
    block_out[0, 0, 0] = jnp.concatenate(
        [slots_out[0].astype(F32)[:rows_out], slots_out[1].astype(F32)[:rows_out]], axis=0).astype(BF16)
    for copy in copies:
        copy.wait()
    for j in range(8):
        wide[rows_in * j:rows_in * (j + 1)] = slots_in[j].astype(F32)[:rows_in]
    block_in[0, 0, 0] = wide[...].astype(BF16)

    half_rows = rows_in * 4
    one = {a: pl.ds(at[a], 1) for a in "xyz"}
    whole = pl.ds(0, SIDE)

    def view(part, where, core):
        if part == 2:
            return w_out.at[where["z"], where["x"], where["y"], :, pl.ds(pl.multiple_of(core * 1280, 128), 1280)]
        rows = pl.ds(half_rows * part, half_rows)
        return w_in.at[where["y"], where["z"], where["x"], rows, pl.ds(pl.multiple_of(core * 256, 128), 256)]

    def rest(part):
        return [
            pltpu.make_async_copy(block_in.at[:, :, :, pl.ds(half_rows * p, half_rows), :] if p < 2 else block_out,
                                  view(p, one, c), local_sem.at[p])
            for p in part]

    stores = rest(range(3))
    for copy in stores:
        copy.start()
    for copy in stores:
        copy.wait()

    orders = ("xyz", "yzx", "zxy")
    twins, sends = [], []

    def to_twin(part, where, slot):
        copy = pltpu.make_async_remote_copy(
            view(part, where, c), view(part, where, c), twin_send.at[part, slot], twin_recv.at[part, slot],
            device_id=device(twin), device_id_type=MESH)
        copy.start()
        twins.append(copy)

    def ring(part, phase, slot, where, step):
        axis = orders[part][phase]
        copy = pltpu.make_async_remote_copy(
            view(part, where, c), view(part, where, c), ring_send.at[part, phase, slot], ring_recv.at[part, phase, slot],
            device_id=device(beside(at, axis, step)), device_id_type=MESH)
        copy.start()
        sends.append(copy)
        return copy

    for phase in range(3):
        def known(part, shift, half):
            order = orders[part]
            where = dict(one)
            for a in order[:phase]:
                where[a] = whole
            if phase and half is not None:
                where[order[0]] = pl.ds(2 * half, 2)
            axis = order[phase]
            where[axis] = pl.ds(lax.rem(at[axis] + shift + SIDE, SIDE), 1)
            return where

        first, last = {}, {}
        halves = (0, 1) if phase else (None,)
        for part in range(3):
            if phase:
                first[part] = (ring(part, phase, 0, known(part, 0, 0), 1), ring(part, phase, 1, known(part, 0, 1), -1))
                last[part] = [ring(part, phase, 2, known(part, 0, 1), 1), ring(part, phase, 3, known(part, 0, 0), -1)]
            else:
                first[part] = (ring(part, 0, 0, known(part, 0, None), 1),)
                last[part] = [ring(part, 0, 1, known(part, 0, None), -1)]
        if phase == 2:
            for part in range(3):
                to_twin(part, known(part, 0, None), 0)
        for part in range(3):
            if phase:
                first[part][0].wait_recv()
                last[part].append(ring(part, phase, 4, known(part, -1, 0), 1))
                first[part][1].wait_recv()
                last[part].append(ring(part, phase, 5, known(part, 1, 1), -1))
                if phase == 2:
                    to_twin(part, known(part, -1, 0), 1)
                    to_twin(part, known(part, 1, 1), 2)
            else:
                first[part][0].wait_recv()
                last[part].append(ring(part, 0, 4, known(part, -1, None), 1))
        for n in range(4):
            for part in range(3):
                if n < len(last[part]):
                    last[part][n].wait_recv()
                    if phase == 2:
                        shift, half = ((-1, 1), (1, 0), (-2, 0), (2, 1))[n]
                        to_twin(part, known(part, shift, half), 3 + n)
    for copy in sends:
        copy.wait_send()
    for copy in twins:
        copy.wait()


def gather_weights(w_query, w_key, w_value, w_out):
    rows_in, rows_out = w_query.shape[0], w_out.shape[0]
    joined = jnp.concatenate([w_query, w_key, w_value], axis=1)
    pieces_in = jnp.pad(joined.reshape(rows_in, 8, 256).transpose(1, 0, 2), ((0, 0), (0, 32 - rows_in), (0, 0)))
    pieces_out = jnp.pad(w_out.reshape(rows_out, 2, 1280).transpose(1, 0, 2), ((0, 0), (0, 16 - rows_out), (0, 0)))
    vmem = pl.BlockSpec(memory_space=pltpu.VMEM)
    hbm = pl.BlockSpec(memory_space=pl.ANY)
    dma = pltpu.SemaphoreType.DMA
    whole_in, whole_out = pl.pallas_call(
        functools.partial(gather_kernel, rows_in, rows_out),
        out_shape=(
            jax.ShapeDtypeStruct((SIDE, SIDE, SIDE, 8 * rows_in, 512), BF16),
            jax.ShapeDtypeStruct((SIDE, SIDE, SIDE, 2 * rows_out, 2560), BF16),
        ),
        in_specs=[vmem, vmem],
        out_specs=(hbm, hbm),
        scratch_shapes=[
            pltpu.VMEM((8, 32, 256), BF16),
            pltpu.VMEM((2, 16, 1280), BF16),
            pltpu.VMEM((8 * rows_in, 256), F32),
            pltpu.VMEM((1, 1, 1, 8 * rows_in, 256), BF16),
            pltpu.VMEM((1, 1, 1, 2 * rows_out, 1280), BF16),
            dma((7,)), dma((7,)), dma((2,)), dma((3,)),
            dma((3, 3, 6)), dma((3, 3, 6)), dma((3, 7)), dma((3, 7)),
        ],
        compiler_params=pltpu.CompilerParams(collective_id=0, has_side_effects=True),
        name="gather_weights",
    )(pieces_in, pieces_out)
    return whole_in.reshape(4, 128 * rows_in, 512), whole_out.reshape(128 * rows_out, 2560)


def add_rows(count, step, body):
    def at(i, carry):
        body(pl.ds(pl.multiple_of(i * step, step), step))
        return carry
    lax.fori_loop(0, count // step, at, 0)


N_IN, N_OUT = 4, 2


def reduce_kernel(in_ref, out_ref, own_in, own_out, mate_in, mate_out, *scratch):
    (sum_in, sum_out, twin_in, twin_out, far_in, far_out, near_in, near_out, load_sem, twin_send, twin_recv,
     far_send, far_recv, near_send, near_recv, mate_send, mate_recv, keep_sem, stage_in, stage_out, done_in, done_out) = scratch
    at = place()
    c, y = at["c"], at["y"]
    twin = sibling(at)
    up, down = beside(at, "y", 1), beside(at, "y", -1)
    x_flip = {**at, "x": at["x"] + 1 - 2 * lax.rem(at["x"], 2)}
    x_turn = {**at, "x": SIDE - 1 - at["x"]}
    z_flip = {**at, "z": at["z"] + 1 - 2 * lax.rem(at["z"], 2)}
    z_turn = {**at, "z": SIDE - 1 - at["z"]}
    greet([twin, up, down, x_flip, x_turn, z_flip, z_turn])

    chunks = [(1, n) for n in range(N_OUT)] + [(0, n) for n in range(N_IN)]
    total = len(chunks)

    def pick(kind, n, inside, outside):
        return (inside if kind == 0 else outside).at[n]

    def columns(kind, n):
        return pl.ds(512 * n, 512) if kind == 0 else pl.ds(1280 * n, 1280)

    def source(kind, n, core):
        ref = in_ref if kind == 0 else out_ref
        return ref.at[:, core, :, columns(kind, n)]

    loads, swaps = [], []
    for k, (kind, n) in enumerate(chunks):
        load = pltpu.make_async_copy(source(kind, n, c), pick(kind, n, sum_in, sum_out), load_sem.at[k])
        swap = pltpu.make_async_remote_copy(
            source(kind, n, 1 - c), pick(kind, n, twin_in, twin_out), twin_send.at[k], twin_recv.at[k],
            device_id=device(twin), device_id_type=MESH)
        swap.start()
        load.start()
        loads.append(load)
        swaps.append(swap)

    y_far, y_up, y_down = lax.rem(y + 2, SIDE), up["y"], down["y"]
    height = {0: in_ref.shape[2], 1: out_ref.shape[2]}
    far, near_own, near_sum, flips, turns, keeps = {}, {}, {}, {}, {}, {}

    def remote(src, dst, send, recv, to):
        copy = pltpu.make_async_remote_copy(src, dst, send, recv, device_id=device(to), device_id_type=MESH)
        copy.start()
        return copy

    def stage_a(k):
        kind, n = chunks[k]
        rows = height[kind]
        sums, extra = pick(kind, n, sum_in, sum_out), pick(kind, n, twin_in, twin_out)
        fars, nears = pick(kind, n, far_in, far_out), pick(kind, n, near_in, near_out)
        h0, h1 = pl.ds(0, rows // 2), pl.ds(rows // 2, rows // 2)
        loads[k].wait()
        swaps[k].wait_recv()

        def add(block):
            def body(r):
                sums[block, r, :] = (sums[block, r, :].astype(F32) + extra[block, r, :].astype(F32)).astype(BF16)
            add_rows(rows, 32, body)
        add(y_far)
        far[k] = (remote(sums.at[y_far, h0], fars.at[0], far_send.at[k, 0], far_recv.at[k, 0], up),
                  remote(sums.at[y_far, h1], fars.at[1], far_send.at[k, 1], far_recv.at[k, 1], down))
        add(y_up)
        add(y_down)
        near_own[k] = (remote(sums.at[y_up, h1], nears.at[0, h1], near_send.at[k, 0], near_recv.at[k, 0], up),
                       remote(sums.at[y_down, h0], nears.at[1, h0], near_send.at[k, 1], near_recv.at[k, 1], down))
        add(y)

    def stage_b(k):
        kind, n = chunks[k]
        rows = height[kind]
        half = rows // 2
        sums = pick(kind, n, sum_in, sum_out)
        fars, nears = pick(kind, n, far_in, far_out), pick(kind, n, near_in, near_out)
        h0, h1 = pl.ds(0, half), pl.ds(half, half)
        far[k][0].wait_recv()

        def low(r):
            sums[y_up, r, :] = (sums[y_up, r, :].astype(F32) + fars[0, r, :].astype(F32)).astype(BF16)
        add_rows(half, 32, low)
        first = remote(sums.at[y_up, h0], nears.at[0, h0], near_send.at[k, 2], near_recv.at[k, 2], up)
        far[k][1].wait_recv()

        def high(i, carry):
            r = pl.ds(pl.multiple_of(i * 32, 32), 32)
            s = pl.ds(pl.multiple_of(i * 32 + half, 32), 32)
            sums[y_down, s, :] = (sums[y_down, s, :].astype(F32) + fars[1, r, :].astype(F32)).astype(BF16)
            return carry
        lax.fori_loop(0, half // 32, high, 0)
        near_sum[k] = (first, remote(sums.at[y_down, h1], nears.at[1, h1], near_send.at[k, 3], near_recv.at[k, 3], down))

    def stage_c(k):
        kind, n = chunks[k]
        rows = height[kind]
        sums = pick(kind, n, sum_in, sum_out)
        nears = pick(kind, n, near_in, near_out)
        done = pick(kind, n, done_in, done_out)
        for copy in near_own[k] + near_sum[k]:
            copy.wait_recv()

        def body(r):
            done[r, :] = (sums[y, r, :].astype(F32) + nears[0, r, :].astype(F32) + nears[1, r, :].astype(F32)).astype(BF16)
        add_rows(rows, 32, body)
        mates = stage_in if kind == 0 else stage_out
        flips[k] = (remote(done, mates.at[0, n], mate_send.at[k, 0], mate_recv.at[k, 0], x_flip),
                    remote(done, mates.at[2, n], mate_send.at[k, 2], mate_recv.at[k, 2], z_flip))
        result = own_in if kind == 0 else own_out
        keeps[k] = [pltpu.make_async_copy(done, result.at[:, columns(kind, n)], keep_sem.at[k, 4])]
        keeps[k][0].start()

    def keep(k, level):
        kind, n = chunks[k]
        mates, result = (stage_in, mate_in) if kind == 0 else (stage_out, mate_out)
        copy = pltpu.make_async_copy(mates.at[level, n], result.at[level, :, columns(kind, n)], keep_sem.at[k, level])
        copy.start()
        keeps[k].append(copy)

    def stage_d(k):
        kind, n = chunks[k]
        mates = stage_in if kind == 0 else stage_out
        flips[k][0].wait_recv()
        first = remote(mates.at[0, n], mates.at[1, n], mate_send.at[k, 1], mate_recv.at[k, 1], x_turn)
        flips[k][1].wait_recv()
        turns[k] = (first, remote(mates.at[2, n], mates.at[3, n], mate_send.at[k, 3], mate_recv.at[k, 3], z_turn))
        keep(k, 0)
        keep(k, 2)

    for t in range(total + 3):
        if t < total:
            stage_a(t)
        if 0 <= t - 1 < total:
            stage_b(t - 1)
        if 0 <= t - 2 < total:
            stage_c(t - 2)
        if 0 <= t - 3 < total:
            stage_d(t - 3)
    for k in range(total):
        turns[k][0].wait_recv()
        keep(k, 1)
        turns[k][1].wait_recv()
        keep(k, 3)
    for k in range(total):
        swaps[k].wait_send()
        for copy in far[k] + near_own[k] + near_sum[k] + flips[k] + turns[k]:
            copy.wait_send()
        for copy in keeps[k]:
            copy.wait()


def reduce_and_trade(term_in, term_out):
    ri, ro = term_in.shape[0] // 8, term_out.shape[0] // 8
    ci, co = term_in.shape[1], term_out.shape[1]
    wi, wo = ci // N_IN, co // N_OUT
    hbm = pl.BlockSpec(memory_space=pl.ANY)
    dma = pltpu.SemaphoreType.DMA
    n = N_IN + N_OUT
    return pl.pallas_call(
        reduce_kernel,
        out_shape=(
            jax.ShapeDtypeStruct((ri, ci), BF16), jax.ShapeDtypeStruct((ro, co), BF16),
            jax.ShapeDtypeStruct((4, ri, ci), BF16), jax.ShapeDtypeStruct((4, ro, co), BF16),
        ),
        in_specs=[hbm, hbm],
        out_specs=(hbm,) * 4,
        scratch_shapes=[
            pltpu.VMEM((N_IN, 4, ri, wi), BF16), pltpu.VMEM((N_OUT, 4, ro, wo), BF16),
            pltpu.VMEM((N_IN, 4, ri, wi), BF16), pltpu.VMEM((N_OUT, 4, ro, wo), BF16),
            pltpu.VMEM((N_IN, 2, ri // 2, wi), BF16), pltpu.VMEM((N_OUT, 2, ro // 2, wo), BF16),
            pltpu.VMEM((N_IN, 2, ri, wi), BF16), pltpu.VMEM((N_OUT, 2, ro, wo), BF16),
            dma((n,)), dma((n,)), dma((n,)),
            dma((n, 2)), dma((n, 2)), dma((n, 4)), dma((n, 4)), dma((n, 4)), dma((n, 4)), dma((n, 5)),
            pltpu.VMEM((4, N_IN, ri, wi), BF16), pltpu.VMEM((4, N_OUT, ro, wo), BF16),
            pltpu.VMEM((N_IN, ri, wi), BF16), pltpu.VMEM((N_OUT, ro, wo), BF16),
        ],
        compiler_params=pltpu.CompilerParams(collective_id=1, has_side_effects=True, vmem_limit_bytes=56 * 2**20),
        name="reduce_and_trade",
    )(term_in.reshape(4, 2, ri, ci), term_out.reshape(4, 2, ro, co))


QUERY_HEADS = 4
KEY_VALUE_HEADS = 2
HEAD_DIM = 256
WINDOW = 1024


epsilon = 1e-06
masked_score = -1e30


def shifted(block, axis, distance):
    devices = range(lax.axis_size(axis))
    route = [(i - distance, i) for i in devices if i - distance in devices]
    return lax.ppermute(block, axis, route)


def norm_rows(inputs, norm_gain):
    values = inputs.astype(jnp.float32)
    power = jnp.mean(values * values, axis=-1, keepdims=True)
    return (values * lax.rsqrt(power + epsilon) * norm_gain).astype(jnp.bfloat16)


def doc_index(positions, lengths):
    count = lengths.shape[-1]
    upto = jnp.arange(count)[:, None] >= jnp.arange(count)[None, :]
    endings = jnp.sum(jnp.where(upto[None], lengths[:, None, :], 0), axis=-1)
    return jnp.sum((endings[:, None, :] <= positions[:, :, None]).astype(jnp.int32), axis=-1)


def allowed(query_pos, key_pos, lengths):
    query_doc = doc_index(query_pos, lengths)
    key_doc = doc_index(key_pos, lengths)
    distance = query_pos[:, :, None] - key_pos[:, None, :]
    same_doc = query_doc[:, :, None] == key_doc[:, None, :]
    return (key_pos[:, None, :] >= 0) & same_doc & (distance >= 0) & (distance < WINDOW)


def split_heads(query_rows, key_tile, value_tile):
    batch_count, query_length, _ = query_rows.shape
    key_length = key_tile.shape[1]
    query_heads = query_rows.reshape(
        batch_count, query_length, KEY_VALUE_HEADS, QUERY_HEADS // KEY_VALUE_HEADS, HEAD_DIM
    )
    key_heads = key_tile.reshape(batch_count, key_length, KEY_VALUE_HEADS, HEAD_DIM)
    value_heads = value_tile.reshape(batch_count, key_length, KEY_VALUE_HEADS, HEAD_DIM)
    return (query_heads, key_heads, value_heads)


def attend(query_rows, key_tile, value_tile, mask):
    query_heads, key_heads, value_heads = split_heads(query_rows, key_tile, value_tile)
    scores = jnp.einsum(
        "btkgd,bskd->bkgts", query_heads, key_heads, preferred_element_type=jnp.float32
    ) * HEAD_DIM ** (-0.5)
    allowed_mask = mask[:, None, None, :, :]
    scores = jnp.where(allowed_mask, scores, masked_score)
    row_max = jnp.max(scores, axis=-1, keepdims=True)
    raised = jnp.where(allowed_mask, jnp.exp(scores - row_max), 0.0)
    attn_probs = (raised / jnp.sum(raised, axis=-1, keepdims=True)).astype(jnp.bfloat16)
    mixed_heads = jnp.einsum(
        "bkgts,bskd->btkgd", attn_probs, value_heads, preferred_element_type=jnp.float32
    )
    return (
        attn_probs,
        mixed_heads.reshape(
            query_rows.shape[0], query_rows.shape[1], QUERY_HEADS * HEAD_DIM
        ).astype(jnp.bfloat16),
    )


def attend_back(query_rows, key_tile, value_tile, attn_probs, blended_block, blended_gradient):
    query_heads, key_heads, value_heads = split_heads(query_rows, key_tile, value_tile)
    batch_count, query_length, _ = query_rows.shape
    key_length = key_tile.shape[1]
    gradient_heads = blended_gradient.reshape(
        batch_count, query_length, KEY_VALUE_HEADS, QUERY_HEADS // KEY_VALUE_HEADS, HEAD_DIM
    )
    output_heads = blended_block.reshape(
        batch_count, query_length, KEY_VALUE_HEADS, QUERY_HEADS // KEY_VALUE_HEADS, HEAD_DIM
    )
    prob_grads = jnp.einsum(
        "btkgd,bskd->bkgts", gradient_heads, value_heads, preferred_element_type=jnp.float32
    )
    row_dots = jnp.sum(
        gradient_heads.astype(jnp.float32) * output_heads.astype(jnp.float32), axis=-1
    )
    row_dots = jnp.transpose(row_dots, (0, 2, 3, 1))[..., None]
    score_grads = (
        attn_probs.astype(jnp.float32) * (prob_grads - row_dots) * HEAD_DIM ** (-0.5)
    ).astype(jnp.bfloat16)
    query_gradients = jnp.einsum(
        "bkgts,bskd->btkgd", score_grads, key_heads, preferred_element_type=jnp.float32
    )
    key_gradients = jnp.einsum(
        "bkgts,btkgd->bskd", score_grads, query_heads, preferred_element_type=jnp.float32
    )
    value_gradients = jnp.einsum(
        "bkgts,btkgd->bskd", attn_probs, gradient_heads, preferred_element_type=jnp.float32
    )
    return (
        query_gradients.reshape(batch_count, query_length, QUERY_HEADS * HEAD_DIM).astype(
            jnp.bfloat16
        ),
        key_gradients.reshape(batch_count, key_length, KEY_VALUE_HEADS * HEAD_DIM).astype(
            jnp.bfloat16
        ),
        value_gradients.reshape(batch_count, key_length, KEY_VALUE_HEADS * HEAD_DIM).astype(
            jnp.bfloat16
        ),
    )


def per_device(
    tokens, target, rewards, doc_lengths, norm_gain, w_query, w_key, w_value, w_out, gossip_bit
):
    seq_count, shard_len, model_width = (tokens.shape[1], tokens.shape[2], tokens.shape[3])
    query_width = w_query.shape[1]
    key_feature_width = w_key.shape[1]
    row_count = seq_count * shard_len
    reach_blocks = WINDOW // shard_len
    span_len = (reach_blocks + 1) * shard_len
    ctx_index = lax.axis_index("ctx")
    lengths = doc_lengths[0]
    normed = norm_rows(tokens[0], norm_gain)
    flat_rows = normed.reshape(row_count, model_width)
    weights_in, out_whole = gather_weights(w_query, w_key, w_value, w_out)
    sums = [jnp.dot(flat_rows, weights_in[n], preferred_element_type=jnp.float32) for n in range(4)]
    query_sum, key_sum, value_sum = jnp.concatenate(sums[:2], axis=1), sums[2], sums[3]
    query_rows = query_sum.astype(jnp.bfloat16).reshape(seq_count, shard_len, query_width)
    key_own = key_sum.astype(jnp.bfloat16).reshape(seq_count, shard_len, key_feature_width)
    value_own = value_sum.astype(jnp.bfloat16).reshape(seq_count, shard_len, key_feature_width)
    key_parts = []
    value_parts = []
    for offset in range(reach_blocks, 0, -1):
        moved = shifted((key_own, value_own), "ctx", offset)
        key_parts.append(moved[0])
        value_parts.append(moved[1])
    key_tile = jnp.concatenate(key_parts + [key_own], axis=1)
    value_tile = jnp.concatenate(value_parts + [value_own], axis=1)
    query_pos = jnp.broadcast_to(
        ctx_index * shard_len + jnp.arange(shard_len, dtype=jnp.int32), (seq_count, shard_len)
    )
    key_pos = jnp.broadcast_to(
        (ctx_index - reach_blocks) * shard_len + jnp.arange(span_len, dtype=jnp.int32),
        (seq_count, span_len),
    )
    mask = allowed(query_pos, key_pos, lengths)
    attn_probs, mixed_heads = attend(query_rows, key_tile, value_tile, mask)
    mixed_flat = mixed_heads.reshape(row_count, query_width)
    update = jnp.dot(mixed_flat, out_whole, preferred_element_type=jnp.float32)
    result = tokens[0].reshape(row_count, model_width).astype(jnp.float32) + update
    delta_rows = (
        rewards[0].reshape(row_count, 1)
        * (result - target[0].reshape(row_count, model_width).astype(jnp.float32))
    ).astype(jnp.bfloat16)
    blended_gradient = lax.dot_general(
        delta_rows, out_whole, (((1,), (1,)), ((), ())), preferred_element_type=jnp.float32
    )
    blended_gradient = blended_gradient.astype(jnp.bfloat16).reshape(
        seq_count, shard_len, query_width
    )
    query_gradients, key_terms, value_terms = attend_back(
        query_rows, key_tile, value_tile, attn_probs, mixed_heads, blended_gradient
    )
    own_start = reach_blocks * shard_len
    key_total = key_terms[:, own_start:].astype(jnp.float32)
    value_total = value_terms[:, own_start:].astype(jnp.float32)
    for offset in range(1, reach_blocks + 1):
        low_row = (reach_blocks - offset) * shard_len
        returned = shifted(
            (
                key_terms[:, low_row : low_row + shard_len],
                value_terms[:, low_row : low_row + shard_len],
            ),
            "ctx",
            -offset,
        )
        key_total = key_total + returned[0].astype(jnp.float32)
        value_total = value_total + returned[1].astype(jnp.float32)
    key_final = key_total.astype(jnp.bfloat16)
    value_final = value_total.astype(jnp.bfloat16)
    joined = jnp.concatenate([query_gradients, key_final, value_final], axis=-1).reshape(
        row_count, query_width + 2 * key_feature_width
    )
    term_in = lax.dot_general(
        flat_rows, joined, (((0,), (0,)), ((), ())), preferred_element_type=jnp.float32
    ).astype(jnp.bfloat16)
    term_out = lax.dot_general(
        mixed_flat, delta_rows, (((0,), (0,)), ((), ())), preferred_element_type=jnp.float32
    ).astype(jnp.bfloat16)
    grad_inputs, grad_outputs, mates_in, mates_out = reduce_and_trade(term_in, term_out)
    own_bit = gossip_bit[0]
    partner_inputs, partner_outputs = mates_in[0], mates_out[0]
    for level in range(1, 4):
        partner_inputs = jnp.where(own_bit == level, mates_in[level], partner_inputs)
        partner_outputs = jnp.where(own_bit == level, mates_out[level], partner_outputs)
    mean_inputs = (grad_inputs.astype(jnp.float32) + partner_inputs.astype(jnp.float32)) * 0.5
    mean_outputs = (grad_outputs.astype(jnp.float32) + partner_outputs.astype(jnp.float32)) * 0.5
    return (
        mean_inputs[None, :, :query_width],
        mean_inputs[None, :, query_width : query_width + key_feature_width],
        mean_inputs[None, :, query_width + key_feature_width :],
        mean_outputs[None],
    )


def solution(mesh):
    placed = (
        P("dp", None, "ctx", None),
        P("dp", None, "ctx", None),
        P("dp", None, "ctx"),
        P("dp", None, None),
        P(),
        P(("dp", "ctx"), None),
        P(("dp", "ctx"), None),
        P(("dp", "ctx"), None),
        P(("dp", "ctx"), None),
        P("dp"),
    )
    return jax.shard_map(
        per_device,
        mesh=mesh,
        in_specs=placed,
        out_specs=(
            P("dp", "ctx", None),
            P("dp", "ctx", None),
            P("dp", "ctx", None),
            P("dp", "ctx", None),
        ),
        check_vma=False,
    )
```

```python
import functools
import jax
import jax.numpy as jnp
from jax import lax
from jax.experimental import pallas as pl
from jax.experimental.pallas import tpu as pltpu
from jax.sharding import PartitionSpec as P

MESH = pl.DeviceIdType.MESH
BF16 = jnp.bfloat16
F32 = jnp.float32
WINDOW = 1024

epsilon = 1e-06
masked_score = -1e30

SIDE = 4


def place():
    dp, ctx = lax.axis_index("dp"), lax.axis_index("ctx")
    return {"x": lax.rem(dp, SIDE), "z": lax.div(dp, SIDE), "y": lax.div(ctx, 2), "c": lax.rem(ctx, 2)}


def device(at):
    return (at["z"] * SIDE + at["x"], at["y"] * 2 + at["c"])


def beside(at, axis, step):
    return {**at, axis: lax.rem(at[axis] + step + SIDE, SIDE)}


def sibling(at):
    return {**at, "c": 1 - at["c"]}


def greet(peers):
    barrier = pltpu.get_barrier_semaphore()
    for peer in peers:
        pl.semaphore_signal(barrier, inc=1, device_id=device(peer), device_id_type=MESH)
    pl.semaphore_wait(barrier, len(peers))


def gather_kernel(rows_in, rows_out, in_ref, out_ref, x_ref, p_ref, w_out, w_in, slots_in, slots_out, wide, block_in,
                  block_out, swap_send, swap_recv, pair_sem, local_sem, ring_send, ring_recv, twin_send, twin_recv):
    at = place()
    c = at["c"]
    ctx = at["y"] * 2 + c
    twin = sibling(at)
    others = [lax.rem(ctx + k, 8) for k in range(1, 8)]
    group = [{**at, "y": lax.div(j, 2), "c": lax.rem(j, 2)} for j in others]
    greet([beside(at, "x", 1), beside(at, "x", -1), beside(at, "z", 1), beside(at, "z", -1)] + group)

    copies = []
    for k in range(7):
        copies.append(pltpu.make_async_remote_copy(
            in_ref.at[others[k]], slots_in.at[ctx], swap_send.at[k], swap_recv.at[k],
            device_id=device(group[k]), device_id_type=MESH))
    pair = pltpu.make_async_remote_copy(
        out_ref.at[1 - c], slots_out.at[c], pair_sem.at[0], pair_sem.at[1], device_id=device(twin), device_id_type=MESH)
    pair.start()
    for copy in copies:
        copy.start()
    slots_in[ctx] = in_ref[ctx]
    slots_out[c] = out_ref[c]
    pair.wait()
    block_out[0, 0, 0] = jnp.concatenate(
        [slots_out[0].astype(F32)[:rows_out], slots_out[1].astype(F32)[:rows_out]], axis=0).astype(BF16)
    for copy in copies:
        copy.wait()
    for j in range(8):
        wide[rows_in * j:rows_in * (j + 1)] = slots_in[j].astype(F32)[:rows_in]
    block_in[0, 0, 0] = wide[...].astype(BF16)

    half_rows = rows_in * 4
    one = {a: pl.ds(at[a], 1) for a in "xyz"}
    whole = pl.ds(0, SIDE)

    def view(part, where, core):
        if part == 2:
            return w_out.at[where["z"], where["x"], where["y"], :, pl.ds(pl.multiple_of(core * 1280, 128), 1280)]
        rows = pl.ds(half_rows * part, half_rows)
        return w_in.at[where["y"], where["z"], where["x"], rows, pl.ds(pl.multiple_of(core * 256, 128), 256)]

    def rest(part):
        return [
            pltpu.make_async_copy(block_in.at[:, :, :, pl.ds(half_rows * p, half_rows), :] if p < 2 else block_out,
                                  view(p, one, c), local_sem.at[p])
            for p in part]

    stores = rest(range(3))
    for copy in stores:
        copy.start()
    for copy in stores:
        copy.wait()

    orders = ("xyz", "yzx", "zxy")
    twins, sends = [], []

    def to_twin(part, where, slot):
        copy = pltpu.make_async_remote_copy(
            view(part, where, c), view(part, where, c), twin_send.at[part, slot], twin_recv.at[part, slot],
            device_id=device(twin), device_id_type=MESH)
        copy.start()
        twins.append(copy)

    def ring(part, phase, slot, where, step):
        axis = orders[part][phase]
        copy = pltpu.make_async_remote_copy(
            view(part, where, c), view(part, where, c), ring_send.at[part, phase, slot], ring_recv.at[part, phase, slot],
            device_id=device(beside(at, axis, step)), device_id_type=MESH)
        copy.start()
        sends.append(copy)
        return copy

    for phase in range(3):
        def known(part, shift, half):
            order = orders[part]
            where = dict(one)
            for a in order[:phase]:
                where[a] = whole
            if phase and half is not None:
                where[order[0]] = pl.ds(2 * half, 2)
            axis = order[phase]
            where[axis] = pl.ds(lax.rem(at[axis] + shift + SIDE, SIDE), 1)
            return where

        first, last = {}, {}
        halves = (0, 1) if phase else (None,)
        for part in range(3):
            if phase:
                first[part] = (ring(part, phase, 0, known(part, 0, 0), 1), ring(part, phase, 1, known(part, 0, 1), -1))
                last[part] = [ring(part, phase, 2, known(part, 0, 1), 1), ring(part, phase, 3, known(part, 0, 0), -1)]
            else:
                first[part] = (ring(part, 0, 0, known(part, 0, None), 1),)
                last[part] = [ring(part, 0, 1, known(part, 0, None), -1)]
        if phase == 2:
            for part in range(3):
                to_twin(part, known(part, 0, None), 0)
        for part in range(3):
            if phase:
                first[part][0].wait_recv()
                last[part].append(ring(part, phase, 4, known(part, -1, 0), 1))
                first[part][1].wait_recv()
                last[part].append(ring(part, phase, 5, known(part, 1, 1), -1))
                if phase == 2:
                    to_twin(part, known(part, -1, 0), 1)
                    to_twin(part, known(part, 1, 1), 2)
            else:
                first[part][0].wait_recv()
                last[part].append(ring(part, 0, 4, known(part, -1, None), 1))
        for n in range(4):
            for part in range(3):
                if n < len(last[part]):
                    last[part][n].wait_recv()
                    if phase == 2:
                        shift, half = ((-1, 1), (1, 0), (-2, 0), (2, 1))[n]
                        to_twin(part, known(part, shift, half), 3 + n)
    for copy in twins:
        copy.wait_recv()

    def project(n, carry):
        weights = w_in[n].reshape(128 * rows_in, 512)
        p_ref[n] = jnp.dot(x_ref[...], weights, preferred_element_type=F32).astype(BF16)
        return carry
    lax.fori_loop(0, 4, project, 0)
    for copy in sends + twins:
        copy.wait_send()


def gather_and_project(normed, w_query, w_key, w_value, w_out):
    rows_in, rows_out = w_query.shape[0], w_out.shape[0]
    joined = jnp.concatenate([w_query, w_key, w_value], axis=1)
    pieces_in = jnp.pad(joined.reshape(rows_in, 8, 256).transpose(1, 0, 2), ((0, 0), (0, 32 - rows_in), (0, 0)))
    pieces_out = jnp.pad(w_out.reshape(rows_out, 2, 1280).transpose(1, 0, 2), ((0, 0), (0, 16 - rows_out), (0, 0)))
    vmem = pl.BlockSpec(memory_space=pltpu.VMEM)
    hbm = pl.BlockSpec(memory_space=pl.ANY)
    dma = pltpu.SemaphoreType.DMA
    projected, whole_out = pl.pallas_call(
        functools.partial(gather_kernel, rows_in, rows_out),
        out_shape=(
            jax.ShapeDtypeStruct((4, normed.shape[0], 512), BF16),
            jax.ShapeDtypeStruct((SIDE, SIDE, SIDE, 2 * rows_out, 2560), BF16),
        ),
        in_specs=[vmem, vmem, vmem],
        out_specs=(vmem, hbm),
        scratch_shapes=[
            pltpu.VMEM((SIDE, SIDE, SIDE, 8 * rows_in, 512), BF16),
            pltpu.VMEM((8, 32, 256), BF16),
            pltpu.VMEM((2, 16, 1280), BF16),
            pltpu.VMEM((8 * rows_in, 256), F32),
            pltpu.VMEM((1, 1, 1, 8 * rows_in, 256), BF16),
            pltpu.VMEM((1, 1, 1, 2 * rows_out, 1280), BF16),
            dma((7,)), dma((7,)), dma((2,)), dma((3,)),
            dma((3, 3, 6)), dma((3, 3, 6)), dma((3, 7)), dma((3, 7)),
        ],
        compiler_params=pltpu.CompilerParams(
            collective_id=0, has_side_effects=True, vmem_limit_bytes=40 * 2**20),
        name="gather_and_project",
    )(pieces_in, pieces_out, normed)
    return projected, whole_out.reshape(128 * rows_out, 2560)


def add_rows(count, step, body):
    def at(i, carry):
        body(pl.ds(pl.multiple_of(i * step, step), step))
        return carry
    lax.fori_loop(0, count // step, at, 0)


HEADS, GROUPS, ROWS, WIDE = 4, 2, 256, 2560
NEAR_UP = 64
NEAR_MID = 160
FAR_DOWN = 80
FAR_MID = 160
CHUNKS = ((1, 0), (1, 1), (0, 0), (0, 1), (0, 2), (0, 3))


def dot(a, b, contract=((1,), (0,))):
    return lax.dot_general(a, b, (contract, ((), ())), preferred_element_type=F32)


def layer_kernel(p_ref, mask_ref, rewards_ref, normed_ref, tokens_ref, target_ref, weight_ref,
                 own_in, own_out, mate_in, mate_out, *scratch):
    (queries, kv, kv_relay, probs, scores, terms, term_mate, term_next, term_far, term_relay, term_end, x_one, x_two,
     weight, turned, mixed, mixed_turned, mixed_grad, joined,
     give_in, give_out, sum_in, sum_out, twin_in, twin_out, far_in, far_out, near_in, near_out, done_in, done_out,
     read_sem, kv_send, kv_recv, term_send, term_recv, twin_send, twin_recv,
     far_send, far_recv, near_send, near_recv, mate_send, mate_recv, keep_sem) = scratch
    at = place()
    c, y = at["c"], at["y"]
    twin = sibling(at)
    up, down = beside(at, "y", 1), beside(at, "y", -1)
    x_flip = {**at, "x": at["x"] + 1 - 2 * lax.rem(at["x"], 2)}
    x_turn = {**at, "x": SIDE - 1 - at["x"]}
    z_flip = {**at, "z": at["z"] + 1 - 2 * lax.rem(at["z"], 2)}
    z_turn = {**at, "z": SIDE - 1 - at["z"]}
    sent = []

    def remote(src, dst, send, recv, to):
        copy = pltpu.make_async_remote_copy(src, dst, send, recv, device_id=device(to), device_id_type=MESH)
        copy.start()
        sent.append(copy)
        return copy

    def read(src, dst, n):
        copy = pltpu.make_async_copy(src, dst, read_sem.at[n])
        copy.start()
        return copy

    read_normed = read(normed_ref, x_one, 0)
    for n in range(2):
        for g in range(2):
            queries[2 * n + g] = p_ref[n, :, 256 * g:256 * g + 256]
            kv[4 + c, 2 * n + g] = p_ref[2 + n, :, 256 * g:256 * g + 256]
    greet([twin, up, down, x_flip, x_turn, z_flip, z_turn])

    def rows_of(slot, low, high):
        return kv.at[slot, :, pl.ds(low, high - low), :]

    def kv_move(src, dst, n, to):
        return remote(src, dst, kv_send.at[n], kv_recv.at[n], to)

    here, before, first = 4 + c, 2 + c, c
    a0 = kv_move(rows_of(here, 0, NEAR_UP), rows_of(before, 0, NEAR_UP), 0, up)
    b0 = kv_move(rows_of(here, NEAR_UP, NEAR_MID), kv_relay.at[:, pl.ds(0, NEAR_MID - NEAR_UP), :], 1, down)
    a1 = kv_move(rows_of(here, NEAR_UP, ROWS), rows_of(before, NEAR_UP, ROWS), 2, up)
    b1 = kv_move(rows_of(here, NEAR_MID, ROWS), kv_relay.at[:, pl.ds(NEAR_MID - NEAR_UP, ROWS - NEAR_MID), :], 3, down)
    t0 = kv_move(kv.at[here], kv.at[here], 4, twin)
    read_weight = read(weight_ref, weight, 1)
    read_tokens = read(tokens_ref, x_two, 2)

    read_normed.wait()

    def turn(i, carry):
        cols = pl.ds(pl.multiple_of(i * 128, 128), 128)
        turned[cols, :] = x_one[:, cols].astype(F32).T.astype(BF16)
        return carry

    a0.wait_recv()
    a2 = kv_move(rows_of(before, 0, NEAR_UP), rows_of(first, 0, NEAR_UP), 5, up)
    lax.fori_loop(0, 10, turn, 0)
    b0.wait_recv()
    b2 = kv_move(kv_relay.at[:, pl.ds(0, NEAR_MID - NEAR_UP), :], rows_of(first, NEAR_UP, NEAR_MID), 6, down)
    lax.fori_loop(10, WIDE // 128, turn, 0)
    read_target = read(target_ref, x_one, 3)
    b1.wait_recv()
    b3 = kv_move(kv_relay.at[:, pl.ds(NEAR_MID - NEAR_UP, ROWS - NEAR_MID), :], rows_of(first, NEAR_MID, ROWS), 7, down)
    a1.wait_recv()
    t1 = kv_move(kv.at[before], kv.at[before], 8, twin)
    a2.wait_recv()
    b2.wait_recv()
    t2 = kv_move(rows_of(first, 0, NEAR_MID), rows_of(first, 0, NEAR_MID), 9, twin)
    b3.wait_recv()
    t3 = kv_move(rows_of(first, NEAR_MID, ROWS), rows_of(first, NEAR_MID, ROWS), 10, twin)
    for copy in (t0, t1, t2, t3):
        copy.wait_recv()

    def tile(n):
        return kv[pl.ds(c, 5), n].reshape(5 * ROWS, 256)

    def attend(h, carry):
        g = h // 2
        seen = mask_ref[...] > 0.5
        score = dot(queries[h], tile(g), ((1,), (1,))) * 256 ** -0.5
        score = jnp.where(seen, score, masked_score)
        raised = jnp.where(seen, jnp.exp(score - jnp.max(score, axis=1, keepdims=True)), 0.0)
        prob = (raised / jnp.sum(raised, axis=1, keepdims=True)).astype(BF16)
        probs[h] = prob
        out = dot(prob, tile(2 + g))
        mixed[h] = out.astype(BF16)
        rounded = out.astype(BF16).astype(F32).T.astype(BF16)
        mixed_turned[2 * h] = rounded[:128]
        mixed_turned[2 * h + 1] = rounded[128:]
        return carry
    lax.fori_loop(0, HEADS, attend, 0)

    for copy in (read_weight, read_tokens, read_target):
        copy.wait()

    def error(i, carry):
        cols = pl.ds(pl.multiple_of(i * 512, 512), 512)
        update = sum(dot(mixed[h], weight[256 * h:256 * h + 256, cols]) for h in range(HEADS))
        result = x_two[:, cols].astype(F32) + update
        x_two[:, cols] = (rewards_ref[...] * (result - x_one[:, cols].astype(F32))).astype(BF16)
        return carry
    lax.fori_loop(0, WIDE // 512, error, 0)
    delta = x_two

    y_far, y_up, y_down = lax.rem(y + 2, SIDE), up["y"], down["y"]
    height = {0: WIDE // 8, 1: HEADS * 256 // 8}
    swaps, far, near_own, near_sum, flips, turns, keeps = {}, {}, {}, {}, {}, {}, {}

    def pick(k, inside, outside):
        kind, n = CHUNKS[k]
        return (outside if kind else inside).at[n]

    def columns(k):
        kind, n = CHUNKS[k]
        return pl.ds(1280 * n, 1280) if kind else pl.ds(512 * n, 512)

    def term(k, dst, core):
        kind, n = CHUNKS[k]

        def body(i, carry):
            j = 2 * i + core
            if kind:
                dst[i] = dot(mixed_turned[j], delta[:, 1280 * n:1280 * n + 1280]).astype(BF16)
            else:
                rows = pl.ds(pl.multiple_of(j * 320, 64), 320)
                dst[i] = dot(turned[rows, :], joined[n]).astype(BF16)
            return carry
        lax.fori_loop(0, 4, body, 0)

    def stage_1(k):
        kind, n = CHUNKS[k]
        give = give_out.at[n] if kind else give_in.at[n % 2]
        if k >= 4:
            swaps[k - 2].wait_send()
        term(k, give, 1 - c)
        swaps[k] = pltpu.make_async_remote_copy(
            give, pick(k, twin_in, twin_out), twin_send.at[k], twin_recv.at[k], device_id=device(twin), device_id_type=MESH)
        swaps[k].start()
        term(k, pick(k, sum_in, sum_out), c)

    def stage_2(k):
        rows = height[CHUNKS[k][0]]
        sums, extra = pick(k, sum_in, sum_out), pick(k, twin_in, twin_out)
        fars, nears = pick(k, far_in, far_out), pick(k, near_in, near_out)
        h0, h1 = pl.ds(0, rows // 2), pl.ds(rows // 2, rows // 2)
        swaps[k].wait_recv()

        def add(block):
            def body(r):
                sums[block, r, :] = (sums[block, r, :].astype(F32) + extra[block, r, :].astype(F32)).astype(BF16)
            add_rows(rows, 32, body)
        add(y_far)
        far[k] = (remote(sums.at[y_far, h0], fars.at[0], far_send.at[k, 0], far_recv.at[k, 0], up),
                  remote(sums.at[y_far, h1], fars.at[1], far_send.at[k, 1], far_recv.at[k, 1], down))
        add(y_up)
        add(y_down)
        near_own[k] = (remote(sums.at[y_up, h1], nears.at[0, h1], near_send.at[k, 0], near_recv.at[k, 0], up),
                       remote(sums.at[y_down, h0], nears.at[1, h0], near_send.at[k, 1], near_recv.at[k, 1], down))
        add(y)

    def stage_3(k):
        rows = height[CHUNKS[k][0]]
        half = rows // 2
        sums = pick(k, sum_in, sum_out)
        fars, nears = pick(k, far_in, far_out), pick(k, near_in, near_out)
        h0, h1 = pl.ds(0, half), pl.ds(half, half)
        far[k][0].wait_recv()

        def low(r):
            sums[y_up, r, :] = (sums[y_up, r, :].astype(F32) + fars[0, r, :].astype(F32)).astype(BF16)
        add_rows(half, 32, low)
        one = remote(sums.at[y_up, h0], nears.at[0, h0], near_send.at[k, 2], near_recv.at[k, 2], up)
        far[k][1].wait_recv()

        def high(i, carry):
            r = pl.ds(pl.multiple_of(i * 32, 32), 32)
            s = pl.ds(pl.multiple_of(i * 32 + half, 32), 32)
            sums[y_down, s, :] = (sums[y_down, s, :].astype(F32) + fars[1, r, :].astype(F32)).astype(BF16)
            return carry
        lax.fori_loop(0, half // 32, high, 0)
        near_sum[k] = (one, remote(sums.at[y_down, h1], nears.at[1, h1], near_send.at[k, 3], near_recv.at[k, 3], down))

    def mates(k, level):
        return (mate_out if CHUNKS[k][0] else mate_in).at[level, :, columns(k)]

    def stage_4(k):
        kind, n = CHUNKS[k]
        sums, nears, done = pick(k, sum_in, sum_out), pick(k, near_in, near_out), pick(k, done_in, done_out)
        for copy in near_own[k] + near_sum[k]:
            copy.wait_recv()

        def body(r):
            done[r, :] = (sums[y, r, :].astype(F32) + nears[0, r, :].astype(F32) + nears[1, r, :].astype(F32)).astype(BF16)
        add_rows(height[kind], 32, body)
        flips[k] = (remote(done, mates(k, 0), mate_send.at[k, 0], mate_recv.at[k, 0], x_flip),
                    remote(done, mates(k, 2), mate_send.at[k, 2], mate_recv.at[k, 2], z_flip))
        keeps[k] = pltpu.make_async_copy(done, (own_out if kind else own_in).at[:, columns(k)], keep_sem.at[k])
        keeps[k].start()

    def stage_5(k):
        flips[k][0].wait_recv()
        one = remote(mates(k, 0), mates(k, 1), mate_send.at[k, 1], mate_recv.at[k, 1], x_turn)
        flips[k][1].wait_recv()
        turns[k] = (one, remote(mates(k, 2), mates(k, 3), mate_send.at[k, 3], mate_recv.at[k, 3], z_turn))

    stage_1(0)
    stage_1(1)
    stage_2(0)

    def spread(h, carry):
        rows = pl.ds(pl.multiple_of(h * 256, 256), 256)
        mixed_grad[h] = dot(delta[...], weight[rows, :], ((1,), (1,))).astype(BF16)
        return carry
    lax.fori_loop(0, HEADS, spread, 0)
    stage_2(1)

    terms[5 * (1 - c)] = jnp.zeros((4, ROWS, 256), BF16)

    def back(g):
        for r in range(2):
            h = 2 * g + r
            grad = mixed_grad[h]
            row_dots = jnp.sum(grad.astype(F32) * mixed[h].astype(F32), axis=1, keepdims=True)
            prob_grads = dot(grad, tile(2 + g), ((1,), (1,)))
            score = (probs[h].astype(F32) * (prob_grads - row_dots) * 256 ** -0.5).astype(BF16)
            scores[r] = score
            joined[g, :, 256 * r:256 * r + 256] = dot(score, tile(g)).astype(BF16)
        key_terms = dot(scores[0], queries[2 * g], ((0,), (0,))) + dot(scores[1], queries[2 * g + 1], ((0,), (0,)))
        terms[pl.ds(c, 5), g] = key_terms.astype(BF16).reshape(5, ROWS, 256)
        value_terms = (dot(probs[2 * g], mixed_grad[2 * g], ((0,), (0,)))
                       + dot(probs[2 * g + 1], mixed_grad[2 * g + 1], ((0,), (0,))))
        terms[pl.ds(c, 5), 2 + g] = value_terms.astype(BF16).reshape(5, ROWS, 256)

    back(0)
    stage_3(0)
    back(1)
    stage_3(1)

    def move(src, dst, n, to):
        return remote(src, dst, term_send.at[n], term_recv.at[n], to)

    to_mate = [move(terms.at[2 * n + 1 - c], term_mate.at[n], n, twin) for n in range(3)]
    stage_4(0)
    stage_1(2)

    def fold(n):
        to_mate[n].wait_recv()
        for q in range(4):
            def body(r):
                terms[2 * n + c, q, r, :] = (
                    terms[2 * n + c, q, r, :].astype(F32) + term_mate[n, q, r, :].astype(F32)).astype(BF16)
            add_rows(ROWS, 64, body)

    def part(ref, low, high, start=0):
        return ref.at[:, pl.ds(low - start, high - low), :]

    fold(0)
    s2 = terms.at[c]
    e0 = move(part(s2, 0, FAR_DOWN), term_far, 3, down)
    f0 = move(part(s2, FAR_DOWN, FAR_MID), part(term_relay, FAR_DOWN, FAR_MID, FAR_DOWN), 4, up)
    f1 = move(part(s2, FAR_MID, ROWS), part(term_relay, FAR_MID, ROWS, FAR_DOWN), 5, up)
    fold(1)
    s1 = terms.at[2 + c]
    e1 = move(part(s1, FAR_DOWN, ROWS), part(term_next, FAR_DOWN, ROWS), 6, down)
    fold(2)
    stage_1(3)
    stage_2(2)
    e0.wait_recv()
    for q in range(4):
        def join(r):
            terms[2 + c, q, r, :] = (terms[2 + c, q, r, :].astype(F32) + term_far[q, r, :].astype(F32)).astype(BF16)
        add_rows(FAR_DOWN, 16, join)
    e2 = move(part(s1, 0, FAR_DOWN), part(term_next, 0, FAR_DOWN), 7, down)
    f0.wait_recv()
    f2 = move(part(term_relay, FAR_DOWN, FAR_MID, FAR_DOWN), part(term_end, FAR_DOWN, FAR_MID, FAR_DOWN), 8, up)
    f1.wait_recv()
    f3 = move(part(term_relay, FAR_MID, ROWS, FAR_DOWN), part(term_end, FAR_MID, ROWS, FAR_DOWN), 9, up)
    stage_4(1)
    stage_2(3)
    stage_5(0)
    stage_3(2)
    for copy in (e1, e2, f2, f3):
        copy.wait_recv()
    for q in range(4):
        n, g = 2 + q // 2, q % 2
        joined[n, 0:FAR_DOWN, 256 * g:256 * g + 256] = (
            terms[4 + c, q, 0:FAR_DOWN, :].astype(F32) + term_next[q, 0:FAR_DOWN, :].astype(F32)).astype(BF16)
        joined[n, FAR_DOWN:ROWS, 256 * g:256 * g + 256] = (
            terms[4 + c, q, FAR_DOWN:ROWS, :].astype(F32) + term_next[q, FAR_DOWN:ROWS, :].astype(F32)
            + term_end[q].astype(F32)).astype(BF16)
    stage_1(4)
    stage_1(5)
    stage_2(4)
    stage_3(3)
    stage_4(2)
    stage_5(1)
    stage_2(5)
    stage_3(4)
    stage_4(3)
    stage_5(2)
    stage_3(5)
    stage_4(4)
    stage_5(3)
    stage_4(5)
    stage_5(4)
    stage_5(5)
    for k in range(6):
        turns[k][0].wait_recv()
        turns[k][1].wait_recv()
        keeps[k].wait()
    for k in (0, 1, 4, 5):
        swaps[k].wait_send()
    for copy in sent:
        copy.wait_send()


def layer_grads(projected, mask, rewards, normed, tokens, target, weight):
    vmem = pl.BlockSpec(memory_space=pltpu.VMEM)
    hbm = pl.BlockSpec(memory_space=pl.ANY)
    dma = pltpu.SemaphoreType.DMA
    ri, ro = WIDE // 8, HEADS * 256 // 8

    def held(*shape):
        return pltpu.VMEM(shape, BF16)

    return pl.pallas_call(
        layer_kernel,
        out_shape=(
            jax.ShapeDtypeStruct((ri, 2048), BF16), jax.ShapeDtypeStruct((ro, WIDE), BF16),
            jax.ShapeDtypeStruct((4, ri, 2048), BF16), jax.ShapeDtypeStruct((4, ro, WIDE), BF16),
        ),
        in_specs=[vmem, vmem, vmem, hbm, hbm, hbm, hbm],
        out_specs=(hbm,) * 4,
        scratch_shapes=[
            held(HEADS, ROWS, 256), held(6, 4, ROWS, 256), held(4, ROWS - NEAR_UP, 256),
            held(HEADS, ROWS, 5 * ROWS), held(2, ROWS, 5 * ROWS),
            held(6, 4, ROWS, 256), held(3, 4, ROWS, 256), held(4, ROWS, 256), held(4, FAR_DOWN, 256),
            held(4, ROWS - FAR_DOWN, 256), held(4, ROWS - FAR_DOWN, 256),
            held(ROWS, WIDE), held(ROWS, WIDE), held(HEADS * 256, WIDE), held(WIDE, ROWS),
            held(HEADS, ROWS, 256), held(8, 128, ROWS), held(HEADS, ROWS, 256), held(4, ROWS, 512),
            held(2, 4, ri, 512), held(2, 4, ro, 1280),
            held(4, 4, ri, 512), held(2, 4, ro, 1280), held(4, 4, ri, 512), held(2, 4, ro, 1280),
            held(4, 2, ri // 2, 512), held(2, 2, ro // 2, 1280), held(4, 2, ri, 512), held(2, 2, ro, 1280),
            held(4, ri, 512), held(2, ro, 1280),
            dma((4,)), dma((11,)), dma((11,)), dma((10,)), dma((10,)), dma((6,)), dma((6,)),
            dma((6, 2)), dma((6, 2)), dma((6, 4)), dma((6, 4)), dma((6, 4)), dma((6, 4)), dma((6,)),
        ],
        compiler_params=pltpu.CompilerParams(
            collective_id=1, has_side_effects=True, vmem_limit_bytes=62 * 2**20),
        name="layer_grads",
    )(projected, mask, rewards, normed, tokens, target, weight)


def norm_rows(inputs, norm_gain):
    values = inputs.astype(jnp.float32)
    power = jnp.mean(values * values, axis=-1, keepdims=True)
    return (values * lax.rsqrt(power + epsilon) * norm_gain).astype(jnp.bfloat16)


def doc_index(positions, lengths):
    count = lengths.shape[-1]
    upto = jnp.arange(count)[:, None] >= jnp.arange(count)[None, :]
    endings = jnp.sum(jnp.where(upto[None], lengths[:, None, :], 0), axis=-1)
    return jnp.sum((endings[:, None, :] <= positions[:, :, None]).astype(jnp.int32), axis=-1)


def allowed(query_pos, key_pos, lengths):
    query_doc = doc_index(query_pos, lengths)
    key_doc = doc_index(key_pos, lengths)
    distance = query_pos[:, :, None] - key_pos[:, None, :]
    same_doc = query_doc[:, :, None] == key_doc[:, None, :]
    return (key_pos[:, None, :] >= 0) & same_doc & (distance >= 0) & (distance < WINDOW)


def per_device(
    tokens, target, rewards, doc_lengths, norm_gain, w_query, w_key, w_value, w_out, gossip_bit
):
    shard_len = tokens.shape[2]
    query_width, key_width = w_query.shape[1], w_key.shape[1]
    reach_blocks = WINDOW // shard_len
    span_len = (reach_blocks + 1) * shard_len
    ctx_index = lax.axis_index("ctx")
    token_rows, target_rows = tokens[0, 0], target[0, 0]
    normed = norm_rows(token_rows, norm_gain)
    projected, out_whole = gather_and_project(normed, w_query, w_key, w_value, w_out)
    query_pos = (ctx_index * shard_len + jnp.arange(shard_len, dtype=jnp.int32))[None]
    key_pos = ((ctx_index - reach_blocks) * shard_len + jnp.arange(span_len, dtype=jnp.int32))[None]
    mask = allowed(query_pos, key_pos, doc_lengths[0])[0].astype(jnp.float32)
    grad_inputs, grad_outputs, mates_in, mates_out = layer_grads(
        projected, mask, rewards.reshape(shard_len, 1), normed, token_rows, target_rows, out_whole
    )
    own_bit = gossip_bit[0]
    partner_inputs, partner_outputs = mates_in[0], mates_out[0]
    for level in range(1, 4):
        partner_inputs = jnp.where(own_bit == level, mates_in[level], partner_inputs)
        partner_outputs = jnp.where(own_bit == level, mates_out[level], partner_outputs)
    mean_inputs = (grad_inputs.astype(jnp.float32) + partner_inputs.astype(jnp.float32)) * 0.5
    mean_outputs = (grad_outputs.astype(jnp.float32) + partner_outputs.astype(jnp.float32)) * 0.5
    return (
        mean_inputs[None, :, :query_width],
        mean_inputs[None, :, query_width : query_width + key_width],
        mean_inputs[None, :, query_width + key_width :],
        mean_outputs[None],
    )


def solution(mesh):
    placed = (
        P("dp", None, "ctx", None),
        P("dp", None, "ctx", None),
        P("dp", None, "ctx"),
        P("dp", None, None),
        P(),
        P(("dp", "ctx"), None),
        P(("dp", "ctx"), None),
        P(("dp", "ctx"), None),
        P(("dp", "ctx"), None),
        P("dp"),
    )
    return jax.shard_map(
        per_device,
        mesh=mesh,
        in_specs=placed,
        out_specs=(
            P("dp", "ctx", None),
            P("dp", "ctx", None),
            P("dp", "ctx", None),
            P("dp", "ctx", None),
        ),
        check_vma=False,
    )
```

```python
import functools
import jax
import jax.numpy as jnp
from jax import lax
from jax.experimental import pallas as pl
from jax.experimental.pallas import tpu as pltpu
from jax.sharding import PartitionSpec as P

MESH = pl.DeviceIdType.MESH
BF16 = jnp.bfloat16
F32 = jnp.float32
WINDOW = 1024

epsilon = 1e-06
masked_score = -1e30

SIDE = 4


def place():
    dp, ctx = lax.axis_index("dp"), lax.axis_index("ctx")
    return {"x": lax.rem(dp, SIDE), "z": lax.div(dp, SIDE), "y": lax.div(ctx, 2), "c": lax.rem(ctx, 2)}


def device(at):
    return (at["z"] * SIDE + at["x"], at["y"] * 2 + at["c"])


def beside(at, axis, step):
    return {**at, axis: lax.rem(at[axis] + step + SIDE, SIDE)}


def sibling(at):
    return {**at, "c": 1 - at["c"]}


def greet(peers):
    barrier = pltpu.get_barrier_semaphore()
    for peer in peers:
        pl.semaphore_signal(barrier, inc=1, device_id=device(peer), device_id_type=MESH)
    pl.semaphore_wait(barrier, len(peers))


HEADS, GROUPS, ROWS, WIDE = 4, 2, 256, 2560
NEAR_UP = 64
NEAR_MID = 160
FAR_DOWN = 80
FAR_MID = 160
CHUNKS = ((1, 0, 0, 1280), (1, 1, 0, 1280), (0, 0, 0, 512), (0, 1, 0, 512), (0, 2, 0, 512), (0, 3, 0, 256), (0, 3, 256, 256))


def dot(a, b, contract=((1,), (0,))):
    return lax.dot_general(a, b, (contract, ((), ())), preferred_element_type=F32)


def add_rows(count, step, body):
    def at(i, carry):
        body(pl.ds(pl.multiple_of(i * step, step), step))
        return carry
    lax.fori_loop(0, count // step, at, 0)


PARTS = (
    ("kv", 0, 64, "xyz"), ("kv", 64, 48, "yzx"), ("kv", 112, 48, "zxy"),
    ("query", 0, 80, "yxz"), ("query", 80, 80, "yzx"),
    ("out", 0, 640, "yxz"), ("out", 640, 640, "yzx"),
)
KV_PARTS, QUERY_PARTS, OUT_PARTS = range(3), range(3, 5), range(5, 7)


def front_kernel(rows_in, rows_out, in_ref, out_ref, tokens_ref, gain_ref, lengths_ref,
                 queries_out, kv_out, turned_out, mask_out, w_out, *scratch):
    (w_kv, w_query, slots_in, slots_out, wide, block_out, x_ref, queries, kv, kv_relay, turned, mask,
     swap_send, swap_recv, pair_sem, local_sem, ring_send, ring_recv, twin_send, twin_recv, kv_send, kv_recv, keep_sem) = scratch
    at = place()
    c = at["c"]
    ctx = at["y"] * 2 + c
    twin = sibling(at)
    up, down = beside(at, "y", 1), beside(at, "y", -1)
    others = [lax.rem(ctx + k, 8) for k in range(1, 8)]
    group = [{**at, "y": lax.div(j, 2), "c": lax.rem(j, 2)} for j in others]
    greet([beside(at, "x", 1), beside(at, "x", -1), beside(at, "z", 1), beside(at, "z", -1)] + group)
    sent = []

    def remote(src, dst, send, recv, to):
        copy = pltpu.make_async_remote_copy(src, dst, send, recv, device_id=device(to), device_id_type=MESH)
        copy.start()
        sent.append(copy)
        return copy

    copies = [remote(in_ref.at[others[k]], slots_in.at[ctx], swap_send.at[k], swap_recv.at[k], group[k]) for k in range(7)]
    pair = remote(out_ref.at[1 - c], slots_out.at[c], pair_sem.at[0], pair_sem.at[1], twin)
    slots_in[ctx] = in_ref[ctx]
    slots_out[c] = out_ref[c]

    def norm(r):
        values = tokens_ref[r, :].astype(F32)
        power = jnp.mean(values * values, axis=1, keepdims=True)
        x_ref[r, :] = (values * lax.rsqrt(power + epsilon) * gain_ref[...]).astype(BF16)

    lane = pl.ds(pl.multiple_of(c * 128, 128), 128)
    for k, copy in enumerate(copies):
        copy.wait_recv()
    for j in range(8):
        wide[rows_in * j:rows_in * (j + 1)] = slots_in[j].astype(F32)[:rows_in]
    w_kv[at["y"], at["z"], at["x"], :, lane] = wide[:, :128].astype(BF16)
    w_query[at["y"], at["z"], at["x"], :, lane] = wide[:, 128:].astype(BF16)

    one = {a: pl.ds(at[a], 1) for a in "xyz"}
    whole = pl.ds(0, SIDE)

    def view(part, where):
        name, start, size, _ = PARTS[part]
        if name == "out":
            cols = pl.ds(pl.multiple_of(c * 1280 + start, 128), size)
            return w_out.at[where["z"], where["x"], where["y"], :, cols]
        ref = w_kv if name == "kv" else w_query
        return ref.at[where["y"], where["z"], where["x"], pl.ds(start, size), lane]

    first, last, twins = {}, {}, {}

    def known(part, phase, shift, half):
        order = PARTS[part][3]
        where = dict(one)
        for a in order[:phase]:
            where[a] = whole
        if phase:
            where[order[0]] = pl.ds(2 * half, 2)
        if half is None and phase:
            where[order[0]] = whole
        axis = order[phase]
        where[axis] = pl.ds(lax.rem(at[axis] + shift + SIDE, SIDE), 1)
        return where

    def ring(part, phase, slot, where, step):
        return remote(view(part, where), view(part, where), ring_send.at[part, phase, slot],
                      ring_recv.at[part, phase, slot], beside(at, PARTS[part][3][phase], step))

    def to_twin(part, where, slot):
        twins.setdefault(part, []).append(
            remote(view(part, where), view(part, where), twin_send.at[part, slot], twin_recv.at[part, slot], twin))

    def begin(part, phase):
        if phase:
            first[part] = (ring(part, phase, 0, known(part, phase, 0, 0), 1), ring(part, phase, 1, known(part, phase, 0, 1), -1))
            last[part] = [ring(part, phase, 2, known(part, phase, 0, 1), 1), ring(part, phase, 3, known(part, phase, 0, 0), -1)]
        else:
            first[part] = (ring(part, 0, 0, known(part, 0, 0, None), 1),)
            last[part] = [ring(part, 0, 1, known(part, 0, 0, None), -1)]

    def share(part):
        where = dict(one)
        for a in PARTS[part][3][:2]:
            where[a] = whole
        to_twin(part, where, 0)

    def relay(part, phase):
        first[part][0].wait_recv()
        if not phase:
            last[part].append(ring(part, 0, 4, known(part, 0, -1, None), 1))
            return
        last[part].append(ring(part, phase, 4, known(part, phase, -1, 0), 1))
        first[part][1].wait_recv()
        last[part].append(ring(part, phase, 5, known(part, phase, 1, 1), -1))
        if phase == 2:
            to_twin(part, known(part, phase, -1, 0), 1)
            to_twin(part, known(part, phase, 1, 1), 2)

    def finish(parts, phase):
        for n in range(4):
            for part in parts:
                if n < len(last[part]):
                    last[part][n].wait_recv()
                    if phase == 2:
                        shift, half = ((-1, 1), (1, 0), (-2, 0), (2, 1))[n]
                        to_twin(part, known(part, phase, shift, half), 3 + n)

    def arrived(parts):
        for part in parts:
            for copy in twins[part]:
                copy.wait_recv()

    later = list(QUERY_PARTS) + list(OUT_PARTS)
    for part in KV_PARTS:
        begin(part, 0)
    for part in QUERY_PARTS:
        begin(part, 0)
    pair.wait_recv()
    block_out[0, 0, 0] = jnp.concatenate(
        [slots_out[0].astype(F32)[:rows_out], slots_out[1].astype(F32)[:rows_out]], axis=0).astype(BF16)
    own_cols = pl.ds(pl.multiple_of(c * 1280, 128), 1280)
    store = pltpu.make_async_copy(block_out, w_out.at[one["z"], one["x"], one["y"], :, own_cols], local_sem)
    store.start()
    for part in KV_PARTS:
        relay(part, 0)
    store.wait()
    for part in OUT_PARTS:
        begin(part, 0)
    finish(KV_PARTS, 0)
    for part in KV_PARTS:
        begin(part, 1)
    add_rows(ROWS // 2, 32, norm)
    for part in later:
        relay(part, 0)
    for part in KV_PARTS:
        relay(part, 1)
    finish(later, 0)
    for part in later:
        begin(part, 1)
    finish(KV_PARTS, 1)
    for part in KV_PARTS:
        begin(part, 2)
        share(part)

    def norm_more(i, carry):
        norm(pl.ds(pl.multiple_of(i * 32, 32), 32))
        return carry
    lax.fori_loop(4, ROWS // 32, norm_more, 0)
    for part in later:
        relay(part, 1)
    finish(later, 1)
    for part in KV_PARTS:
        relay(part, 2)
    for part in QUERY_PARTS:
        begin(part, 2)
    finish(KV_PARTS, 2)
    for part in QUERY_PARTS:
        share(part)
    arrived(KV_PARTS)

    here, before, old = 4 + c, 2 + c, c

    def project_kv(n, carry):
        kv[here, n] = dot(x_ref[...], w_kv[n].reshape(128 * rows_in, 256)).astype(BF16)
        return carry
    lax.fori_loop(0, 4, project_kv, 0)

    def rows_of(slot, low, high):
        return kv.at[slot, :, pl.ds(low, high - low), :]

    def kv_move(src, dst, n, to):
        return remote(src, dst, kv_send.at[n], kv_recv.at[n], to)

    mid = NEAR_MID - NEAR_UP
    a0 = kv_move(rows_of(here, 0, NEAR_UP), rows_of(before, 0, NEAR_UP), 0, up)
    b0 = kv_move(rows_of(here, NEAR_UP, NEAR_MID), kv_relay.at[:, pl.ds(0, mid), :], 1, down)
    a1 = kv_move(rows_of(here, NEAR_UP, ROWS), rows_of(before, NEAR_UP, ROWS), 2, up)
    b1 = kv_move(rows_of(here, NEAR_MID, ROWS), kv_relay.at[:, pl.ds(mid, ROWS - NEAR_MID), :], 3, down)
    t0 = kv_move(kv.at[here], kv.at[here], 4, twin)
    for part in QUERY_PARTS:
        relay(part, 2)
    for part in OUT_PARTS:
        begin(part, 2)

    def turn(i, carry):
        cols = pl.ds(pl.multiple_of(i * 128, 128), 128)
        turned[cols, :] = x_ref[:, cols].astype(F32).T.astype(BF16)
        return carry
    a0.wait_recv()
    a2 = kv_move(rows_of(before, 0, NEAR_UP), rows_of(old, 0, NEAR_UP), 5, up)
    lax.fori_loop(0, 10, turn, 0)
    b0.wait_recv()
    b2 = kv_move(kv_relay.at[:, pl.ds(0, mid), :], rows_of(old, NEAR_UP, NEAR_MID), 6, down)
    finish(QUERY_PARTS, 2)
    for part in OUT_PARTS:
        share(part)
    lax.fori_loop(10, WIDE // 128, turn, 0)
    keep_turned = pltpu.make_async_copy(turned, turned_out, keep_sem.at[0])
    keep_turned.start()
    b1.wait_recv()
    b3 = kv_move(kv_relay.at[:, pl.ds(mid, ROWS - NEAR_MID), :], rows_of(old, NEAR_MID, ROWS), 7, down)
    for part in OUT_PARTS:
        relay(part, 2)

    query_pos = ctx * ROWS + lax.broadcasted_iota(jnp.int32, (ROWS, 1), 0)
    key_pos = (ctx - 4) * ROWS + lax.broadcasted_iota(jnp.int32, (1, 5 * ROWS), 1)
    query_doc, key_doc, ending = 0 * query_pos, 0 * key_pos, 0
    for n in range(lengths_ref.shape[1]):
        ending = ending + lengths_ref[0, n]
        query_doc = query_doc + jnp.where(query_pos >= ending, 1, 0)
        key_doc = key_doc + jnp.where(key_pos >= ending, 1, 0)
    gap = query_pos - key_pos
    seen = (query_doc == key_doc) & (key_pos >= 0) & (gap >= 0) & (gap < WINDOW)
    mask[...] = jnp.where(seen, 1.0, 0.0)
    keep_mask = pltpu.make_async_copy(mask, mask_out, keep_sem.at[1])
    keep_mask.start()

    arrived(QUERY_PARTS)

    def project_query(n, carry):
        queries[n] = dot(x_ref[...], w_query[n].reshape(128 * rows_in, 256)).astype(BF16)
        return carry
    lax.fori_loop(0, 4, project_query, 0)
    keep_queries = pltpu.make_async_copy(queries, queries_out, keep_sem.at[2])
    keep_queries.start()
    a1.wait_recv()
    t1 = kv_move(kv.at[before], kv.at[before], 8, twin)
    a2.wait_recv()
    b2.wait_recv()
    t2 = kv_move(rows_of(old, 0, NEAR_MID), rows_of(old, 0, NEAR_MID), 9, twin)
    finish(OUT_PARTS, 2)
    b3.wait_recv()
    t3 = kv_move(rows_of(old, NEAR_MID, ROWS), rows_of(old, NEAR_MID, ROWS), 10, twin)
    for copy in (t0, t1, t2, t3):
        copy.wait_recv()
    keep_kv = pltpu.make_async_copy(kv, kv_out, keep_sem.at[3])
    keep_kv.start()
    arrived(OUT_PARTS)
    for copy in sent:
        copy.wait_send()
    for copy in (keep_turned, keep_mask, keep_queries, keep_kv):
        copy.wait()


def front(tokens, norm_gain, lengths, w_query, w_key, w_value, w_out):
    rows_in, rows_out = w_query.shape[0], w_out.shape[0]
    cut = [w.reshape(rows_in, 8, 128) for w in (jnp.concatenate([w_key, w_value], axis=1), w_query)]
    pieces_in = jnp.pad(jnp.concatenate(cut, axis=2).transpose(1, 0, 2), ((0, 0), (0, 32 - rows_in), (0, 0)))
    pieces_out = jnp.pad(w_out.reshape(rows_out, 2, 1280).transpose(1, 0, 2), ((0, 0), (0, 16 - rows_out), (0, 0)))
    vmem = pl.BlockSpec(memory_space=pltpu.VMEM)
    hbm = pl.BlockSpec(memory_space=pl.ANY)
    smem = pl.BlockSpec(memory_space=pltpu.SMEM)
    dma = pltpu.SemaphoreType.DMA

    def held(*shape):
        return pltpu.VMEM(shape, BF16)

    *rest, whole_out = pl.pallas_call(
        functools.partial(front_kernel, rows_in, rows_out),
        out_shape=(
            jax.ShapeDtypeStruct((HEADS, ROWS, 256), BF16),
            jax.ShapeDtypeStruct((6, 4, ROWS, 256), BF16),
            jax.ShapeDtypeStruct((WIDE, ROWS), BF16),
            jax.ShapeDtypeStruct((ROWS, 5 * ROWS), F32),
            jax.ShapeDtypeStruct((SIDE, SIDE, SIDE, 2 * rows_out, WIDE), BF16),
        ),
        in_specs=[vmem, vmem, vmem, vmem, smem],
        out_specs=(hbm,) * 5,
        scratch_shapes=[
            held(SIDE, SIDE, SIDE, 8 * rows_in, 256), held(SIDE, SIDE, SIDE, 8 * rows_in, 256),
            held(8, 32, 256), held(2, 16, 1280), pltpu.VMEM((8 * rows_in, 256), F32), held(1, 1, 1, 2 * rows_out, 1280),
            held(ROWS, WIDE), held(HEADS, ROWS, 256), held(6, 4, ROWS, 256), held(4, ROWS - NEAR_UP, 256),
            held(WIDE, ROWS), pltpu.VMEM((ROWS, 5 * ROWS), F32),
            dma((7,)), dma((7,)), dma((2,)), dma,
            dma((7, 3, 6)), dma((7, 3, 6)), dma((7, 7)), dma((7, 7)), dma((11,)), dma((11,)), dma((4,)),
        ],
        compiler_params=pltpu.CompilerParams(
            collective_id=0, has_side_effects=True, vmem_limit_bytes=62 * 2**20),
        name="front",
    )(pieces_in, pieces_out, tokens, norm_gain.reshape(1, -1), lengths)
    return (*rest, whole_out.reshape(128 * rows_out, WIDE))


def layer_kernel(queries, kv, mask_ref, rewards_ref, turned_ref, tokens_ref, target_ref, weight_ref,
                 own_query, own_key, own_value, own_out, mate_query, mate_key, mate_value, mate_out, *scratch):
    (probs, scores, terms, term_mate, term_next, term_far, term_relay, term_end, x_one, x_two,
     weight, turned, mixed, mixed_turned, mixed_grad, joined,
     give_in, give_out, sum_in, sum_out, twin_in, twin_out, far_in, far_out, near_in, near_out, done_in, done_out,
     read_sem, term_send, term_recv, twin_send, twin_recv,
     far_send, far_recv, near_send, near_recv, mate_send, mate_recv, keep_sem) = scratch
    at = place()
    c, y = at["c"], at["y"]
    twin = sibling(at)
    up, down = beside(at, "y", 1), beside(at, "y", -1)
    x_flip = {**at, "x": at["x"] + 1 - 2 * lax.rem(at["x"], 2)}
    x_turn = {**at, "x": SIDE - 1 - at["x"]}
    z_flip = {**at, "z": at["z"] + 1 - 2 * lax.rem(at["z"], 2)}
    z_turn = {**at, "z": SIDE - 1 - at["z"]}
    sent = []

    def remote(src, dst, send, recv, to):
        copy = pltpu.make_async_remote_copy(src, dst, send, recv, device_id=device(to), device_id_type=MESH)
        copy.start()
        sent.append(copy)
        return copy

    def read(src, dst, n):
        copy = pltpu.make_async_copy(src, dst, read_sem.at[n])
        copy.start()
        return copy

    read_weight = read(weight_ref, weight, 1)
    read_tokens = read(tokens_ref, x_two, 2)
    read_target = read(target_ref, x_one, 3)
    read_turned = read(turned_ref, turned, 0)
    greet([twin, up, down, x_flip, x_turn, z_flip, z_turn])

    def tile(n):
        return kv[pl.ds(c, 5), n].reshape(5 * ROWS, 256)

    def attend(h, carry):
        g = h // 2
        seen = mask_ref[...] > 0.5
        score = dot(queries[h], tile(g), ((1,), (1,))) * 256 ** -0.5
        score = jnp.where(seen, score, masked_score)
        raised = jnp.where(seen, jnp.exp(score - jnp.max(score, axis=1, keepdims=True)), 0.0)
        prob = (raised / jnp.sum(raised, axis=1, keepdims=True)).astype(BF16)
        probs[h] = prob
        out = dot(prob, tile(2 + g))
        mixed[h] = out.astype(BF16)
        rounded = out.astype(BF16).astype(F32).T.astype(BF16)
        mixed_turned[2 * h] = rounded[:128]
        mixed_turned[2 * h + 1] = rounded[128:]
        return carry
    lax.fori_loop(0, HEADS, attend, 0)

    for copy in (read_weight, read_tokens, read_target):
        copy.wait()

    def error(i, carry):
        cols = pl.ds(pl.multiple_of(i * 512, 512), 512)
        update = sum(dot(mixed[h], weight[256 * h:256 * h + 256, cols]) for h in range(HEADS))
        result = x_two[:, cols].astype(F32) + update
        x_two[:, cols] = (rewards_ref[...] * (result - x_one[:, cols].astype(F32))).astype(BF16)
        return carry
    lax.fori_loop(0, WIDE // 512, error, 0)
    delta = x_two

    y_far, y_up, y_down = lax.rem(y + 2, SIDE), up["y"], down["y"]
    height = {0: WIDE // 8, 1: HEADS * 256 // 8}
    swaps, far, near_own, near_sum, flips, turns, keeps = {}, {}, {}, {}, {}, {}, {}

    def pick(k, inside, outside):
        kind, n, start, width = CHUNKS[k]
        if kind:
            return outside.at[n]
        if start == 0 and width == 512:
            return inside.at[n]
        return inside.at[n, :, pl.ds(start, width)] if len(inside.shape) == 3 else inside.at[n, :, :, pl.ds(start, width)]

    def term(k, dst, core):
        kind, n, start, width = CHUNKS[k]

        def body(i, carry):
            j = 2 * i + core
            if kind:
                dst[i] = dot(mixed_turned[j], delta[:, 1280 * n:1280 * n + 1280]).astype(BF16)
            else:
                rows = pl.ds(pl.multiple_of(j * 320, 64), 320)
                dst[i] = dot(turned[rows, :], joined[n, :, start:start + width]).astype(BF16)
            return carry
        lax.fori_loop(0, 4, body, 0)

    def stage_1(k):
        kind, n, start, width = CHUNKS[k]
        give = give_out.at[n] if kind else give_in.at[n % 2, :, :, pl.ds(start, width)]
        if k in (4, 5):
            swaps[k - 2].wait_send()
        term(k, give, 1 - c)
        swaps[k] = pltpu.make_async_remote_copy(
            give, pick(k, twin_in, twin_out), twin_send.at[k], twin_recv.at[k], device_id=device(twin), device_id_type=MESH)
        swaps[k].start()
        term(k, pick(k, sum_in, sum_out), c)

    def stage_2(k):
        rows = height[CHUNKS[k][0]]
        sums, extra = pick(k, sum_in, sum_out), pick(k, twin_in, twin_out)
        fars, nears = pick(k, far_in, far_out), pick(k, near_in, near_out)
        h0, h1 = pl.ds(0, rows // 2), pl.ds(rows // 2, rows // 2)
        swaps[k].wait_recv()

        def add(block):
            def body(r):
                sums[block, r, :] = (sums[block, r, :].astype(F32) + extra[block, r, :].astype(F32)).astype(BF16)
            add_rows(rows, 32, body)
        add(y_far)
        far[k] = (remote(sums.at[y_far, h0], fars.at[0], far_send.at[k, 0], far_recv.at[k, 0], up),
                  remote(sums.at[y_far, h1], fars.at[1], far_send.at[k, 1], far_recv.at[k, 1], down))
        add(y_up)
        add(y_down)
        near_own[k] = (remote(sums.at[y_up, h1], nears.at[0, h1], near_send.at[k, 0], near_recv.at[k, 0], up),
                       remote(sums.at[y_down, h0], nears.at[1, h0], near_send.at[k, 1], near_recv.at[k, 1], down))
        add(y)

    def stage_3(k):
        rows = height[CHUNKS[k][0]]
        half = rows // 2
        sums = pick(k, sum_in, sum_out)
        fars, nears = pick(k, far_in, far_out), pick(k, near_in, near_out)
        h0, h1 = pl.ds(0, half), pl.ds(half, half)
        far[k][0].wait_recv()

        def low(r):
            sums[y_up, r, :] = (sums[y_up, r, :].astype(F32) + fars[0, r, :].astype(F32)).astype(BF16)
        add_rows(half, 32, low)
        one = remote(sums.at[y_up, h0], nears.at[0, h0], near_send.at[k, 2], near_recv.at[k, 2], up)
        far[k][1].wait_recv()

        def high(i, carry):
            r = pl.ds(pl.multiple_of(i * 32, 32), 32)
            s = pl.ds(pl.multiple_of(i * 32 + half, 32), 32)
            sums[y_down, s, :] = (sums[y_down, s, :].astype(F32) + fars[1, r, :].astype(F32)).astype(BF16)
            return carry
        lax.fori_loop(0, half // 32, high, 0)
        near_sum[k] = (one, remote(sums.at[y_down, h1], nears.at[1, h1], near_send.at[k, 3], near_recv.at[k, 3], down))

    def result(k, query, key, value, out):
        kind, n, start, width = CHUNKS[k]
        ref = out if kind else (query, query, key, value)[n]
        begin = 1280 * n if kind else start if n > 1 else 512 * n
        return ref, pl.ds(begin, width)

    def mates(k, level):
        ref, cols = result(k, mate_query, mate_key, mate_value, mate_out)
        return ref.at[level, :, cols]

    def stage_4(k):
        kind = CHUNKS[k][0]
        sums, nears, done = pick(k, sum_in, sum_out), pick(k, near_in, near_out), pick(k, done_in, done_out)
        for copy in near_own[k] + near_sum[k]:
            copy.wait_recv()

        def body(r):
            done[r, :] = (sums[y, r, :].astype(F32) + nears[0, r, :].astype(F32) + nears[1, r, :].astype(F32)).astype(BF16)
        add_rows(height[kind], 32, body)
        flips[k] = (remote(done, mates(k, 0), mate_send.at[k, 0], mate_recv.at[k, 0], x_flip),
                    remote(done, mates(k, 2), mate_send.at[k, 2], mate_recv.at[k, 2], z_flip))
        own, cols = result(k, own_query, own_key, own_value, own_out)
        keeps[k] = pltpu.make_async_copy(done, own.at[:, cols], keep_sem.at[k])
        keeps[k].start()

    def stage_5(k):
        flips[k][0].wait_recv()
        one = remote(mates(k, 0), mates(k, 1), mate_send.at[k, 1], mate_recv.at[k, 1], x_turn)
        flips[k][1].wait_recv()
        turns[k] = (one, remote(mates(k, 2), mates(k, 3), mate_send.at[k, 3], mate_recv.at[k, 3], z_turn))

    stage_1(0)
    stage_1(1)
    stage_2(0)

    def spread(h, carry):
        rows = pl.ds(pl.multiple_of(h * 256, 256), 256)
        mixed_grad[h] = dot(delta[...], weight[rows, :], ((1,), (1,))).astype(BF16)
        return carry
    lax.fori_loop(0, HEADS, spread, 0)
    stage_2(1)

    terms[5 * (1 - c)] = jnp.zeros((4, ROWS, 256), BF16)

    def back(g):
        for r in range(2):
            h = 2 * g + r
            grad = mixed_grad[h]
            row_dots = jnp.sum(grad.astype(F32) * mixed[h].astype(F32), axis=1, keepdims=True)
            prob_grads = dot(grad, tile(2 + g), ((1,), (1,)))
            score = (probs[h].astype(F32) * (prob_grads - row_dots) * 256 ** -0.5).astype(BF16)
            scores[r] = score
            joined[g, :, 256 * r:256 * r + 256] = dot(score, tile(g)).astype(BF16)
        key_terms = dot(scores[0], queries[2 * g], ((0,), (0,))) + dot(scores[1], queries[2 * g + 1], ((0,), (0,)))
        terms[pl.ds(c, 5), g] = key_terms.astype(BF16).reshape(5, ROWS, 256)
        value_terms = (dot(probs[2 * g], mixed_grad[2 * g], ((0,), (0,)))
                       + dot(probs[2 * g + 1], mixed_grad[2 * g + 1], ((0,), (0,))))
        terms[pl.ds(c, 5), 2 + g] = value_terms.astype(BF16).reshape(5, ROWS, 256)

    back(0)
    stage_3(0)
    back(1)
    stage_3(1)

    def move(src, dst, n, to):
        return remote(src, dst, term_send.at[n], term_recv.at[n], to)

    to_mate = [move(terms.at[2 * n + 1 - c], term_mate.at[n], n, twin) for n in range(3)]
    stage_4(0)
    read_turned.wait()
    stage_1(2)

    def fold(n):
        to_mate[n].wait_recv()
        for q in range(4):
            def body(r):
                terms[2 * n + c, q, r, :] = (
                    terms[2 * n + c, q, r, :].astype(F32) + term_mate[n, q, r, :].astype(F32)).astype(BF16)
            add_rows(ROWS, 64, body)

    def part(ref, low, high, start=0):
        return ref.at[:, pl.ds(low - start, high - low), :]

    fold(0)
    s2 = terms.at[c]
    e0 = move(part(s2, 0, FAR_DOWN), term_far, 3, down)
    f0 = move(part(s2, FAR_DOWN, FAR_MID), part(term_relay, FAR_DOWN, FAR_MID, FAR_DOWN), 4, up)
    f1 = move(part(s2, FAR_MID, ROWS), part(term_relay, FAR_MID, ROWS, FAR_DOWN), 5, up)
    fold(1)
    s1 = terms.at[2 + c]
    e1 = move(part(s1, FAR_DOWN, ROWS), part(term_next, FAR_DOWN, ROWS), 6, down)
    fold(2)
    stage_1(3)
    stage_2(2)
    e0.wait_recv()
    for q in range(4):
        def join(r):
            terms[2 + c, q, r, :] = (terms[2 + c, q, r, :].astype(F32) + term_far[q, r, :].astype(F32)).astype(BF16)
        add_rows(FAR_DOWN, 16, join)
    e2 = move(part(s1, 0, FAR_DOWN), part(term_next, 0, FAR_DOWN), 7, down)
    f0.wait_recv()
    f2 = move(part(term_relay, FAR_DOWN, FAR_MID, FAR_DOWN), part(term_end, FAR_DOWN, FAR_MID, FAR_DOWN), 8, up)
    f1.wait_recv()
    f3 = move(part(term_relay, FAR_MID, ROWS, FAR_DOWN), part(term_end, FAR_MID, ROWS, FAR_DOWN), 9, up)
    stage_4(1)
    stage_2(3)
    stage_5(0)
    stage_3(2)
    for copy in (e1, e2, f2, f3):
        copy.wait_recv()
    for q in range(4):
        n, g = 2 + q // 2, q % 2
        joined[n, 0:FAR_DOWN, 256 * g:256 * g + 256] = (
            terms[4 + c, q, 0:FAR_DOWN, :].astype(F32) + term_next[q, 0:FAR_DOWN, :].astype(F32)).astype(BF16)
        joined[n, FAR_DOWN:ROWS, 256 * g:256 * g + 256] = (
            terms[4 + c, q, FAR_DOWN:ROWS, :].astype(F32) + term_next[q, FAR_DOWN:ROWS, :].astype(F32)
            + term_end[q].astype(F32)).astype(BF16)
    order = ((1, 4), (1, 5), (2, 4), (1, 6), (3, 3), (2, 5), (4, 2), (5, 1), (2, 6), (3, 4), (4, 3), (5, 2), (3, 5),
             (3, 6), (4, 4), (5, 3), (4, 5), (5, 4), (4, 6), (5, 5), (5, 6))
    for stage, k in order:
        (stage_1, stage_2, stage_3, stage_4, stage_5)[stage - 1](k)
    for k in range(len(CHUNKS)):
        turns[k][0].wait_recv()
        turns[k][1].wait_recv()
        keeps[k].wait()
    for k in (0, 1, 4, 5, 6):
        swaps[k].wait_send()
    for copy in sent:
        copy.wait_send()


def layer_grads(queries, kv, mask, rewards, turned, tokens, target, weight):
    vmem = pl.BlockSpec(memory_space=pltpu.VMEM)
    hbm = pl.BlockSpec(memory_space=pl.ANY)
    dma = pltpu.SemaphoreType.DMA
    ri, ro, n = WIDE // 8, HEADS * 256 // 8, len(CHUNKS)
    results = ((ri, 1024), (ri, 512), (ri, 512), (ro, WIDE))

    def held(*shape):
        return pltpu.VMEM(shape, BF16)

    return pl.pallas_call(
        layer_kernel,
        out_shape=tuple(jax.ShapeDtypeStruct(shape, BF16) for shape in results)
        + tuple(jax.ShapeDtypeStruct((4, *shape), BF16) for shape in results),
        in_specs=[vmem, vmem, vmem, vmem, hbm, hbm, hbm, hbm],
        out_specs=(hbm,) * 8,
        scratch_shapes=[
            held(HEADS, ROWS, 5 * ROWS), held(2, ROWS, 5 * ROWS),
            held(6, 4, ROWS, 256), held(3, 4, ROWS, 256), held(4, ROWS, 256), held(4, FAR_DOWN, 256),
            held(4, ROWS - FAR_DOWN, 256), held(4, ROWS - FAR_DOWN, 256),
            held(ROWS, WIDE), held(ROWS, WIDE), held(HEADS * 256, WIDE), held(WIDE, ROWS),
            held(HEADS, ROWS, 256), held(8, 128, ROWS), held(HEADS, ROWS, 256), held(4, ROWS, 512),
            held(2, 4, ri, 512), held(2, 4, ro, 1280),
            held(4, 4, ri, 512), held(2, 4, ro, 1280), held(4, 4, ri, 512), held(2, 4, ro, 1280),
            held(4, 2, ri // 2, 512), held(2, 2, ro // 2, 1280), held(4, 2, ri, 512), held(2, 2, ro, 1280),
            held(4, ri, 512), held(2, ro, 1280),
            dma((4,)), dma((10,)), dma((10,)), dma((n,)), dma((n,)),
            dma((n, 2)), dma((n, 2)), dma((n, 4)), dma((n, 4)), dma((n, 4)), dma((n, 4)), dma((n,)),
        ],
        compiler_params=pltpu.CompilerParams(
            collective_id=1, has_side_effects=True, vmem_limit_bytes=62 * 2**20),
        name="layer_grads",
    )(queries, kv, mask, rewards, turned, tokens, target, weight)


def per_device(
    tokens, target, rewards, doc_lengths, norm_gain, w_query, w_key, w_value, w_out, gossip_bit
):
    token_rows, target_rows = tokens[0, 0], target[0, 0]
    queries, kv, turned, mask, out_whole = front(
        token_rows, norm_gain, doc_lengths[0], w_query, w_key, w_value, w_out
    )
    results = layer_grads(
        queries, kv, mask, rewards.reshape(ROWS, 1), turned, token_rows, target_rows, out_whole
    )
    own_bit = gossip_bit[0]

    def mean(own, mates):
        partner = mates[0]
        for level in range(1, 4):
            partner = jnp.where(own_bit == level, mates[level], partner)
        return ((own.astype(F32) + partner.astype(F32)) * 0.5)[None]

    return tuple(mean(own, mates) for own, mates in zip(results[:4], results[4:]))


def solution(mesh):
    placed = (
        P("dp", None, "ctx", None),
        P("dp", None, "ctx", None),
        P("dp", None, "ctx"),
        P("dp", None, None),
        P(),
        P(("dp", "ctx"), None),
        P(("dp", "ctx"), None),
        P(("dp", "ctx"), None),
        P(("dp", "ctx"), None),
        P("dp"),
    )
    return jax.shard_map(
        per_device,
        mesh=mesh,
        in_specs=placed,
        out_specs=(
            P("dp", "ctx", None),
            P("dp", "ctx", None),
            P("dp", "ctx", None),
            P("dp", "ctx", None),
        ),
        check_vma=False,
    )
```

```python
import functools
import jax
import jax.numpy as jnp
from jax import lax
from jax.experimental import pallas as pl
from jax.experimental.pallas import tpu as pltpu
from jax.sharding import PartitionSpec as P

MESH = pl.DeviceIdType.MESH
BF16 = jnp.bfloat16
F32 = jnp.float32
WINDOW = 1024

epsilon = 1e-06
masked_score = -1e30

SIDE = 4


def place():
    dp, ctx = lax.axis_index("dp"), lax.axis_index("ctx")
    return {"x": lax.rem(dp, SIDE), "z": lax.div(dp, SIDE), "y": lax.div(ctx, 2), "c": lax.rem(ctx, 2)}


def device(at):
    return (at["z"] * SIDE + at["x"], at["y"] * 2 + at["c"])


def beside(at, axis, step):
    return {**at, axis: lax.rem(at[axis] + step + SIDE, SIDE)}


def sibling(at):
    return {**at, "c": 1 - at["c"]}


def greet(peers):
    barrier = pltpu.get_barrier_semaphore()
    for peer in peers:
        pl.semaphore_signal(barrier, inc=1, device_id=device(peer), device_id_type=MESH)
    pl.semaphore_wait(barrier, len(peers))


HEADS, GROUPS, ROWS, WIDE = 4, 2, 256, 2560
NEAR_UP = 64
NEAR_MID = 160
FAR_DOWN = 80
FAR_MID = 160
CHUNKS = ((1, 0, 0, 1280), (1, 1, 0, 1280), (0, 0, 0, 512), (0, 1, 0, 512), (0, 2, 0, 512), (0, 3, 0, 256), (0, 3, 256, 128),
          (0, 3, 384, 128))


def dot(a, b, contract=((1,), (0,))):
    return lax.dot_general(a, b, (contract, ((), ())), preferred_element_type=F32)


def add_rows(count, step, body):
    def at(i, carry):
        body(pl.ds(pl.multiple_of(i * step, step), step))
        return carry
    lax.fori_loop(0, count // step, at, 0)


PARTS = (
    ("kv", 0, 80, "xz"), ("kv", 80, 80, "zx"),
    ("query", 0, 80, "xz"), ("query", 80, 80, "zx"),
    ("out", 0, 32, "xz"), ("out", 32, 32, "zx"),
)
KV_PARTS, QUERY_PARTS, OUT_PARTS = (0, 1), (2, 3), (4, 5)


def front_kernel(rows_in, rows_out, kv_ref, query_ref, out_ref, tokens_ref, gain_ref, lengths_ref,
                 queries_out, kv_out, turned_out, mask_out, w_out, *scratch):
    (w_kv, w_query, slots_kv, slots_query, slots_out, wide, block_out, x_ref, queries, kv, kv_relay, turned, mask,
     swap_send, swap_recv, local_sem, line_send, line_recv, ring_send, ring_recv, twin_send, twin_recv,
     kv_send, kv_recv, keep_sem) = scratch
    at = place()
    c = at["c"]
    ctx = at["y"] * 2 + c
    twin = sibling(at)
    up, down = beside(at, "y", 1), beside(at, "y", -1)
    others = [lax.rem(ctx + k, 8) for k in range(1, 8)]
    group = [{**at, "y": lax.div(j, 2), "c": lax.rem(j, 2)} for j in others]
    greet([beside(at, a, step) for a in "xz" for step in (1, -1)] + group)
    sent = []

    def remote(src, dst, send, recv, to):
        copy = pltpu.make_async_remote_copy(src, dst, send, recv, device_id=device(to), device_id_type=MESH)
        copy.start()
        sent.append(copy)
        return copy

    def spread(n, ref, slots):
        return [remote(ref.at[group[k]["c"]], slots.at[ctx], swap_send.at[n, k], swap_recv.at[n, k], group[k]) for k in range(7)]

    def norm(i, carry):
        r = pl.ds(pl.multiple_of(i * 32, 32), 32)
        values = tokens_ref[r, :].astype(F32)
        power = jnp.mean(values * values, axis=1, keepdims=True)
        x_ref[r, :] = (values * lax.rsqrt(power + epsilon) * gain_ref[...]).astype(BF16)
        return carry

    def merged(slots, rows, copies):
        for copy in copies:
            copy.wait_recv()
        width = slots.shape[2]
        for j in range(8):
            wide[rows * j:rows * (j + 1), :width] = slots[j].astype(F32)[:rows]
        return wide[:8 * rows, :width].astype(BF16)

    half = pl.ds(pl.multiple_of(c * 512, 128), 512)
    spread_kv = spread(0, kv_ref, slots_kv)
    slots_kv[ctx] = kv_ref[c]
    slots_query[ctx] = query_ref[c]
    slots_out[ctx] = out_ref[c]
    w_kv[at["z"], at["x"], :, half] = merged(slots_kv, rows_in, spread_kv)

    one = {a: pl.ds(at[a], 1) for a in "xz"}
    whole = pl.ds(0, SIDE)

    def view(part, where, piece=None):
        name, start, size, _ = PARTS[part]
        cut = size // 32 * 16 if size % 32 == 0 else 48
        rows = pl.ds(*((start, size) if piece is None else ((start, cut), (start + cut, size - cut))[piece]))
        if name == "out":
            return w_out.at[where["z"], where["x"], rows, pl.ds(pl.multiple_of(c * 1280, 128), 1280)]
        return (w_kv if name == "kv" else w_query).at[where["z"], where["x"], rows, half]

    lines, first, last, twins = {}, {}, {}, {}

    def beside_line(part, step):
        axis = PARTS[part][3][0]
        return {**one, axis: pl.ds(beside(at, axis, step)[axis], 1)}

    def hop(part, n, where, step, piece=None):
        lines.setdefault(part, []).append(
            remote(view(part, where, piece), view(part, where, piece), line_send.at[part, n], line_recv.at[part, n],
                   beside(at, PARTS[part][3][0], step)))

    def line(part):
        hop(part, 0, one, 1)
        hop(part, 1, one, -1)

    def pass_on(parts):
        for part in parts:
            lines[part][0].wait_recv()
            hop(part, 2, beside_line(part, -1), 1, 0)
            lines[part][1].wait_recv()
            hop(part, 3, beside_line(part, 1), -1, 1)

    def lined(parts):
        for part in parts:
            for copy in lines[part][2:]:
                copy.wait_recv()

    def known(part, shift, which):
        order = PARTS[part][3]
        axis = order[1]
        return {order[0]: pl.ds(2 * which, 2), axis: pl.ds(lax.rem(at[axis] + shift + SIDE, SIDE), 1)}

    def ring(part, slot, where, step):
        return remote(view(part, where), view(part, where), ring_send.at[part, slot], ring_recv.at[part, slot],
                      beside(at, PARTS[part][3][1], step))

    def to_twin(part, where, slot):
        twins.setdefault(part, []).append(
            remote(view(part, where), view(part, where), twin_send.at[part, slot], twin_recv.at[part, slot], twin))

    def begin(parts):
        for part in parts:
            first[part] = (ring(part, 0, known(part, 0, 0), 1), ring(part, 1, known(part, 0, 1), -1))
        for part in parts:
            last[part] = [ring(part, 2, known(part, 0, 1), 1), ring(part, 3, known(part, 0, 0), -1)]
        for part in parts:
            to_twin(part, {**one, PARTS[part][3][0]: whole}, 0)

    def relay(parts):
        for part in parts:
            first[part][0].wait_recv()
            last[part].append(ring(part, 4, known(part, -1, 0), 1))
        for part in parts:
            first[part][1].wait_recv()
            last[part].append(ring(part, 5, known(part, 1, 1), -1))
        for part in parts:
            to_twin(part, known(part, -1, 0), 1)
            to_twin(part, known(part, 1, 1), 2)

    def finish(parts):
        for n in range(4):
            for part in parts:
                last[part][n].wait_recv()
                shift, which = ((-1, 1), (1, 0), (-2, 0), (2, 1))[n]
                to_twin(part, known(part, shift, which), 3 + n)

    def arrived(parts):
        for part in parts:
            for copy in twins[part]:
                copy.wait_recv()

    for part in KV_PARTS:
        line(part)
    spread_query = spread(1, query_ref, slots_query)
    spread_out = spread(2, out_ref, slots_out)
    lax.fori_loop(0, 2, norm, 0)
    pass_on(KV_PARTS)
    lax.fori_loop(2, 4, norm, 0)
    lined(KV_PARTS)
    begin(KV_PARTS)
    w_query[at["z"], at["x"], :, half] = merged(slots_query, rows_in, spread_query)
    for part in QUERY_PARTS:
        line(part)
    block_out[0, 0] = merged(slots_out, rows_out, spread_out)
    store = pltpu.make_async_copy(
        block_out, w_out.at[one["z"], one["x"], :, pl.ds(pl.multiple_of(c * 1280, 128), 1280)], local_sem)
    store.start()
    relay(KV_PARTS)
    store.wait()
    for part in OUT_PARTS:
        line(part)
    pass_on(QUERY_PARTS)
    lax.fori_loop(4, ROWS // 32, norm, 0)
    finish(KV_PARTS)
    lined(QUERY_PARTS)
    begin(QUERY_PARTS)
    arrived(KV_PARTS)

    here, before, old = 4 + c, 2 + c, c
    for n in range(4):
        kv[here, n] = dot(x_ref[...], w_kv[:, :, :, 256 * n:256 * n + 256].reshape(128 * rows_in, 256)).astype(BF16)

    def rows_of(slot, low, high):
        return kv.at[slot, :, pl.ds(low, high - low), :]

    def kv_move(src, dst, n, to):
        return remote(src, dst, kv_send.at[n], kv_recv.at[n], to)

    mid = NEAR_MID - NEAR_UP
    a0 = kv_move(rows_of(here, 0, NEAR_UP), rows_of(before, 0, NEAR_UP), 0, up)
    b0 = kv_move(rows_of(here, NEAR_UP, NEAR_MID), kv_relay.at[:, pl.ds(0, mid), :], 1, down)
    a1 = kv_move(rows_of(here, NEAR_UP, ROWS), rows_of(before, NEAR_UP, ROWS), 2, up)
    b1 = kv_move(rows_of(here, NEAR_MID, ROWS), kv_relay.at[:, pl.ds(mid, ROWS - NEAR_MID), :], 3, down)
    t0 = kv_move(kv.at[here], kv.at[here], 4, twin)
    pass_on(OUT_PARTS)
    relay(QUERY_PARTS)
    lined(OUT_PARTS)
    begin(OUT_PARTS)

    def turn(i, carry):
        cols = pl.ds(pl.multiple_of(i * 128, 128), 128)
        turned[cols, :] = x_ref[:, cols].astype(F32).T.astype(BF16)
        return carry
    a0.wait_recv()
    a2 = kv_move(rows_of(before, 0, NEAR_UP), rows_of(old, 0, NEAR_UP), 5, up)
    lax.fori_loop(0, 10, turn, 0)
    b0.wait_recv()
    b2 = kv_move(kv_relay.at[:, pl.ds(0, mid), :], rows_of(old, NEAR_UP, NEAR_MID), 6, down)
    finish(QUERY_PARTS)
    b1.wait_recv()
    b3 = kv_move(kv_relay.at[:, pl.ds(mid, ROWS - NEAR_MID), :], rows_of(old, NEAR_MID, ROWS), 7, down)
    relay(OUT_PARTS)
    lax.fori_loop(10, WIDE // 128, turn, 0)
    keep_turned = pltpu.make_async_copy(turned, turned_out, keep_sem.at[0])
    keep_turned.start()

    query_pos = ctx * ROWS + lax.broadcasted_iota(jnp.int32, (ROWS, 1), 0)
    key_pos = (ctx - 4) * ROWS + lax.broadcasted_iota(jnp.int32, (1, 5 * ROWS), 1)
    query_doc, key_doc, ending = 0 * query_pos, 0 * key_pos, 0
    for n in range(lengths_ref.shape[1]):
        ending = ending + lengths_ref[0, n]
        query_doc = query_doc + jnp.where(query_pos >= ending, 1, 0)
        key_doc = key_doc + jnp.where(key_pos >= ending, 1, 0)
    gap = query_pos - key_pos
    seen = (query_doc == key_doc) & (key_pos >= 0) & (gap >= 0) & (gap < WINDOW)
    mask[...] = jnp.where(seen, 1.0, 0.0)
    keep_mask = pltpu.make_async_copy(mask, mask_out, keep_sem.at[1])
    keep_mask.start()

    a1.wait_recv()
    t1 = kv_move(kv.at[before], kv.at[before], 8, twin)
    arrived(QUERY_PARTS)
    for n in range(4):
        queries[n] = dot(x_ref[...], w_query[:, :, :, 256 * n:256 * n + 256].reshape(128 * rows_in, 256)).astype(BF16)
    keep_queries = pltpu.make_async_copy(queries, queries_out, keep_sem.at[2])
    keep_queries.start()
    a2.wait_recv()
    b2.wait_recv()
    t2 = kv_move(rows_of(old, 0, NEAR_MID), rows_of(old, 0, NEAR_MID), 9, twin)
    b3.wait_recv()
    t3 = kv_move(rows_of(old, NEAR_MID, ROWS), rows_of(old, NEAR_MID, ROWS), 10, twin)
    finish(OUT_PARTS)
    for copy in (t0, t1, t2, t3):
        copy.wait_recv()
    keep_kv = pltpu.make_async_copy(kv, kv_out, keep_sem.at[3])
    keep_kv.start()
    arrived(OUT_PARTS)
    for copy in sent:
        copy.wait_send()
    for copy in (keep_turned, keep_mask, keep_queries, keep_kv):
        copy.wait()


def front(tokens, norm_gain, lengths, w_query, w_key, w_value, w_out):
    rows_in, rows_out = w_query.shape[0], w_out.shape[0]
    pad_in, pad_out = (0, 32 - rows_in), (0, 16 - rows_out)
    kv_pieces = jnp.pad(jnp.stack([w_key, w_value]), ((0, 0), pad_in, (0, 0)))
    query_pieces = jnp.pad(jnp.stack([w_query[:, :512], w_query[:, 512:]]), ((0, 0), pad_in, (0, 0)))
    out_pieces = jnp.pad(jnp.stack([w_out[:, :1280], w_out[:, 1280:]]), ((0, 0), pad_out, (0, 0)))
    vmem = pl.BlockSpec(memory_space=pltpu.VMEM)
    hbm = pl.BlockSpec(memory_space=pl.ANY)
    smem = pl.BlockSpec(memory_space=pltpu.SMEM)
    dma = pltpu.SemaphoreType.DMA

    def held(*shape):
        return pltpu.VMEM(shape, BF16)

    *rest, whole_out = pl.pallas_call(
        functools.partial(front_kernel, rows_in, rows_out),
        out_shape=(
            jax.ShapeDtypeStruct((HEADS, ROWS, 256), BF16),
            jax.ShapeDtypeStruct((6, 4, ROWS, 256), BF16),
            jax.ShapeDtypeStruct((WIDE, ROWS), BF16),
            jax.ShapeDtypeStruct((ROWS, 5 * ROWS), F32),
            jax.ShapeDtypeStruct((SIDE, SIDE, 8 * rows_out, WIDE), BF16),
        ),
        in_specs=[vmem, vmem, vmem, vmem, vmem, smem],
        out_specs=(hbm,) * 5,
        scratch_shapes=[
            held(SIDE, SIDE, 8 * rows_in, 1024), held(SIDE, SIDE, 8 * rows_in, 1024),
            held(8, 32, 512), held(8, 32, 512), held(8, 16, 1280), pltpu.VMEM((8 * rows_in, 1280), F32),
            held(1, 1, 8 * rows_out, 1280),
            held(ROWS, WIDE), held(HEADS, ROWS, 256), held(6, 4, ROWS, 256), held(4, ROWS - NEAR_UP, 256),
            held(WIDE, ROWS), pltpu.VMEM((ROWS, 5 * ROWS), F32),
            dma((3, 7)), dma((3, 7)), dma, dma((6, 4)), dma((6, 4)),
            dma((6, 6)), dma((6, 6)), dma((6, 7)), dma((6, 7)), dma((11,)), dma((11,)), dma((4,)),
        ],
        compiler_params=pltpu.CompilerParams(
            collective_id=0, has_side_effects=True, vmem_limit_bytes=62 * 2**20),
        name="front",
    )(kv_pieces, query_pieces, out_pieces, tokens, norm_gain.reshape(1, -1), lengths)
    return (*rest, whole_out.reshape(128 * rows_out, WIDE))


def layer_kernel(queries, kv, mask_ref, rewards_ref, turned_ref, tokens_ref, target_ref, weight_ref,
                 own_query, own_key, own_value, own_out, mate_query, mate_key, mate_value, mate_out, *scratch):
    (probs, scores, terms, term_mate, term_next, term_far, term_relay, term_end, x_one, x_two,
     weight, turned, mixed, mixed_turned, mixed_grad, joined,
     give_in, give_out, sum_in, sum_out, twin_in, twin_out, far_in, far_out, near_in, near_out, done_in, done_out,
     read_sem, term_send, term_recv, twin_send, twin_recv,
     far_send, far_recv, near_send, near_recv, mate_send, mate_recv, keep_sem) = scratch
    at = place()
    c, y = at["c"], at["y"]
    twin = sibling(at)
    up, down = beside(at, "y", 1), beside(at, "y", -1)
    x_flip = {**at, "x": at["x"] + 1 - 2 * lax.rem(at["x"], 2)}
    x_turn = {**at, "x": SIDE - 1 - at["x"]}
    z_flip = {**at, "z": at["z"] + 1 - 2 * lax.rem(at["z"], 2)}
    z_turn = {**at, "z": SIDE - 1 - at["z"]}
    sent = []

    def remote(src, dst, send, recv, to):
        copy = pltpu.make_async_remote_copy(src, dst, send, recv, device_id=device(to), device_id_type=MESH)
        copy.start()
        sent.append(copy)
        return copy

    def read(src, dst, n):
        copy = pltpu.make_async_copy(src, dst, read_sem.at[n])
        copy.start()
        return copy

    read_weight = read(weight_ref, weight, 1)
    read_tokens = read(tokens_ref, x_two, 2)
    read_target = read(target_ref, x_one, 3)
    read_turned = [read(turned_ref.at[:, core], turned.at[core], (0, 4)[core]) for core in range(2)]
    greet([twin, up, down, x_flip, x_turn, z_flip, z_turn])

    def tile(n):
        return kv[pl.ds(c, 5), n].reshape(5 * ROWS, 256)

    def attend(h, carry):
        g = h // 2
        seen = mask_ref[...] > 0.5
        score = dot(queries[h], tile(g), ((1,), (1,))) * 256 ** -0.5
        score = jnp.where(seen, score, masked_score)
        raised = jnp.where(seen, jnp.exp(score - jnp.max(score, axis=1, keepdims=True)), 0.0)
        prob = (raised / jnp.sum(raised, axis=1, keepdims=True)).astype(BF16)
        probs[h] = prob
        out = dot(prob, tile(2 + g))
        mixed[h] = out.astype(BF16)
        rounded = out.astype(BF16).astype(F32).T.astype(BF16)
        mixed_turned[0, h] = rounded[:128]
        mixed_turned[1, h] = rounded[128:]
        return carry
    lax.fori_loop(0, HEADS, attend, 0)

    for copy in (read_weight, read_tokens, read_target):
        copy.wait()

    def error(i, carry):
        cols = pl.ds(pl.multiple_of(i * 512, 512), 512)
        update = sum(dot(mixed[h], weight[256 * h:256 * h + 256, cols]) for h in range(HEADS))
        result = x_two[:, cols].astype(F32) + update
        x_two[:, cols] = (rewards_ref[...] * (result - x_one[:, cols].astype(F32))).astype(BF16)
        return carry
    lax.fori_loop(0, WIDE // 512, error, 0)
    delta = x_two

    y_far, y_up, y_down = lax.rem(y + 2, SIDE), up["y"], down["y"]
    height = {0: WIDE // 8, 1: HEADS * 256 // 8}
    swaps, far, near_own, near_sum, flips, turns, keeps = {}, {}, {}, {}, {}, {}, {}

    def pick(k, inside, outside):
        kind, n, start, width = CHUNKS[k]
        if kind:
            return outside.at[n]
        if start == 0 and width == 512:
            return inside.at[n]
        return inside.at[n, :, pl.ds(start, width)] if len(inside.shape) == 3 else inside.at[n, :, :, pl.ds(start, width)]

    def term(k, dst, core):
        kind, n, start, width = CHUNKS[k]

        for m in range(2):
            if kind:
                cols = slice(1280 * n + 640 * m, 1280 * n + 640 * m + 640)
                part = dot(mixed_turned[core].reshape(512, ROWS), delta[:, cols])
                dst[:, :, 640 * m:640 * m + 640] = part.astype(BF16).reshape(4, 128, 640)
            else:
                part = dot(turned[core, 2 * m:2 * m + 2].reshape(640, ROWS), joined[n, :, start:start + width])
                dst[2 * m:2 * m + 2] = part.astype(BF16).reshape(2, 320, width)

    def stage_1(k):
        kind, n, start, width = CHUNKS[k]
        give = give_out.at[n] if kind else give_in.at[n % 2, :, :, pl.ds(start, width)]
        if k in (4, 5):
            swaps[k - 2].wait_send()
        term(k, give, 1 - c)
        swaps[k] = pltpu.make_async_remote_copy(
            give, pick(k, twin_in, twin_out), twin_send.at[k], twin_recv.at[k], device_id=device(twin), device_id_type=MESH)
        swaps[k].start()
        term(k, pick(k, sum_in, sum_out), c)

    def stage_2(k):
        rows = height[CHUNKS[k][0]]
        sums, extra = pick(k, sum_in, sum_out), pick(k, twin_in, twin_out)
        fars, nears = pick(k, far_in, far_out), pick(k, near_in, near_out)
        h0, h1 = pl.ds(0, rows // 2), pl.ds(rows // 2, rows // 2)
        swaps[k].wait_recv()

        def add(block):
            def body(r):
                sums[block, r, :] = sums[block, r, :] + extra[block, r, :]
            add_rows(rows, rows // 2, body)
        add(y_far)
        far[k] = (remote(sums.at[y_far, h0], fars.at[0], far_send.at[k, 0], far_recv.at[k, 0], up),
                  remote(sums.at[y_far, h1], fars.at[1], far_send.at[k, 1], far_recv.at[k, 1], down))
        add(y_up)
        add(y_down)
        near_own[k] = (remote(sums.at[y_up, h1], nears.at[0, h1], near_send.at[k, 0], near_recv.at[k, 0], up),
                       remote(sums.at[y_down, h0], nears.at[1, h0], near_send.at[k, 1], near_recv.at[k, 1], down))
        add(y)

    def stage_3(k):
        rows = height[CHUNKS[k][0]]
        half = rows // 2
        sums = pick(k, sum_in, sum_out)
        fars, nears = pick(k, far_in, far_out), pick(k, near_in, near_out)
        h0, h1 = pl.ds(0, half), pl.ds(half, half)
        far[k][0].wait_recv()

        sums[y_up, h0, :] = sums[y_up, h0, :] + fars[0]
        one = remote(sums.at[y_up, h0], nears.at[0, h0], near_send.at[k, 2], near_recv.at[k, 2], up)
        far[k][1].wait_recv()

        sums[y_down, h1, :] = sums[y_down, h1, :] + fars[1]
        near_sum[k] = (one, remote(sums.at[y_down, h1], nears.at[1, h1], near_send.at[k, 3], near_recv.at[k, 3], down))

    def result(k, query, key, value, out):
        kind, n, start, width = CHUNKS[k]
        ref = out if kind else (query, query, key, value)[n]
        begin = 1280 * n if kind else start if n > 1 else 512 * n
        return ref, pl.ds(begin, width)

    def mates(k, level):
        ref, cols = result(k, mate_query, mate_key, mate_value, mate_out)
        return ref.at[level, :, cols]

    def stage_4(k):
        kind = CHUNKS[k][0]
        sums, nears, done = pick(k, sum_in, sum_out), pick(k, near_in, near_out), pick(k, done_in, done_out)
        for copy in near_own[k] + near_sum[k]:
            copy.wait_recv()

        def body(r):
            done[r, :] = (sums[y, r, :].astype(F32) + nears[0, r, :].astype(F32) + nears[1, r, :].astype(F32)).astype(BF16)
        add_rows(height[kind], height[kind] // 4 if kind else 80, body)
        flips[k] = (remote(done, mates(k, 0), mate_send.at[k, 0], mate_recv.at[k, 0], x_flip),
                    remote(done, mates(k, 2), mate_send.at[k, 2], mate_recv.at[k, 2], z_flip))
        own, cols = result(k, own_query, own_key, own_value, own_out)
        keeps[k] = pltpu.make_async_copy(done, own.at[:, cols], keep_sem.at[k])
        keeps[k].start()

    def stage_5(k):
        flips[k][0].wait_recv()
        one = remote(mates(k, 0), mates(k, 1), mate_send.at[k, 1], mate_recv.at[k, 1], x_turn)
        flips[k][1].wait_recv()
        turns[k] = (one, remote(mates(k, 2), mates(k, 3), mate_send.at[k, 3], mate_recv.at[k, 3], z_turn))

    stage_1(0)

    def spread(h, carry):
        rows = pl.ds(pl.multiple_of(h * 256, 256), 256)
        mixed_grad[h] = dot(delta[...], weight[rows, :], ((1,), (1,))).astype(BF16)
        return carry
    lax.fori_loop(0, HEADS, spread, 0)
    stage_2(0)

    terms[5 * (1 - c)] = jnp.zeros((4, ROWS, 256), BF16)

    def back(g):
        for r in range(2):
            h = 2 * g + r
            grad = mixed_grad[h]
            row_dots = jnp.sum(grad.astype(F32) * mixed[h].astype(F32), axis=1, keepdims=True)
            prob_grads = dot(grad, tile(2 + g), ((1,), (1,)))
            score = (probs[h].astype(F32) * (prob_grads - row_dots) * 256 ** -0.5).astype(BF16)
            scores[r] = score
            joined[g, :, 256 * r:256 * r + 256] = dot(score, tile(g)).astype(BF16)
        key_terms = dot(scores[0], queries[2 * g], ((0,), (0,))) + dot(scores[1], queries[2 * g + 1], ((0,), (0,)))
        terms[pl.ds(c, 5), g] = key_terms.astype(BF16).reshape(5, ROWS, 256)
        value_terms = (dot(probs[2 * g], mixed_grad[2 * g], ((0,), (0,)))
                       + dot(probs[2 * g + 1], mixed_grad[2 * g + 1], ((0,), (0,))))
        terms[pl.ds(c, 5), 2 + g] = value_terms.astype(BF16).reshape(5, ROWS, 256)

    back(0)
    stage_3(0)
    back(1)

    def move(src, dst, n, to):
        return remote(src, dst, term_send.at[n], term_recv.at[n], to)

    to_mate = [move(terms.at[2 * n + 1 - c], term_mate.at[n], n, twin) for n in range(3)]
    stage_1(1)

    def fold(n):
        to_mate[n].wait_recv()
        for q in range(4):
            terms[2 * n + c, q] = terms[2 * n + c, q] + term_mate[n, q]

    def part(ref, low, high, start=0):
        return ref.at[:, pl.ds(low - start, high - low), :]

    fold(0)
    s2 = terms.at[c]
    e0 = move(part(s2, 0, FAR_DOWN), term_far, 3, down)
    f0 = move(part(s2, FAR_DOWN, FAR_MID), part(term_relay, FAR_DOWN, FAR_MID, FAR_DOWN), 4, up)
    f1 = move(part(s2, FAR_MID, ROWS), part(term_relay, FAR_MID, ROWS, FAR_DOWN), 5, up)
    fold(1)
    s1 = terms.at[2 + c]
    e1 = move(part(s1, FAR_DOWN, ROWS), part(term_next, FAR_DOWN, ROWS), 6, down)
    stage_2(1)
    for copy in read_turned:
        copy.wait()
    stage_1(2)
    e0.wait_recv()
    for q in range(4):
        terms[2 + c, q, 0:FAR_DOWN, :] = terms[2 + c, q, 0:FAR_DOWN, :] + term_far[q]
    e2 = move(part(s1, 0, FAR_DOWN), part(term_next, 0, FAR_DOWN), 7, down)
    f0.wait_recv()
    f2 = move(part(term_relay, FAR_DOWN, FAR_MID, FAR_DOWN), part(term_end, FAR_DOWN, FAR_MID, FAR_DOWN), 8, up)
    fold(2)
    f1.wait_recv()
    f3 = move(part(term_relay, FAR_MID, ROWS, FAR_DOWN), part(term_end, FAR_MID, ROWS, FAR_DOWN), 9, up)
    stage_2(2)
    stage_4(0)
    stage_3(1)
    stage_1(3)
    stage_3(2)
    for copy in (e1, e2, f2, f3):
        copy.wait_recv()
    for q in range(4):
        n, g = 2 + q // 2, q % 2
        joined[n, 0:FAR_DOWN, 256 * g:256 * g + 256] = (
            terms[4 + c, q, 0:FAR_DOWN, :].astype(F32) + term_next[q, 0:FAR_DOWN, :].astype(F32)).astype(BF16)
        joined[n, FAR_DOWN:ROWS, 256 * g:256 * g + 256] = (
            terms[4 + c, q, FAR_DOWN:ROWS, :].astype(F32) + term_next[q, FAR_DOWN:ROWS, :].astype(F32)
            + term_end[q].astype(F32)).astype(BF16)
    order = ((2, 3), (1, 4), (4, 1), (5, 0), (2, 4), (3, 3), (1, 5), (4, 2), (5, 1), (2, 5), (3, 4), (1, 6), (4, 3), (5, 2),
             (2, 6), (3, 5), (1, 7), (4, 4), (5, 3), (2, 7), (3, 6), (4, 5), (5, 4), (3, 7), (4, 6), (5, 5), (4, 7), (5, 6), (5, 7))
    for stage, k in order:
        (stage_1, stage_2, stage_3, stage_4, stage_5)[stage - 1](k)
    for k in range(len(CHUNKS)):
        turns[k][0].wait_recv()
        turns[k][1].wait_recv()
        keeps[k].wait()
    for k in (0, 1, 4, 5, 6, 7):
        swaps[k].wait_send()
    for copy in sent:
        copy.wait_send()


def layer_grads(queries, kv, mask, rewards, turned, tokens, target, weight):
    vmem = pl.BlockSpec(memory_space=pltpu.VMEM)
    hbm = pl.BlockSpec(memory_space=pl.ANY)
    dma = pltpu.SemaphoreType.DMA
    ri, ro, n = WIDE // 8, HEADS * 256 // 8, len(CHUNKS)
    results = ((ri, 1024), (ri, 512), (ri, 512), (ro, WIDE))

    def held(*shape):
        return pltpu.VMEM(shape, BF16)

    return pl.pallas_call(
        layer_kernel,
        out_shape=tuple(jax.ShapeDtypeStruct(shape, BF16) for shape in results)
        + tuple(jax.ShapeDtypeStruct((4, *shape), BF16) for shape in results),
        in_specs=[vmem, vmem, vmem, vmem, hbm, hbm, hbm, hbm],
        out_specs=(hbm,) * 8,
        scratch_shapes=[
            held(HEADS, ROWS, 5 * ROWS), held(2, ROWS, 5 * ROWS),
            held(6, 4, ROWS, 256), held(3, 4, ROWS, 256), held(4, ROWS, 256), held(4, FAR_DOWN, 256),
            held(4, ROWS - FAR_DOWN, 256), held(4, ROWS - FAR_DOWN, 256),
            held(ROWS, WIDE), held(ROWS, WIDE), held(HEADS * 256, WIDE), held(2, 4, WIDE // 8, ROWS),
            held(HEADS, ROWS, 256), held(2, 4, 128, ROWS), held(HEADS, ROWS, 256), held(4, ROWS, 512),
            held(2, 4, ri, 512), held(2, 4, ro, 1280),
            held(4, 4, ri, 512), held(2, 4, ro, 1280), held(4, 4, ri, 512), held(2, 4, ro, 1280),
            held(4, 2, ri // 2, 512), held(2, 2, ro // 2, 1280), held(4, 2, ri, 512), held(2, 2, ro, 1280),
            held(4, ri, 512), held(2, ro, 1280),
            dma((5,)), dma((10,)), dma((10,)), dma((n,)), dma((n,)),
            dma((n, 2)), dma((n, 2)), dma((n, 4)), dma((n, 4)), dma((n, 4)), dma((n, 4)), dma((n,)),
        ],
        compiler_params=pltpu.CompilerParams(
            collective_id=1, has_side_effects=True, vmem_limit_bytes=62 * 2**20),
        name="layer_grads",
    )(queries, kv, mask, rewards, turned.reshape(4, 2, WIDE // 8, ROWS), tokens, target, weight)


def per_device(
    tokens, target, rewards, doc_lengths, norm_gain, w_query, w_key, w_value, w_out, gossip_bit
):
    token_rows, target_rows = tokens[0, 0], target[0, 0]
    queries, kv, turned, mask, out_whole = front(
        token_rows, norm_gain, doc_lengths[0], w_query, w_key, w_value, w_out
    )
    results = layer_grads(
        queries, kv, mask, rewards.reshape(ROWS, 1), turned, token_rows, target_rows, out_whole
    )
    own_bit = gossip_bit[0]

    def mean(own, mates):
        partner = mates[0]
        for level in range(1, 4):
            partner = jnp.where(own_bit == level, mates[level], partner)
        return ((own.astype(F32) + partner.astype(F32)) * 0.5)[None]

    return tuple(mean(own, mates) for own, mates in zip(results[:4], results[4:]))


def solution(mesh):
    placed = (
        P("dp", None, "ctx", None),
        P("dp", None, "ctx", None),
        P("dp", None, "ctx"),
        P("dp", None, None),
        P(),
        P(("dp", "ctx"), None),
        P(("dp", "ctx"), None),
        P(("dp", "ctx"), None),
        P(("dp", "ctx"), None),
        P("dp"),
    )
    return jax.shard_map(
        per_device,
        mesh=mesh,
        in_specs=placed,
        out_specs=(
            P("dp", "ctx", None),
            P("dp", "ctx", None),
            P("dp", "ctx", None),
            P("dp", "ctx", None),
        ),
        check_vma=False,
    )
```

```python
import functools
import jax
import jax.numpy as jnp
from jax import lax
from jax.experimental import pallas as pl
from jax.experimental.pallas import tpu as pltpu
from jax.sharding import PartitionSpec as P

MESH = pl.DeviceIdType.MESH
BF16 = jnp.bfloat16
F32 = jnp.float32
WINDOW = 1024

epsilon = 1e-06
masked_score = -1e30

SIDE = 4


def place():
    dp, ctx = lax.axis_index("dp"), lax.axis_index("ctx")
    return {"x": lax.rem(dp, SIDE), "z": lax.div(dp, SIDE), "y": lax.div(ctx, 2), "c": lax.rem(ctx, 2)}


def device(at):
    return (at["z"] * SIDE + at["x"], at["y"] * 2 + at["c"])


def beside(at, axis, step):
    return {**at, axis: lax.rem(at[axis] + step + SIDE, SIDE)}


def sibling(at):
    return {**at, "c": 1 - at["c"]}


def greet(peers):
    barrier = pltpu.get_barrier_semaphore()
    for peer in peers:
        pl.semaphore_signal(barrier, inc=1, device_id=device(peer), device_id_type=MESH)
    pl.semaphore_wait(barrier, len(peers))


HEADS, GROUPS, ROWS, WIDE = 4, 2, 256, 2560
NEAR_UP = 64
NEAR_MID = 160
FAR_DOWN = 80
FAR_MID = 160
CHUNKS = ((1, 0, 0, 1280), (1, 1, 0, 1280), (0, 0, 0, 512), (0, 1, 0, 512), (0, 2, 0, 512), (0, 3, 0, 256), (0, 3, 256, 128),
          (0, 3, 384, 128))


def dot(a, b, contract=((1,), (0,))):
    return lax.dot_general(a, b, (contract, ((), ())), preferred_element_type=F32)


def add_rows(count, step, body):
    def at(i, carry):
        body(pl.ds(pl.multiple_of(i * step, step), step))
        return carry
    lax.fori_loop(0, count // step, at, 0)


PARTS = (
    ("kv", 0, 80, "xz"), ("kv", 80, 80, "zx"),
    ("query", 0, 80, "xz"), ("query", 80, 80, "zx"),
    ("out", 0, 32, "xz"), ("out", 32, 32, "zx"),
)
KV_PARTS, QUERY_PARTS, OUT_PARTS = (0, 1), (2, 3), (4, 5)


def front_kernel(rows_in, rows_out, kv_ref, query_ref, out_ref, tokens_ref, gain_ref, lengths_ref,
                 queries_out, kv_out, turned_out, mask_out, w_out, *scratch):
    (w_kv, w_query, slots_kv, slots_query, slots_out, wide, block_out, x_ref, queries, kv, kv_relay, turned, mask,
     swap_send, swap_recv, local_sem, line_send, line_recv, ring_send, ring_recv, twin_send, twin_recv,
     kv_send, kv_recv, keep_sem) = scratch
    at = place()
    c = at["c"]
    ctx = at["y"] * 2 + c
    twin = sibling(at)
    up, down = beside(at, "y", 1), beside(at, "y", -1)
    others = [lax.rem(ctx + k, 8) for k in range(1, 8)]
    group = [{**at, "y": lax.div(j, 2), "c": lax.rem(j, 2)} for j in others]
    greet([beside(at, a, step) for a in "xz" for step in (1, -1)] + group)
    sent = []

    def remote(src, dst, send, recv, to):
        copy = pltpu.make_async_remote_copy(src, dst, send, recv, device_id=device(to), device_id_type=MESH)
        copy.start()
        sent.append(copy)
        return copy

    def spread(n, ref, slots):
        return [remote(ref.at[group[k]["c"]], slots.at[ctx], swap_send.at[n, k], swap_recv.at[n, k], group[k]) for k in range(7)]

    def norm(i, carry):
        r = pl.ds(pl.multiple_of(i * 32, 32), 32)
        values = tokens_ref[r, :].astype(F32)
        power = jnp.mean(values * values, axis=1, keepdims=True)
        x_ref[r, :] = (values * lax.rsqrt(power + epsilon) * gain_ref[...]).astype(BF16)
        return carry

    def merged(slots, rows, copies):
        for copy in copies:
            copy.wait_recv()
        width = slots.shape[2]
        for j in range(8):
            wide[rows * j:rows * (j + 1), :width] = slots[j].astype(F32)[:rows]
        return wide[:8 * rows, :width].astype(BF16)

    half = pl.ds(pl.multiple_of(c * 512, 128), 512)
    spread_kv = spread(0, kv_ref, slots_kv)
    slots_kv[ctx] = kv_ref[c]
    slots_query[ctx] = query_ref[c]
    slots_out[ctx] = out_ref[c]
    w_kv[at["z"], at["x"], :, half] = merged(slots_kv, rows_in, spread_kv)

    one = {a: pl.ds(at[a], 1) for a in "xz"}
    whole = pl.ds(0, SIDE)

    def view(part, where, piece=None):
        name, start, size, _ = PARTS[part]
        cut = size // 32 * 16 if size % 32 == 0 else 48
        rows = pl.ds(*((start, size) if piece is None else ((start, cut), (start + cut, size - cut))[piece]))
        if name == "out":
            return w_out.at[where["z"], where["x"], rows, pl.ds(pl.multiple_of(c * 1280, 128), 1280)]
        return (w_kv if name == "kv" else w_query).at[where["z"], where["x"], rows, half]

    lines, first, last, twins = {}, {}, {}, {}

    def beside_line(part, step):
        axis = PARTS[part][3][0]
        return {**one, axis: pl.ds(beside(at, axis, step)[axis], 1)}

    def hop(part, n, where, step, piece=None):
        lines.setdefault(part, []).append(
            remote(view(part, where, piece), view(part, where, piece), line_send.at[part, n], line_recv.at[part, n],
                   beside(at, PARTS[part][3][0], step)))

    def line(part):
        hop(part, 0, one, 1)
        hop(part, 1, one, -1)

    def pass_on(parts):
        for part in parts:
            lines[part][0].wait_recv()
            hop(part, 2, beside_line(part, -1), 1, 0)
            lines[part][1].wait_recv()
            hop(part, 3, beside_line(part, 1), -1, 1)

    def lined(parts):
        for part in parts:
            for copy in lines[part][2:]:
                copy.wait_recv()

    def known(part, shift, which):
        order = PARTS[part][3]
        axis = order[1]
        return {order[0]: pl.ds(2 * which, 2), axis: pl.ds(lax.rem(at[axis] + shift + SIDE, SIDE), 1)}

    def ring(part, slot, where, step):
        return remote(view(part, where), view(part, where), ring_send.at[part, slot], ring_recv.at[part, slot],
                      beside(at, PARTS[part][3][1], step))

    def to_twin(part, where, slot):
        twins.setdefault(part, []).append(
            remote(view(part, where), view(part, where), twin_send.at[part, slot], twin_recv.at[part, slot], twin))

    def begin(parts):
        for part in parts:
            first[part] = (ring(part, 0, known(part, 0, 0), 1), ring(part, 1, known(part, 0, 1), -1))
        for part in parts:
            last[part] = [ring(part, 2, known(part, 0, 1), 1), ring(part, 3, known(part, 0, 0), -1)]
        for part in parts:
            to_twin(part, {**one, PARTS[part][3][0]: whole}, 0)

    def relay(parts):
        for part in parts:
            first[part][0].wait_recv()
            last[part].append(ring(part, 4, known(part, -1, 0), 1))
        for part in parts:
            first[part][1].wait_recv()
            last[part].append(ring(part, 5, known(part, 1, 1), -1))
        for part in parts:
            to_twin(part, known(part, -1, 0), 1)
            to_twin(part, known(part, 1, 1), 2)

    def finish(parts):
        for n in range(4):
            for part in parts:
                last[part][n].wait_recv()
                shift, which = ((-1, 1), (1, 0), (-2, 0), (2, 1))[n]
                to_twin(part, known(part, shift, which), 3 + n)

    def arrived(parts):
        for part in parts:
            for copy in twins[part]:
                copy.wait_recv()

    for part in KV_PARTS:
        line(part)
    spread_query = spread(1, query_ref, slots_query)
    spread_out = spread(2, out_ref, slots_out)
    lax.fori_loop(0, 2, norm, 0)
    pass_on(KV_PARTS)
    lax.fori_loop(2, 4, norm, 0)
    lined(KV_PARTS)
    begin(KV_PARTS)
    w_query[at["z"], at["x"], :, half] = merged(slots_query, rows_in, spread_query)
    for part in QUERY_PARTS:
        line(part)
    block_out[0, 0] = merged(slots_out, rows_out, spread_out)
    store = pltpu.make_async_copy(
        block_out, w_out.at[one["z"], one["x"], :, pl.ds(pl.multiple_of(c * 1280, 128), 1280)], local_sem)
    store.start()
    relay(KV_PARTS)
    store.wait()
    for part in OUT_PARTS:
        line(part)
    pass_on(QUERY_PARTS)
    lax.fori_loop(4, ROWS // 32, norm, 0)
    finish(KV_PARTS)
    lined(QUERY_PARTS)
    begin(QUERY_PARTS)
    arrived(KV_PARTS)

    here, before, old = 4 + c, 2 + c, c
    for n in range(4):
        kv[here, n] = dot(x_ref[...], w_kv[:, :, :, 256 * n:256 * n + 256].reshape(128 * rows_in, 256)).astype(BF16)

    def rows_of(slot, low, high):
        return kv.at[slot, :, pl.ds(low, high - low), :]

    def kv_move(src, dst, n, to):
        return remote(src, dst, kv_send.at[n], kv_recv.at[n], to)

    mid = NEAR_MID - NEAR_UP
    a0 = kv_move(rows_of(here, 0, NEAR_UP), rows_of(before, 0, NEAR_UP), 0, up)
    b0 = kv_move(rows_of(here, NEAR_UP, NEAR_MID), kv_relay.at[:, pl.ds(0, mid), :], 1, down)
    a1 = kv_move(rows_of(here, NEAR_UP, ROWS), rows_of(before, NEAR_UP, ROWS), 2, up)
    b1 = kv_move(rows_of(here, NEAR_MID, ROWS), kv_relay.at[:, pl.ds(mid, ROWS - NEAR_MID), :], 3, down)
    t0 = kv_move(kv.at[here], kv.at[here], 4, twin)
    pass_on(OUT_PARTS)
    relay(QUERY_PARTS)
    lined(OUT_PARTS)
    begin(OUT_PARTS)

    def turn(i, carry):
        cols = pl.ds(pl.multiple_of(i * 128, 128), 128)
        turned[cols, :] = x_ref[:, cols].astype(F32).T.astype(BF16)
        return carry
    a0.wait_recv()
    a2 = kv_move(rows_of(before, 0, NEAR_UP), rows_of(old, 0, NEAR_UP), 5, up)
    lax.fori_loop(0, 10, turn, 0)
    b0.wait_recv()
    b2 = kv_move(kv_relay.at[:, pl.ds(0, mid), :], rows_of(old, NEAR_UP, NEAR_MID), 6, down)
    finish(QUERY_PARTS)
    b1.wait_recv()
    b3 = kv_move(kv_relay.at[:, pl.ds(mid, ROWS - NEAR_MID), :], rows_of(old, NEAR_MID, ROWS), 7, down)
    relay(OUT_PARTS)
    lax.fori_loop(10, WIDE // 128, turn, 0)
    keep_turned = pltpu.make_async_copy(turned, turned_out, keep_sem.at[0])
    keep_turned.start()

    query_pos = ctx * ROWS + lax.broadcasted_iota(jnp.int32, (ROWS, 1), 0)
    key_pos = (ctx - 4) * ROWS + lax.broadcasted_iota(jnp.int32, (1, 5 * ROWS), 1)
    query_doc, key_doc, ending = 0 * query_pos, 0 * key_pos, 0
    for n in range(lengths_ref.shape[1]):
        ending = ending + lengths_ref[0, n]
        query_doc = query_doc + jnp.where(query_pos >= ending, 1, 0)
        key_doc = key_doc + jnp.where(key_pos >= ending, 1, 0)
    gap = query_pos - key_pos
    seen = (query_doc == key_doc) & (key_pos >= 0) & (gap >= 0) & (gap < WINDOW)
    mask[...] = jnp.where(seen, 1.0, 0.0)
    keep_mask = pltpu.make_async_copy(mask, mask_out, keep_sem.at[1])
    keep_mask.start()

    a1.wait_recv()
    t1 = kv_move(kv.at[before], kv.at[before], 8, twin)
    arrived(QUERY_PARTS)
    for n in range(4):
        queries[n] = dot(x_ref[...], w_query[:, :, :, 256 * n:256 * n + 256].reshape(128 * rows_in, 256)).astype(BF16)
    keep_queries = pltpu.make_async_copy(queries, queries_out, keep_sem.at[2])
    keep_queries.start()
    a2.wait_recv()
    b2.wait_recv()
    t2 = kv_move(rows_of(old, 0, NEAR_MID), rows_of(old, 0, NEAR_MID), 9, twin)
    b3.wait_recv()
    t3 = kv_move(rows_of(old, NEAR_MID, ROWS), rows_of(old, NEAR_MID, ROWS), 10, twin)
    finish(OUT_PARTS)
    for copy in (t0, t1, t2, t3):
        copy.wait_recv()
    keep_kv = pltpu.make_async_copy(kv, kv_out, keep_sem.at[3])
    keep_kv.start()
    arrived(OUT_PARTS)
    for copy in sent:
        copy.wait_send()
    for copy in (keep_turned, keep_mask, keep_queries, keep_kv):
        copy.wait()


def front(tokens, norm_gain, lengths, w_query, w_key, w_value, w_out):
    rows_in, rows_out = w_query.shape[0], w_out.shape[0]
    pad_in, pad_out = (0, 32 - rows_in), (0, 16 - rows_out)
    kv_pieces = jnp.pad(jnp.stack([w_key, w_value]), ((0, 0), pad_in, (0, 0)))
    query_pieces = jnp.pad(jnp.stack([w_query[:, :512], w_query[:, 512:]]), ((0, 0), pad_in, (0, 0)))
    out_pieces = jnp.pad(jnp.stack([w_out[:, :1280], w_out[:, 1280:]]), ((0, 0), pad_out, (0, 0)))
    vmem = pl.BlockSpec(memory_space=pltpu.VMEM)
    hbm = pl.BlockSpec(memory_space=pl.ANY)
    smem = pl.BlockSpec(memory_space=pltpu.SMEM)
    dma = pltpu.SemaphoreType.DMA

    def held(*shape):
        return pltpu.VMEM(shape, BF16)

    *rest, whole_out = pl.pallas_call(
        functools.partial(front_kernel, rows_in, rows_out),
        out_shape=(
            jax.ShapeDtypeStruct((HEADS, ROWS, 256), BF16),
            jax.ShapeDtypeStruct((6, 4, ROWS, 256), BF16),
            jax.ShapeDtypeStruct((WIDE, ROWS), BF16),
            jax.ShapeDtypeStruct((ROWS, 5 * ROWS), F32),
            jax.ShapeDtypeStruct((SIDE, SIDE, 8 * rows_out, WIDE), BF16),
        ),
        in_specs=[vmem, vmem, vmem, vmem, vmem, smem],
        out_specs=(hbm,) * 5,
        scratch_shapes=[
            held(SIDE, SIDE, 8 * rows_in, 1024), held(SIDE, SIDE, 8 * rows_in, 1024),
            held(8, 32, 512), held(8, 32, 512), held(8, 16, 1280), pltpu.VMEM((8 * rows_in, 1280), F32),
            held(1, 1, 8 * rows_out, 1280),
            held(ROWS, WIDE), held(HEADS, ROWS, 256), held(6, 4, ROWS, 256), held(4, ROWS - NEAR_UP, 256),
            held(WIDE, ROWS), pltpu.VMEM((ROWS, 5 * ROWS), F32),
            dma((3, 7)), dma((3, 7)), dma, dma((6, 4)), dma((6, 4)),
            dma((6, 6)), dma((6, 6)), dma((6, 7)), dma((6, 7)), dma((11,)), dma((11,)), dma((4,)),
        ],
        compiler_params=pltpu.CompilerParams(
            collective_id=0, has_side_effects=True, vmem_limit_bytes=62 * 2**20),
        name="front",
    )(kv_pieces, query_pieces, out_pieces, tokens, norm_gain.reshape(1, -1), lengths)
    return (*rest, whole_out.reshape(128 * rows_out, WIDE))


def layer_kernel(queries_in, kv_in, mask_in, rewards_ref, turned_ref, tokens_ref, target_ref, weight_ref,
                 own_query, own_key, own_value, own_out, mate_query, mate_key, mate_value, mate_out, *scratch):
    (queries, kv, mask_ref, probs, scores, terms, term_mate, term_next, term_far, term_relay, term_end, x_one, x_two,
     weight, turned, mixed, mixed_turned, mixed_grad, joined,
     give_in, give_out, sum_in, sum_out, twin_in, twin_out, far_in, far_out, near_in, near_out, done_in, done_out,
     read_sem, term_send, term_recv, twin_send, twin_recv,
     far_send, far_recv, near_send, near_recv, mate_send, mate_recv, keep_sem) = scratch
    at = place()
    c, y = at["c"], at["y"]
    twin = sibling(at)
    up, down = beside(at, "y", 1), beside(at, "y", -1)
    x_flip = {**at, "x": at["x"] + 1 - 2 * lax.rem(at["x"], 2)}
    x_turn = {**at, "x": SIDE - 1 - at["x"]}
    z_flip = {**at, "z": at["z"] + 1 - 2 * lax.rem(at["z"], 2)}
    z_turn = {**at, "z": SIDE - 1 - at["z"]}
    sent = []

    def remote(src, dst, send, recv, to):
        copy = pltpu.make_async_remote_copy(src, dst, send, recv, device_id=device(to), device_id_type=MESH)
        copy.start()
        sent.append(copy)
        return copy

    def read(src, dst, n):
        copy = pltpu.make_async_copy(src, dst, read_sem.at[n])
        copy.start()
        return copy

    read_operands = [read(queries_in, queries, 5), read(kv_in, kv, 6), read(mask_in, mask_ref, 7)]
    read_weight = read(weight_ref, weight, 1)
    read_tokens = read(tokens_ref, x_two, 2)
    read_target = read(target_ref, x_one, 3)
    read_turned = [read(turned_ref.at[:, core], turned.at[core], (0, 4)[core]) for core in range(2)]
    greet([twin, up, down, x_flip, x_turn, z_flip, z_turn])

    for copy in read_operands:
        copy.wait()

    def tile(n):
        return kv[pl.ds(c, 5), n].reshape(5 * ROWS, 256)

    def attend(h, carry):
        g = h // 2
        seen = mask_ref[...] > 0.5
        score = dot(queries[h], tile(g), ((1,), (1,))) * 256 ** -0.5
        score = jnp.where(seen, score, masked_score)
        raised = jnp.where(seen, jnp.exp(score - jnp.max(score, axis=1, keepdims=True)), 0.0)
        prob = (raised / jnp.sum(raised, axis=1, keepdims=True)).astype(BF16)
        probs[h] = prob
        out = dot(prob, tile(2 + g))
        mixed[h] = out.astype(BF16)
        rounded = out.astype(BF16).astype(F32).T.astype(BF16)
        mixed_turned[0, h] = rounded[:128]
        mixed_turned[1, h] = rounded[128:]
        return carry
    lax.fori_loop(0, HEADS, attend, 0)

    for copy in (read_weight, read_tokens, read_target):
        copy.wait()

    def error(i, carry):
        cols = pl.ds(pl.multiple_of(i * 512, 512), 512)
        update = sum(dot(mixed[h], weight[256 * h:256 * h + 256, cols]) for h in range(HEADS))
        result = x_two[:, cols].astype(F32) + update
        x_two[:, cols] = (rewards_ref[...] * (result - x_one[:, cols].astype(F32))).astype(BF16)
        return carry
    lax.fori_loop(0, WIDE // 512, error, 0)
    delta = x_two

    y_far, y_up, y_down = lax.rem(y + 2, SIDE), up["y"], down["y"]
    height = {0: WIDE // 8, 1: HEADS * 256 // 8}
    swaps, far, near_own, near_sum, flips, turns, keeps = {}, {}, {}, {}, {}, {}, {}

    def pick(k, inside, outside):
        kind, n, start, width = CHUNKS[k]
        if kind:
            return outside.at[n]
        if start == 0 and width == 512:
            return inside.at[n]
        return inside.at[n, :, pl.ds(start, width)] if len(inside.shape) == 3 else inside.at[n, :, :, pl.ds(start, width)]

    def term(k, dst, core):
        kind, n, start, width = CHUNKS[k]

        for m in range(2):
            if kind:
                cols = slice(1280 * n + 640 * m, 1280 * n + 640 * m + 640)
                part = dot(mixed_turned[core].reshape(512, ROWS), delta[:, cols])
                dst[:, :, 640 * m:640 * m + 640] = part.astype(BF16).reshape(4, 128, 640)
            else:
                part = dot(turned[core, 2 * m:2 * m + 2].reshape(640, ROWS), joined[n, :, start:start + width])
                dst[2 * m:2 * m + 2] = part.astype(BF16).reshape(2, 320, width)

    def stage_1(k):
        kind, n, start, width = CHUNKS[k]
        give = give_out.at[n] if kind else give_in.at[n % 2, :, :, pl.ds(start, width)]
        if k in (4, 5):
            swaps[k - 2].wait_send()
        term(k, give, 1 - c)
        swaps[k] = pltpu.make_async_remote_copy(
            give, pick(k, twin_in, twin_out), twin_send.at[k], twin_recv.at[k], device_id=device(twin), device_id_type=MESH)
        swaps[k].start()
        term(k, pick(k, sum_in, sum_out), c)

    def stage_2(k):
        rows = height[CHUNKS[k][0]]
        sums, extra = pick(k, sum_in, sum_out), pick(k, twin_in, twin_out)
        fars, nears = pick(k, far_in, far_out), pick(k, near_in, near_out)
        h0, h1 = pl.ds(0, rows // 2), pl.ds(rows // 2, rows // 2)
        swaps[k].wait_recv()

        def add(block):
            def body(r):
                sums[block, r, :] = sums[block, r, :] + extra[block, r, :]
            add_rows(rows, rows // 2, body)
        add(y_far)
        far[k] = (remote(sums.at[y_far, h0], fars.at[0], far_send.at[k, 0], far_recv.at[k, 0], up),
                  remote(sums.at[y_far, h1], fars.at[1], far_send.at[k, 1], far_recv.at[k, 1], down))
        add(y_up)
        add(y_down)
        near_own[k] = (remote(sums.at[y_up, h1], nears.at[0, h1], near_send.at[k, 0], near_recv.at[k, 0], up),
                       remote(sums.at[y_down, h0], nears.at[1, h0], near_send.at[k, 1], near_recv.at[k, 1], down))
        add(y)

    def stage_3(k):
        rows = height[CHUNKS[k][0]]
        half = rows // 2
        sums = pick(k, sum_in, sum_out)
        fars, nears = pick(k, far_in, far_out), pick(k, near_in, near_out)
        h0, h1 = pl.ds(0, half), pl.ds(half, half)
        far[k][0].wait_recv()

        sums[y_up, h0, :] = sums[y_up, h0, :] + fars[0]
        one = remote(sums.at[y_up, h0], nears.at[0, h0], near_send.at[k, 2], near_recv.at[k, 2], up)
        far[k][1].wait_recv()

        sums[y_down, h1, :] = sums[y_down, h1, :] + fars[1]
        near_sum[k] = (one, remote(sums.at[y_down, h1], nears.at[1, h1], near_send.at[k, 3], near_recv.at[k, 3], down))

    def result(k, query, key, value, out):
        kind, n, start, width = CHUNKS[k]
        ref = out if kind else (query, query, key, value)[n]
        begin = 1280 * n if kind else start if n > 1 else 512 * n
        return ref, pl.ds(begin, width)

    def mates(k, level):
        ref, cols = result(k, mate_query, mate_key, mate_value, mate_out)
        return ref.at[level, :, cols]

    def stage_4(k):
        kind = CHUNKS[k][0]
        sums, nears, done = pick(k, sum_in, sum_out), pick(k, near_in, near_out), pick(k, done_in, done_out)
        for copy in near_own[k] + near_sum[k]:
            copy.wait_recv()

        def body(r):
            done[r, :] = (sums[y, r, :].astype(F32) + nears[0, r, :].astype(F32) + nears[1, r, :].astype(F32)).astype(BF16)
        add_rows(height[kind], height[kind] // 4 if kind else 80, body)
        flips[k] = (remote(done, mates(k, 0), mate_send.at[k, 0], mate_recv.at[k, 0], x_flip),
                    remote(done, mates(k, 2), mate_send.at[k, 2], mate_recv.at[k, 2], z_flip))
        own, cols = result(k, own_query, own_key, own_value, own_out)
        keeps[k] = pltpu.make_async_copy(done, own.at[:, cols], keep_sem.at[k])
        keeps[k].start()

    def stage_5(k):
        flips[k][0].wait_recv()
        one = remote(mates(k, 0), mates(k, 1), mate_send.at[k, 1], mate_recv.at[k, 1], x_turn)
        flips[k][1].wait_recv()
        turns[k] = (one, remote(mates(k, 2), mates(k, 3), mate_send.at[k, 3], mate_recv.at[k, 3], z_turn))

    stage_1(0)

    def spread(h, carry):
        rows = pl.ds(pl.multiple_of(h * 256, 256), 256)
        mixed_grad[h] = dot(delta[...], weight[rows, :], ((1,), (1,))).astype(BF16)
        return carry
    lax.fori_loop(0, HEADS, spread, 0)
    stage_2(0)

    terms[5 * (1 - c)] = jnp.zeros((4, ROWS, 256), BF16)

    def back(g):
        for r in range(2):
            h = 2 * g + r
            grad = mixed_grad[h]
            row_dots = jnp.sum(grad.astype(F32) * mixed[h].astype(F32), axis=1, keepdims=True)
            prob_grads = dot(grad, tile(2 + g), ((1,), (1,)))
            score = (probs[h].astype(F32) * (prob_grads - row_dots) * 256 ** -0.5).astype(BF16)
            scores[r] = score
            joined[g, :, 256 * r:256 * r + 256] = dot(score, tile(g)).astype(BF16)
        key_terms = dot(scores[0], queries[2 * g], ((0,), (0,))) + dot(scores[1], queries[2 * g + 1], ((0,), (0,)))
        terms[pl.ds(c, 5), g] = key_terms.astype(BF16).reshape(5, ROWS, 256)
        value_terms = (dot(probs[2 * g], mixed_grad[2 * g], ((0,), (0,)))
                       + dot(probs[2 * g + 1], mixed_grad[2 * g + 1], ((0,), (0,))))
        terms[pl.ds(c, 5), 2 + g] = value_terms.astype(BF16).reshape(5, ROWS, 256)

    back(0)
    stage_3(0)
    back(1)

    def move(src, dst, n, to):
        return remote(src, dst, term_send.at[n], term_recv.at[n], to)

    to_mate = [move(terms.at[2 * n + 1 - c], term_mate.at[n], n, twin) for n in range(3)]
    stage_1(1)

    def fold(n):
        to_mate[n].wait_recv()
        for q in range(4):
            terms[2 * n + c, q] = terms[2 * n + c, q] + term_mate[n, q]

    def part(ref, low, high, start=0):
        return ref.at[:, pl.ds(low - start, high - low), :]

    fold(0)
    s2 = terms.at[c]
    e0 = move(part(s2, 0, FAR_DOWN), term_far, 3, down)
    f0 = move(part(s2, FAR_DOWN, FAR_MID), part(term_relay, FAR_DOWN, FAR_MID, FAR_DOWN), 4, up)
    f1 = move(part(s2, FAR_MID, ROWS), part(term_relay, FAR_MID, ROWS, FAR_DOWN), 5, up)
    fold(1)
    s1 = terms.at[2 + c]
    e1 = move(part(s1, FAR_DOWN, ROWS), part(term_next, FAR_DOWN, ROWS), 6, down)
    stage_2(1)
    for copy in read_turned:
        copy.wait()
    stage_1(2)
    e0.wait_recv()
    for q in range(4):
        terms[2 + c, q, 0:FAR_DOWN, :] = terms[2 + c, q, 0:FAR_DOWN, :] + term_far[q]
    e2 = move(part(s1, 0, FAR_DOWN), part(term_next, 0, FAR_DOWN), 7, down)
    f0.wait_recv()
    f2 = move(part(term_relay, FAR_DOWN, FAR_MID, FAR_DOWN), part(term_end, FAR_DOWN, FAR_MID, FAR_DOWN), 8, up)
    fold(2)
    f1.wait_recv()
    f3 = move(part(term_relay, FAR_MID, ROWS, FAR_DOWN), part(term_end, FAR_MID, ROWS, FAR_DOWN), 9, up)
    stage_2(2)
    stage_4(0)
    stage_3(1)
    stage_1(3)
    stage_3(2)
    for copy in (e1, e2, f2, f3):
        copy.wait_recv()
    for q in range(4):
        n, g = 2 + q // 2, q % 2
        joined[n, 0:FAR_DOWN, 256 * g:256 * g + 256] = (
            terms[4 + c, q, 0:FAR_DOWN, :].astype(F32) + term_next[q, 0:FAR_DOWN, :].astype(F32)).astype(BF16)
        joined[n, FAR_DOWN:ROWS, 256 * g:256 * g + 256] = (
            terms[4 + c, q, FAR_DOWN:ROWS, :].astype(F32) + term_next[q, FAR_DOWN:ROWS, :].astype(F32)
            + term_end[q].astype(F32)).astype(BF16)
    order = ((2, 3), (1, 4), (4, 1), (5, 0), (2, 4), (3, 3), (1, 5), (4, 2), (5, 1), (2, 5), (3, 4), (1, 6), (4, 3), (5, 2),
             (2, 6), (3, 5), (1, 7), (4, 4), (5, 3), (2, 7), (3, 6), (4, 5), (5, 4), (3, 7), (4, 6), (5, 5), (4, 7), (5, 6), (5, 7))
    for stage, k in order:
        (stage_1, stage_2, stage_3, stage_4, stage_5)[stage - 1](k)
    for k in range(len(CHUNKS)):
        turns[k][0].wait_recv()
        turns[k][1].wait_recv()
        keeps[k].wait()
    for k in (0, 1, 4, 5, 6, 7):
        swaps[k].wait_send()
    for copy in sent:
        copy.wait_send()


def layer_grads(queries, kv, mask, rewards, turned, tokens, target, weight):
    vmem = pl.BlockSpec(memory_space=pltpu.VMEM)
    hbm = pl.BlockSpec(memory_space=pl.ANY)
    dma = pltpu.SemaphoreType.DMA
    ri, ro, n = WIDE // 8, HEADS * 256 // 8, len(CHUNKS)
    results = ((ri, 1024), (ri, 512), (ri, 512), (ro, WIDE))

    def held(*shape):
        return pltpu.VMEM(shape, BF16)

    return pl.pallas_call(
        layer_kernel,
        out_shape=tuple(jax.ShapeDtypeStruct(shape, BF16) for shape in results)
        + tuple(jax.ShapeDtypeStruct((4, *shape), BF16) for shape in results),
        in_specs=[hbm, hbm, hbm, vmem, hbm, hbm, hbm, hbm],
        out_specs=(hbm,) * 8,
        scratch_shapes=[
            held(HEADS, ROWS, 256), held(6, 4, ROWS, 256), pltpu.VMEM((ROWS, 5 * ROWS), F32),
            held(HEADS, ROWS, 5 * ROWS), held(2, ROWS, 5 * ROWS),
            held(6, 4, ROWS, 256), held(3, 4, ROWS, 256), held(4, ROWS, 256), held(4, FAR_DOWN, 256),
            held(4, ROWS - FAR_DOWN, 256), held(4, ROWS - FAR_DOWN, 256),
            held(ROWS, WIDE), held(ROWS, WIDE), held(HEADS * 256, WIDE), held(2, 4, WIDE // 8, ROWS),
            held(HEADS, ROWS, 256), held(2, 4, 128, ROWS), held(HEADS, ROWS, 256), held(4, ROWS, 512),
            held(2, 4, ri, 512), held(2, 4, ro, 1280),
            held(4, 4, ri, 512), held(2, 4, ro, 1280), held(4, 4, ri, 512), held(2, 4, ro, 1280),
            held(4, 2, ri // 2, 512), held(2, 2, ro // 2, 1280), held(4, 2, ri, 512), held(2, 2, ro, 1280),
            held(4, ri, 512), held(2, ro, 1280),
            dma((8,)), dma((10,)), dma((10,)), dma((n,)), dma((n,)),
            dma((n, 2)), dma((n, 2)), dma((n, 4)), dma((n, 4)), dma((n, 4)), dma((n, 4)), dma((n,)),
        ],
        compiler_params=pltpu.CompilerParams(
            collective_id=1, has_side_effects=True, vmem_limit_bytes=62 * 2**20),
        name="layer_grads",
    )(queries, kv, mask, rewards, turned.reshape(4, 2, WIDE // 8, ROWS), tokens, target, weight)


def per_device(
    tokens, target, rewards, doc_lengths, norm_gain, w_query, w_key, w_value, w_out, gossip_bit
):
    token_rows, target_rows = tokens[0, 0], target[0, 0]
    queries, kv, turned, mask, out_whole = front(
        token_rows, norm_gain, doc_lengths[0], w_query, w_key, w_value, w_out
    )
    results = layer_grads(
        queries, kv, mask, rewards.reshape(ROWS, 1), turned, token_rows, target_rows, out_whole
    )
    own_bit = gossip_bit[0]

    def mean(own, mates):
        partner = mates[0]
        for level in range(1, 4):
            partner = jnp.where(own_bit == level, mates[level], partner)
        return ((own.astype(F32) + partner.astype(F32)) * 0.5)[None]

    return tuple(mean(own, mates) for own, mates in zip(results[:4], results[4:]))


def solution(mesh):
    placed = (
        P("dp", None, "ctx", None),
        P("dp", None, "ctx", None),
        P("dp", None, "ctx"),
        P("dp", None, None),
        P(),
        P(("dp", "ctx"), None),
        P(("dp", "ctx"), None),
        P(("dp", "ctx"), None),
        P(("dp", "ctx"), None),
        P("dp"),
    )
    return jax.shard_map(
        per_device,
        mesh=mesh,
        in_specs=placed,
        out_specs=(
            P("dp", "ctx", None),
            P("dp", "ctx", None),
            P("dp", "ctx", None),
            P("dp", "ctx", None),
        ),
        check_vma=False,
    )
```

```python
import functools
import jax
import jax.numpy as jnp
from jax import lax
from jax.experimental import pallas as pl
from jax.experimental.pallas import tpu as pltpu
from jax.sharding import PartitionSpec as P

MESH = pl.DeviceIdType.MESH
BF16 = jnp.bfloat16
F32 = jnp.float32
WINDOW = 1024

epsilon = 1e-06
masked_score = -1e30

SIDE = 4


def place():
    dp, ctx = lax.axis_index("dp"), lax.axis_index("ctx")
    return {"x": lax.rem(dp, SIDE), "z": lax.div(dp, SIDE), "y": lax.div(ctx, 2), "c": lax.rem(ctx, 2)}


def device(at):
    return (at["z"] * SIDE + at["x"], at["y"] * 2 + at["c"])


def beside(at, axis, step):
    return {**at, axis: lax.rem(at[axis] + step + SIDE, SIDE)}


def sibling(at):
    return {**at, "c": 1 - at["c"]}


def greet(peers):
    barrier = pltpu.get_barrier_semaphore()
    for peer in peers:
        pl.semaphore_signal(barrier, inc=1, device_id=device(peer), device_id_type=MESH)
    pl.semaphore_wait(barrier, len(peers))


HEADS, GROUPS, ROWS, WIDE = 4, 2, 256, 2560
NEAR_UP = 64
NEAR_MID = 160
FAR_DOWN = 80
FAR_MID = 160
CHUNKS = ((1, 0, 0, 1280), (1, 1, 0, 1280), (0, 0, 0, 512), (0, 1, 0, 512), (0, 2, 0, 512), (0, 3, 0, 256), (0, 3, 256, 128),
          (0, 3, 384, 128))


def dot(a, b, contract=((1,), (0,))):
    return lax.dot_general(a, b, (contract, ((), ())), preferred_element_type=F32)


def add_rows(count, step, body):
    def at(i, carry):
        body(pl.ds(pl.multiple_of(i * step, step), step))
        return carry
    lax.fori_loop(0, count // step, at, 0)


PARTS = (
    ("kv", 0, 80, "xz"), ("kv", 80, 80, "zx"),
    ("query", 0, 80, "xz"), ("query", 80, 80, "zx"),
    ("out", 0, 32, "xz"), ("out", 32, 32, "zx"),
)
KV_PARTS, QUERY_PARTS, OUT_PARTS = (0, 1), (2, 3), (4, 5)


def front_kernel(rows_in, rows_out, kv_ref, query_ref, out_ref, tokens_ref, gain_ref, lengths_ref,
                 queries_out, kv_out, turned_out, mask_out, w_out, *scratch):
    (w_kv, w_query, slots_kv, slots_query, slots_out, wide, block_out, x_ref, queries, kv, kv_relay, turned, mask,
     swap_send, swap_recv, local_sem, line_send, line_recv, ring_send, ring_recv, twin_send, twin_recv,
     kv_send, kv_recv, keep_sem) = scratch
    at = place()
    c = at["c"]
    ctx = at["y"] * 2 + c
    twin = sibling(at)
    up, down = beside(at, "y", 1), beside(at, "y", -1)
    others = [lax.rem(ctx + k, 8) for k in range(1, 8)]
    group = [{**at, "y": lax.div(j, 2), "c": lax.rem(j, 2)} for j in others]
    greet([beside(at, a, step) for a in "xz" for step in (1, -1)] + group)
    sent = []

    def remote(src, dst, send, recv, to):
        copy = pltpu.make_async_remote_copy(src, dst, send, recv, device_id=device(to), device_id_type=MESH)
        copy.start()
        sent.append(copy)
        return copy

    def spread(n, ref, slots):
        return [remote(ref.at[group[k]["c"]], slots.at[ctx], swap_send.at[n, k], swap_recv.at[n, k], group[k]) for k in range(7)]

    def norm(i, carry):
        r = pl.ds(pl.multiple_of(i * 32, 32), 32)
        values = tokens_ref[r, :].astype(F32)
        power = jnp.mean(values * values, axis=1, keepdims=True)
        x_ref[r, :] = (values * lax.rsqrt(power + epsilon) * gain_ref[...].reshape(1, WIDE)).astype(BF16)
        return carry

    def merged(slots, rows, copies):
        for copy in copies:
            copy.wait_recv()
        width = slots.shape[2]
        for j in range(8):
            wide[rows * j:rows * (j + 1), :width] = slots[j].astype(F32)[:rows]
        return wide[:8 * rows, :width].astype(BF16)

    half = pl.ds(pl.multiple_of(c * 512, 128), 512)
    spread_kv = spread(0, kv_ref, slots_kv)
    slots_kv[ctx] = kv_ref[c]
    slots_query[ctx] = query_ref[c]
    slots_out[ctx] = out_ref[c]
    w_kv[at["z"], at["x"], :, half] = merged(slots_kv, rows_in, spread_kv)

    one = {a: pl.ds(at[a], 1) for a in "xz"}
    whole = pl.ds(0, SIDE)

    def view(part, where, piece=None):
        name, start, size, _ = PARTS[part]
        cut = size // 32 * 16 if size % 32 == 0 else 48
        rows = pl.ds(*((start, size) if piece is None else ((start, cut), (start + cut, size - cut))[piece]))
        if name == "out":
            return w_out.at[where["z"], where["x"], rows, pl.ds(pl.multiple_of(c * 1280, 128), 1280)]
        return (w_kv if name == "kv" else w_query).at[where["z"], where["x"], rows, half]

    lines, first, last, twins = {}, {}, {}, {}

    def beside_line(part, step):
        axis = PARTS[part][3][0]
        return {**one, axis: pl.ds(beside(at, axis, step)[axis], 1)}

    def hop(part, n, where, step, piece=None):
        lines.setdefault(part, []).append(
            remote(view(part, where, piece), view(part, where, piece), line_send.at[part, n], line_recv.at[part, n],
                   beside(at, PARTS[part][3][0], step)))

    def line(part):
        hop(part, 0, one, 1)
        hop(part, 1, one, -1)

    def pass_on(parts):
        for part in parts:
            lines[part][0].wait_recv()
            hop(part, 2, beside_line(part, -1), 1, 0)
            lines[part][1].wait_recv()
            hop(part, 3, beside_line(part, 1), -1, 1)

    def lined(parts):
        for part in parts:
            for copy in lines[part][2:]:
                copy.wait_recv()

    def known(part, shift, which):
        order = PARTS[part][3]
        axis = order[1]
        return {order[0]: pl.ds(2 * which, 2), axis: pl.ds(lax.rem(at[axis] + shift + SIDE, SIDE), 1)}

    def ring(part, slot, where, step):
        return remote(view(part, where), view(part, where), ring_send.at[part, slot], ring_recv.at[part, slot],
                      beside(at, PARTS[part][3][1], step))

    def to_twin(part, where, slot):
        twins.setdefault(part, []).append(
            remote(view(part, where), view(part, where), twin_send.at[part, slot], twin_recv.at[part, slot], twin))

    def begin(parts):
        for part in parts:
            first[part] = (ring(part, 0, known(part, 0, 0), 1), ring(part, 1, known(part, 0, 1), -1))
        for part in parts:
            last[part] = [ring(part, 2, known(part, 0, 1), 1), ring(part, 3, known(part, 0, 0), -1)]
        for part in parts:
            to_twin(part, {**one, PARTS[part][3][0]: whole}, 0)

    def relay(parts):
        for part in parts:
            first[part][0].wait_recv()
            last[part].append(ring(part, 4, known(part, -1, 0), 1))
        for part in parts:
            first[part][1].wait_recv()
            last[part].append(ring(part, 5, known(part, 1, 1), -1))
        for part in parts:
            to_twin(part, known(part, -1, 0), 1)
            to_twin(part, known(part, 1, 1), 2)

    def finish(parts):
        for n in range(4):
            for part in parts:
                last[part][n].wait_recv()
                shift, which = ((-1, 1), (1, 0), (-2, 0), (2, 1))[n]
                to_twin(part, known(part, shift, which), 3 + n)

    def arrived(parts):
        for part in parts:
            for copy in twins[part]:
                copy.wait_recv()

    for part in KV_PARTS:
        line(part)
    spread_query = spread(1, query_ref, slots_query)
    spread_out = spread(2, out_ref, slots_out)
    lax.fori_loop(0, 2, norm, 0)
    pass_on(KV_PARTS)
    lax.fori_loop(2, 4, norm, 0)
    lined(KV_PARTS)
    begin(KV_PARTS)
    w_query[at["z"], at["x"], :, half] = merged(slots_query, rows_in, spread_query)
    for part in QUERY_PARTS:
        line(part)
    block_out[0, 0] = merged(slots_out, rows_out, spread_out)
    store = pltpu.make_async_copy(
        block_out, w_out.at[one["z"], one["x"], :, pl.ds(pl.multiple_of(c * 1280, 128), 1280)], local_sem)
    store.start()
    relay(KV_PARTS)
    store.wait()
    for part in OUT_PARTS:
        line(part)
    pass_on(QUERY_PARTS)
    lax.fori_loop(4, ROWS // 32, norm, 0)
    finish(KV_PARTS)
    lined(QUERY_PARTS)
    begin(QUERY_PARTS)
    arrived(KV_PARTS)

    here, before, old = 4 + c, 2 + c, c
    for n in range(4):
        kv[here, n] = dot(x_ref[...], w_kv[:, :, :, 256 * n:256 * n + 256].reshape(128 * rows_in, 256)).astype(BF16)

    def rows_of(slot, low, high):
        return kv.at[slot, :, pl.ds(low, high - low), :]

    def kv_move(src, dst, n, to):
        return remote(src, dst, kv_send.at[n], kv_recv.at[n], to)

    mid = NEAR_MID - NEAR_UP
    a0 = kv_move(rows_of(here, 0, NEAR_UP), rows_of(before, 0, NEAR_UP), 0, up)
    b0 = kv_move(rows_of(here, NEAR_UP, NEAR_MID), kv_relay.at[:, pl.ds(0, mid), :], 1, down)
    a1 = kv_move(rows_of(here, NEAR_UP, ROWS), rows_of(before, NEAR_UP, ROWS), 2, up)
    b1 = kv_move(rows_of(here, NEAR_MID, ROWS), kv_relay.at[:, pl.ds(mid, ROWS - NEAR_MID), :], 3, down)
    t0 = kv_move(kv.at[here], kv.at[here], 4, twin)
    pass_on(OUT_PARTS)
    relay(QUERY_PARTS)
    lined(OUT_PARTS)
    begin(OUT_PARTS)

    def turn(i, carry):
        cols = pl.ds(pl.multiple_of(i * 128, 128), 128)
        turned[cols, :] = x_ref[:, cols].astype(F32).T.astype(BF16)
        return carry
    a0.wait_recv()
    a2 = kv_move(rows_of(before, 0, NEAR_UP), rows_of(old, 0, NEAR_UP), 5, up)
    lax.fori_loop(0, 10, turn, 0)
    b0.wait_recv()
    b2 = kv_move(kv_relay.at[:, pl.ds(0, mid), :], rows_of(old, NEAR_UP, NEAR_MID), 6, down)
    finish(QUERY_PARTS)
    b1.wait_recv()
    b3 = kv_move(kv_relay.at[:, pl.ds(mid, ROWS - NEAR_MID), :], rows_of(old, NEAR_MID, ROWS), 7, down)
    relay(OUT_PARTS)
    lax.fori_loop(10, WIDE // 128, turn, 0)
    keep_turned = pltpu.make_async_copy(turned, turned_out, keep_sem.at[0])
    keep_turned.start()

    query_pos = ctx * ROWS + lax.broadcasted_iota(jnp.int32, (ROWS, 1), 0)
    key_pos = (ctx - 4) * ROWS + lax.broadcasted_iota(jnp.int32, (1, 5 * ROWS), 1)
    query_doc, key_doc, ending = 0 * query_pos, 0 * key_pos, 0
    for n in range(lengths_ref.shape[1]):
        ending = ending + lengths_ref[0, n]
        query_doc = query_doc + jnp.where(query_pos >= ending, 1, 0)
        key_doc = key_doc + jnp.where(key_pos >= ending, 1, 0)
    gap = query_pos - key_pos
    seen = (query_doc == key_doc) & (key_pos >= 0) & (gap >= 0) & (gap < WINDOW)
    mask[...] = jnp.where(seen, 1.0, 0.0)
    keep_mask = pltpu.make_async_copy(mask, mask_out, keep_sem.at[1])
    keep_mask.start()

    a1.wait_recv()
    t1 = kv_move(kv.at[before], kv.at[before], 8, twin)
    arrived(QUERY_PARTS)
    for n in range(4):
        queries[n] = dot(x_ref[...], w_query[:, :, :, 256 * n:256 * n + 256].reshape(128 * rows_in, 256)).astype(BF16)
    keep_queries = pltpu.make_async_copy(queries, queries_out, keep_sem.at[2])
    keep_queries.start()
    a2.wait_recv()
    b2.wait_recv()
    t2 = kv_move(rows_of(old, 0, NEAR_MID), rows_of(old, 0, NEAR_MID), 9, twin)
    b3.wait_recv()
    t3 = kv_move(rows_of(old, NEAR_MID, ROWS), rows_of(old, NEAR_MID, ROWS), 10, twin)
    finish(OUT_PARTS)
    for copy in (t0, t1, t2, t3):
        copy.wait_recv()
    keep_kv = pltpu.make_async_copy(kv, kv_out, keep_sem.at[3])
    keep_kv.start()
    arrived(OUT_PARTS)
    for copy in sent:
        copy.wait_send()
    for copy in (keep_turned, keep_mask, keep_queries, keep_kv):
        copy.wait()


def front(tokens, norm_gain, lengths, w_query, w_key, w_value, w_out):
    rows_in, rows_out = w_query.shape[0], w_out.shape[0]
    pad_in, pad_out = (0, 32 - rows_in), (0, 16 - rows_out)
    kv_pieces = jnp.pad(jnp.stack([w_key, w_value]), ((0, 0), pad_in, (0, 0)))
    query_pieces = jnp.pad(jnp.stack([w_query[:, :512], w_query[:, 512:]]), ((0, 0), pad_in, (0, 0)))
    out_pieces = jnp.pad(jnp.stack([w_out[:, :1280], w_out[:, 1280:]]), ((0, 0), pad_out, (0, 0)))
    vmem = pl.BlockSpec(memory_space=pltpu.VMEM)
    hbm = pl.BlockSpec(memory_space=pl.ANY)
    smem = pl.BlockSpec(memory_space=pltpu.SMEM)
    dma = pltpu.SemaphoreType.DMA

    def held(*shape):
        return pltpu.VMEM(shape, BF16)

    *rest, whole_out = pl.pallas_call(
        functools.partial(front_kernel, rows_in, rows_out),
        out_shape=(
            jax.ShapeDtypeStruct((HEADS, ROWS, 256), BF16),
            jax.ShapeDtypeStruct((6, 4, ROWS, 256), BF16),
            jax.ShapeDtypeStruct((WIDE, ROWS), BF16),
            jax.ShapeDtypeStruct((ROWS, 5 * ROWS), F32),
            jax.ShapeDtypeStruct((SIDE, SIDE, 8 * rows_out, WIDE), BF16),
        ),
        in_specs=[vmem, vmem, vmem, vmem, vmem, smem],
        out_specs=(hbm,) * 5,
        scratch_shapes=[
            held(SIDE, SIDE, 8 * rows_in, 1024), held(SIDE, SIDE, 8 * rows_in, 1024),
            held(8, 32, 512), held(8, 32, 512), held(8, 16, 1280), pltpu.VMEM((8 * rows_in, 1280), F32),
            held(1, 1, 8 * rows_out, 1280),
            held(ROWS, WIDE), held(HEADS, ROWS, 256), held(6, 4, ROWS, 256), held(4, ROWS - NEAR_UP, 256),
            held(WIDE, ROWS), pltpu.VMEM((ROWS, 5 * ROWS), F32),
            dma((3, 7)), dma((3, 7)), dma, dma((6, 4)), dma((6, 4)),
            dma((6, 6)), dma((6, 6)), dma((6, 7)), dma((6, 7)), dma((11,)), dma((11,)), dma((4,)),
        ],
        compiler_params=pltpu.CompilerParams(
            collective_id=0, has_side_effects=True, vmem_limit_bytes=62 * 2**20),
        name="front",
    )(kv_pieces, query_pieces, out_pieces, tokens, norm_gain, lengths)
    return (*rest, whole_out.reshape(128 * rows_out, WIDE))


def layer_kernel(queries_in, kv_in, mask_in, rewards_ref, turned_ref, tokens_ref, target_ref, weight_ref,
                 own_query, own_key, own_value, own_out, mate_query, mate_key, mate_value, mate_out, *scratch):
    (queries, kv, mask_ref, probs, scores, terms, term_mate, term_next, term_far, term_relay, term_end, x_one, x_two,
     weight, turned, mixed, mixed_turned, mixed_grad, joined,
     give_in, give_out, sum_in, sum_out, twin_in, twin_out, far_in, far_out, near_in, near_out, done_in, done_out,
     read_sem, term_send, term_recv, twin_send, twin_recv,
     far_send, far_recv, near_send, near_recv, mate_send, mate_recv, keep_sem) = scratch
    at = place()
    c, y = at["c"], at["y"]
    twin = sibling(at)
    up, down = beside(at, "y", 1), beside(at, "y", -1)
    x_flip = {**at, "x": at["x"] + 1 - 2 * lax.rem(at["x"], 2)}
    x_turn = {**at, "x": SIDE - 1 - at["x"]}
    z_flip = {**at, "z": at["z"] + 1 - 2 * lax.rem(at["z"], 2)}
    z_turn = {**at, "z": SIDE - 1 - at["z"]}
    sent = []

    def remote(src, dst, send, recv, to):
        copy = pltpu.make_async_remote_copy(src, dst, send, recv, device_id=device(to), device_id_type=MESH)
        copy.start()
        sent.append(copy)
        return copy

    def read(src, dst, n):
        copy = pltpu.make_async_copy(src, dst, read_sem.at[n])
        copy.start()
        return copy

    read_operands = [read(queries_in, queries, 5), read(kv_in, kv, 6), read(mask_in, mask_ref, 7)]
    read_weight = read(weight_ref, weight, 1)
    read_tokens = read(tokens_ref, x_two, 2)
    read_target = read(target_ref, x_one, 3)
    read_turned = [read(turned_ref.at[:, core], turned.at[core], (0, 4)[core]) for core in range(2)]
    greet([twin, up, down, x_flip, x_turn, z_flip, z_turn])

    for copy in read_operands:
        copy.wait()

    def tile(n):
        return kv[pl.ds(c, 5), n].reshape(5 * ROWS, 256)

    def attend(h, carry):
        g = h // 2
        seen = mask_ref[...] > 0.5
        score = dot(queries[h], tile(g), ((1,), (1,))) * 256 ** -0.5
        score = jnp.where(seen, score, masked_score)
        raised = jnp.where(seen, jnp.exp(score - jnp.max(score, axis=1, keepdims=True)), 0.0)
        prob = (raised / jnp.sum(raised, axis=1, keepdims=True)).astype(BF16)
        probs[h] = prob
        out = dot(prob, tile(2 + g))
        mixed[h] = out.astype(BF16)
        rounded = out.astype(BF16).astype(F32).T.astype(BF16)
        mixed_turned[0, h] = rounded[:128]
        mixed_turned[1, h] = rounded[128:]
        return carry
    lax.fori_loop(0, HEADS, attend, 0)

    for copy in (read_weight, read_tokens, read_target):
        copy.wait()

    reward = jnp.broadcast_to(rewards_ref[...], (128, ROWS)).T[:, :1]

    def error(i, carry):
        cols = pl.ds(pl.multiple_of(i * 512, 512), 512)
        update = sum(dot(mixed[h], weight[256 * h:256 * h + 256, cols]) for h in range(HEADS))
        result = x_two[:, cols].astype(F32) + update
        x_two[:, cols] = (reward * (result - x_one[:, cols].astype(F32))).astype(BF16)
        return carry
    lax.fori_loop(0, WIDE // 512, error, 0)
    delta = x_two

    y_far, y_up, y_down = lax.rem(y + 2, SIDE), up["y"], down["y"]
    height = {0: WIDE // 8, 1: HEADS * 256 // 8}
    swaps, far, near_own, near_sum, flips, turns, keeps = {}, {}, {}, {}, {}, {}, {}

    def pick(k, inside, outside):
        kind, n, start, width = CHUNKS[k]
        if kind:
            return outside.at[n]
        if start == 0 and width == 512:
            return inside.at[n]
        return inside.at[n, :, pl.ds(start, width)] if len(inside.shape) == 3 else inside.at[n, :, :, pl.ds(start, width)]

    def term(k, dst, core):
        kind, n, start, width = CHUNKS[k]

        for m in range(2):
            if kind:
                cols = slice(1280 * n + 640 * m, 1280 * n + 640 * m + 640)
                part = dot(mixed_turned[core].reshape(512, ROWS), delta[:, cols])
                dst[:, :, 640 * m:640 * m + 640] = part.astype(BF16).reshape(4, 128, 640)
            else:
                part = dot(turned[core, 2 * m:2 * m + 2].reshape(640, ROWS), joined[n, :, start:start + width])
                dst[2 * m:2 * m + 2] = part.astype(BF16).reshape(2, 320, width)

    def stage_1(k):
        kind, n, start, width = CHUNKS[k]
        give = give_out.at[n] if kind else give_in.at[n % 2, :, :, pl.ds(start, width)]
        if k in (4, 5):
            swaps[k - 2].wait_send()
        term(k, give, 1 - c)
        swaps[k] = pltpu.make_async_remote_copy(
            give, pick(k, twin_in, twin_out), twin_send.at[k], twin_recv.at[k], device_id=device(twin), device_id_type=MESH)
        swaps[k].start()
        term(k, pick(k, sum_in, sum_out), c)

    def stage_2(k):
        rows = height[CHUNKS[k][0]]
        sums, extra = pick(k, sum_in, sum_out), pick(k, twin_in, twin_out)
        fars, nears = pick(k, far_in, far_out), pick(k, near_in, near_out)
        h0, h1 = pl.ds(0, rows // 2), pl.ds(rows // 2, rows // 2)
        swaps[k].wait_recv()

        def add(block):
            def body(r):
                sums[block, r, :] = sums[block, r, :] + extra[block, r, :]
            add_rows(rows, rows // 2, body)
        add(y_far)
        far[k] = (remote(sums.at[y_far, h0], fars.at[0], far_send.at[k, 0], far_recv.at[k, 0], up),
                  remote(sums.at[y_far, h1], fars.at[1], far_send.at[k, 1], far_recv.at[k, 1], down))
        add(y_up)
        add(y_down)
        near_own[k] = (remote(sums.at[y_up, h1], nears.at[0, h1], near_send.at[k, 0], near_recv.at[k, 0], up),
                       remote(sums.at[y_down, h0], nears.at[1, h0], near_send.at[k, 1], near_recv.at[k, 1], down))
        add(y)

    def stage_3(k):
        rows = height[CHUNKS[k][0]]
        half = rows // 2
        sums = pick(k, sum_in, sum_out)
        fars, nears = pick(k, far_in, far_out), pick(k, near_in, near_out)
        h0, h1 = pl.ds(0, half), pl.ds(half, half)
        far[k][0].wait_recv()

        sums[y_up, h0, :] = sums[y_up, h0, :] + fars[0]
        one = remote(sums.at[y_up, h0], nears.at[0, h0], near_send.at[k, 2], near_recv.at[k, 2], up)
        far[k][1].wait_recv()

        sums[y_down, h1, :] = sums[y_down, h1, :] + fars[1]
        near_sum[k] = (one, remote(sums.at[y_down, h1], nears.at[1, h1], near_send.at[k, 3], near_recv.at[k, 3], down))

    def result(k, query, key, value, out):
        kind, n, start, width = CHUNKS[k]
        ref = out if kind else (query, query, key, value)[n]
        begin = 1280 * n if kind else start if n > 1 else 512 * n
        return ref, pl.ds(begin, width)

    def mates(k, level):
        ref, cols = result(k, mate_query, mate_key, mate_value, mate_out)
        return ref.at[level, :, cols]

    def stage_4(k):
        kind = CHUNKS[k][0]
        sums, nears, done = pick(k, sum_in, sum_out), pick(k, near_in, near_out), pick(k, done_in, done_out)
        for copy in near_own[k] + near_sum[k]:
            copy.wait_recv()

        def body(r):
            done[r, :] = (sums[y, r, :].astype(F32) + nears[0, r, :].astype(F32) + nears[1, r, :].astype(F32)).astype(BF16)
        add_rows(height[kind], height[kind] // 4 if kind else 80, body)
        flips[k] = (remote(done, mates(k, 0), mate_send.at[k, 0], mate_recv.at[k, 0], x_flip),
                    remote(done, mates(k, 2), mate_send.at[k, 2], mate_recv.at[k, 2], z_flip))
        own, cols = result(k, own_query, own_key, own_value, own_out)
        keeps[k] = pltpu.make_async_copy(done, own.at[:, cols], keep_sem.at[k])
        keeps[k].start()

    def stage_5(k):
        flips[k][0].wait_recv()
        one = remote(mates(k, 0), mates(k, 1), mate_send.at[k, 1], mate_recv.at[k, 1], x_turn)
        flips[k][1].wait_recv()
        turns[k] = (one, remote(mates(k, 2), mates(k, 3), mate_send.at[k, 3], mate_recv.at[k, 3], z_turn))

    stage_1(0)

    def spread(h, carry):
        rows = pl.ds(pl.multiple_of(h * 256, 256), 256)
        mixed_grad[h] = dot(delta[...], weight[rows, :], ((1,), (1,))).astype(BF16)
        return carry
    lax.fori_loop(0, HEADS, spread, 0)
    stage_2(0)

    terms[5 * (1 - c)] = jnp.zeros((4, ROWS, 256), BF16)

    def back(g):
        for r in range(2):
            h = 2 * g + r
            grad = mixed_grad[h]
            row_dots = jnp.sum(grad.astype(F32) * mixed[h].astype(F32), axis=1, keepdims=True)
            prob_grads = dot(grad, tile(2 + g), ((1,), (1,)))
            score = (probs[h].astype(F32) * (prob_grads - row_dots) * 256 ** -0.5).astype(BF16)
            scores[r] = score
            joined[g, :, 256 * r:256 * r + 256] = dot(score, tile(g)).astype(BF16)
        key_terms = dot(scores[0], queries[2 * g], ((0,), (0,))) + dot(scores[1], queries[2 * g + 1], ((0,), (0,)))
        terms[pl.ds(c, 5), g] = key_terms.astype(BF16).reshape(5, ROWS, 256)
        value_terms = (dot(probs[2 * g], mixed_grad[2 * g], ((0,), (0,)))
                       + dot(probs[2 * g + 1], mixed_grad[2 * g + 1], ((0,), (0,))))
        terms[pl.ds(c, 5), 2 + g] = value_terms.astype(BF16).reshape(5, ROWS, 256)

    back(0)
    stage_3(0)
    back(1)

    def move(src, dst, n, to):
        return remote(src, dst, term_send.at[n], term_recv.at[n], to)

    to_mate = [move(terms.at[2 * n + 1 - c], term_mate.at[n], n, twin) for n in range(3)]
    stage_1(1)

    def fold(n):
        to_mate[n].wait_recv()
        for q in range(4):
            terms[2 * n + c, q] = terms[2 * n + c, q] + term_mate[n, q]

    def part(ref, low, high, start=0):
        return ref.at[:, pl.ds(low - start, high - low), :]

    fold(0)
    s2 = terms.at[c]
    e0 = move(part(s2, 0, FAR_DOWN), term_far, 3, down)
    f0 = move(part(s2, FAR_DOWN, FAR_MID), part(term_relay, FAR_DOWN, FAR_MID, FAR_DOWN), 4, up)
    f1 = move(part(s2, FAR_MID, ROWS), part(term_relay, FAR_MID, ROWS, FAR_DOWN), 5, up)
    fold(1)
    s1 = terms.at[2 + c]
    e1 = move(part(s1, FAR_DOWN, ROWS), part(term_next, FAR_DOWN, ROWS), 6, down)
    stage_2(1)
    for copy in read_turned:
        copy.wait()
    stage_1(2)
    e0.wait_recv()
    for q in range(4):
        terms[2 + c, q, 0:FAR_DOWN, :] = terms[2 + c, q, 0:FAR_DOWN, :] + term_far[q]
    e2 = move(part(s1, 0, FAR_DOWN), part(term_next, 0, FAR_DOWN), 7, down)
    f0.wait_recv()
    f2 = move(part(term_relay, FAR_DOWN, FAR_MID, FAR_DOWN), part(term_end, FAR_DOWN, FAR_MID, FAR_DOWN), 8, up)
    fold(2)
    f1.wait_recv()
    f3 = move(part(term_relay, FAR_MID, ROWS, FAR_DOWN), part(term_end, FAR_MID, ROWS, FAR_DOWN), 9, up)
    stage_2(2)
    stage_4(0)
    stage_3(1)
    stage_1(3)
    stage_3(2)
    for copy in (e1, e2, f2, f3):
        copy.wait_recv()
    for q in range(4):
        n, g = 2 + q // 2, q % 2
        joined[n, 0:FAR_DOWN, 256 * g:256 * g + 256] = (
            terms[4 + c, q, 0:FAR_DOWN, :].astype(F32) + term_next[q, 0:FAR_DOWN, :].astype(F32)).astype(BF16)
        joined[n, FAR_DOWN:ROWS, 256 * g:256 * g + 256] = (
            terms[4 + c, q, FAR_DOWN:ROWS, :].astype(F32) + term_next[q, FAR_DOWN:ROWS, :].astype(F32)
            + term_end[q].astype(F32)).astype(BF16)
    order = ((2, 3), (1, 4), (4, 1), (5, 0), (2, 4), (3, 3), (1, 5), (4, 2), (5, 1), (2, 5), (3, 4), (1, 6), (4, 3), (5, 2),
             (2, 6), (3, 5), (1, 7), (4, 4), (5, 3), (2, 7), (3, 6), (4, 5), (5, 4), (3, 7), (4, 6), (5, 5), (4, 7), (5, 6), (5, 7))
    for stage, k in order:
        (stage_1, stage_2, stage_3, stage_4, stage_5)[stage - 1](k)
    for k in range(len(CHUNKS)):
        turns[k][0].wait_recv()
        turns[k][1].wait_recv()
        keeps[k].wait()
    for k in (0, 1, 4, 5, 6, 7):
        swaps[k].wait_send()
    for copy in sent:
        copy.wait_send()


def layer_grads(queries, kv, mask, rewards, turned, tokens, target, weight):
    vmem = pl.BlockSpec(memory_space=pltpu.VMEM)
    hbm = pl.BlockSpec(memory_space=pl.ANY)
    dma = pltpu.SemaphoreType.DMA
    ri, ro, n = WIDE // 8, HEADS * 256 // 8, len(CHUNKS)
    results = ((ri, 1024), (ri, 512), (ri, 512), (ro, WIDE))

    def held(*shape):
        return pltpu.VMEM(shape, BF16)

    return pl.pallas_call(
        layer_kernel,
        out_shape=tuple(jax.ShapeDtypeStruct(shape, BF16) for shape in results)
        + tuple(jax.ShapeDtypeStruct((4, *shape), BF16) for shape in results),
        in_specs=[hbm, hbm, hbm, vmem, hbm, hbm, hbm, hbm],
        out_specs=(hbm,) * 8,
        scratch_shapes=[
            held(HEADS, ROWS, 256), held(6, 4, ROWS, 256), pltpu.VMEM((ROWS, 5 * ROWS), F32),
            held(HEADS, ROWS, 5 * ROWS), held(2, ROWS, 5 * ROWS),
            held(6, 4, ROWS, 256), held(3, 4, ROWS, 256), held(4, ROWS, 256), held(4, FAR_DOWN, 256),
            held(4, ROWS - FAR_DOWN, 256), held(4, ROWS - FAR_DOWN, 256),
            held(ROWS, WIDE), held(ROWS, WIDE), held(HEADS * 256, WIDE), held(2, 4, WIDE // 8, ROWS),
            held(HEADS, ROWS, 256), held(2, 4, 128, ROWS), held(HEADS, ROWS, 256), held(4, ROWS, 512),
            held(2, 4, ri, 512), held(2, 4, ro, 1280),
            held(4, 4, ri, 512), held(2, 4, ro, 1280), held(4, 4, ri, 512), held(2, 4, ro, 1280),
            held(4, 2, ri // 2, 512), held(2, 2, ro // 2, 1280), held(4, 2, ri, 512), held(2, 2, ro, 1280),
            held(4, ri, 512), held(2, ro, 1280),
            dma((8,)), dma((10,)), dma((10,)), dma((n,)), dma((n,)),
            dma((n, 2)), dma((n, 2)), dma((n, 4)), dma((n, 4)), dma((n, 4)), dma((n, 4)), dma((n,)),
        ],
        compiler_params=pltpu.CompilerParams(
            collective_id=1, has_side_effects=True, vmem_limit_bytes=62 * 2**20),
        name="layer_grads",
    )(queries, kv, mask, rewards, turned.reshape(4, 2, WIDE // 8, ROWS), tokens, target, weight)


def per_device(
    tokens, target, rewards, doc_lengths, norm_gain, w_query, w_key, w_value, w_out, gossip_bit
):
    token_rows, target_rows = tokens[0, 0], target[0, 0]
    queries, kv, turned, mask, out_whole = front(
        token_rows, norm_gain, doc_lengths[0], w_query, w_key, w_value, w_out
    )
    results = layer_grads(
        queries, kv, mask, rewards.reshape(1, ROWS), turned, token_rows, target_rows, out_whole
    )
    own_bit = gossip_bit[0]

    def mean(own, mates):
        partner = mates[0]
        for level in range(1, 4):
            partner = jnp.where(own_bit == level, mates[level], partner)
        return ((own.astype(F32) + partner.astype(F32)) * 0.5)[None]

    return tuple(mean(own, mates) for own, mates in zip(results[:4], results[4:]))


def solution(mesh):
    placed = (
        P("dp", None, "ctx", None),
        P("dp", None, "ctx", None),
        P("dp", None, "ctx"),
        P("dp", None, None),
        P(),
        P(("dp", "ctx"), None),
        P(("dp", "ctx"), None),
        P(("dp", "ctx"), None),
        P(("dp", "ctx"), None),
        P("dp"),
    )
    return jax.shard_map(
        per_device,
        mesh=mesh,
        in_specs=placed,
        out_specs=(
            P("dp", "ctx", None),
            P("dp", "ctx", None),
            P("dp", "ctx", None),
            P("dp", "ctx", None),
        ),
        check_vma=False,
    )
```
